32 devices in a mesh: sec: 2 (over core), dev: 16 (over z, y, x).
Axes of the slice: x: 2, y: 2, z: 4, core: 2. Of those that a mesh axis runs over, the one named last changes fastest.
Arguments:
- queries: bfloat16 [256, 8192], P('dev', 'sec'), may hold values from -160 to 160
- key_cache: bfloat16 [256, 768, 512], P('dev', None, 'sec'), may hold values from -5 to 5
- value_cache: bfloat16 [256, 768, 512], P('dev', None, 'sec'), may hold values from -6 to 6
- new_key: bfloat16 [256, 512], P('dev', 'sec'), may hold values from -4 to 4
- new_value: bfloat16 [256, 512], P('dev', 'sec'), may hold values from -6 to 6
- cache_lengths: int32 [256], P('dev'), may hold values from 1 to 768, 98304 in all
- residual_in: bfloat16 [256, 4096], P('dev'), may hold values from -14 to 14
- out_weight: bfloat16 [8192, 4096], P('sec', 'dev'), may hold values from -0.5 to 0.5
- norm_gain: float32 [4096], replicated, may hold values from 0.1 to 1.9
- router_weight: bfloat16 [4096, 16], replicated, may hold values from -8 to 8
- expert_ids: int32 [256, 8], P('dev'), may hold values from 0 to 15, all different within a row; in each aligned block of 16 rows (0 to 15, 16 to 31, ...) at most 16 rows name the same one
- gate_weight: bfloat16 [16, 4096, 768], P('dev', None, 'sec'), may hold values from -0.09375 to 0.09375
- up_weight: bfloat16 [16, 4096, 768], P('dev', None, 'sec'), may hold values from -0.09375 to 0.09375
- down_weight: bfloat16 [16, 768, 4096], P('dev', 'sec'), may hold values from -0.625 to 0.625
Outputs:
- layer_out: bfloat16 [256, 4096], P('dev')
The draws below stay inside these ranges and needn't reach their ends.
Inputs may be any that keep to these rules, and one draw needn't show every extreme that they name: `cache_lengths`: the longest row has exactly 768 filled slots. `expert_ids`: in each aligned block of 16 rows (the rows of one chip) no expert is named by more than 16 rows, a bound that some block reaches.
All inputs are finite; a program needn't handle non-finite values. No bound on the sum of `cache_lengths` on one device may be relied on, other than what follows from the above.
Results may differ from the reference program's by a relative error of at most 0.012.
Values may be sent and summed in bfloat16 or wider, within the bound.
No kernel may reach another device: no remote copies, remote signals or barrier semaphores. Data moves between devices by JAX's collectives and lax.ppermute only.
A program may use at most 128 MiB of HBM per device.

```python
import math
import jax
import jax.numpy as jnp
import numpy as np
from jax import lax

D = 4096
HEADS = 64
KV_HEADS = 4
HEAD = 128
FFW = 768
TOPK = 8
ROW_DEV = 16
CACHE = 768
EXPERTS = 16
ROWS = 256
CAP = 16
N_DEV = 16


def base_new_key(key):
    return jnp.clip(jax.random.normal(jax.random.fold_in(key, 11), (ROWS, KV_HEADS * HEAD), jnp.float32), -4.0, 4.0)


def draw_new_key(key, part):
    return base_new_key(key).astype(jnp.bfloat16)


def draw_queries(key, part):
    values = jnp.clip(jax.random.normal(jax.random.fold_in(key, 12), (ROWS, HEADS * HEAD), jnp.float32), -6.0, 6.0)
    return values.astype(jnp.bfloat16)


def draw_key_cache(key, part):
    values = jnp.clip(jax.random.normal(jax.random.fold_in(key, 14), (ROWS, CACHE, KV_HEADS * HEAD), jnp.float32), -5.0, 5.0)
    return values.astype(jnp.bfloat16)


def draw_residual_in(key, part):
    noise = 0.5 * jnp.clip(jax.random.normal(jax.random.fold_in(key, 16), (ROWS, D), jnp.float32), -3.0, 3.0)
    row_scale = jnp.exp(jax.random.uniform(jax.random.fold_in(key, 18), (ROWS, 1), jnp.float32, math.log(0.3), math.log(3.0)))
    col_scale = jnp.exp(jax.random.uniform(jax.random.fold_in(key, 19), (1, D), jnp.float32, math.log(0.3), math.log(3.0)))
    return (noise * row_scale * col_scale).astype(jnp.bfloat16)


def draw_router_weight(key, part):
    values = jnp.clip(jax.random.normal(jax.random.fold_in(key, 21), (D, EXPERTS), jnp.float32), -4.0, 4.0) * (1.5 / math.sqrt(D))
    return values.astype(jnp.bfloat16)


def level_of(stream_key, extent, pieces, smallest, largest):
    factor_of = 1.0
    for axis_at, shards_of in pieces:
        steps = jax.random.uniform(jax.random.fold_in(jax.random.fold_in(stream_key, 6), axis_at), (shards_of,), jnp.float32, smallest / len(pieces), largest / len(pieces))
        factor_of = factor_of * jnp.repeat(jnp.exp(steps), extent[axis_at] // shards_of).reshape((-1,) + (1,) * (len(extent) - 1 - axis_at))
    return factor_of


def length_profile(amount, total, bound, lean):
    portions = [(1 << 20) // math.isqrt(standing ** lean) + 1 for standing in range(2, amount + 1)]
    surplus, counts = total - bound - (amount - 1), [1] * (amount - 1)
    while surplus > 0:
        candidates = [i for i in range(amount - 1) if counts[i] < bound]
        whole, remaining = sum([portions[i] for i in candidates]), surplus
        for i in candidates:
            extra = min(bound - counts[i], max(1, remaining * portions[i] // whole), surplus)
            counts[i] = counts[i] + extra
            surplus = surplus - extra
    return np.array([bound] + counts)


def ragged(stream_key, amount, total, limit, lean):
    if amount == 2:
        one = jax.random.randint(stream_key, (), max(1, total - limit), min(limit, total - 1) + 1)
        return jnp.stack([one, total - one])
    sizes = jnp.asarray(length_profile(amount, total, limit, lean), jnp.int32)
    twos = (amount - 1) // 2
    source_of, sink = sizes[1:1 + 2 * twos:2], sizes[2:2 + 2 * twos:2]
    room = jnp.minimum(source_of - 1, limit - sink)
    passed = jax.random.randint(jax.random.fold_in(stream_key, 1), (twos,), 0, 1 << 20) % (room + 1)
    sizes = sizes.at[1:1 + 2 * twos:2].set(source_of - passed).at[2:2 + 2 * twos:2].set(sink + passed)
    return sizes[jax.random.permutation(jax.random.fold_in(stream_key, 2), amount)]


def assign_block(own_key, own, number, rows, number_of, top, reach, lean):
    order = jax.random.permutation(own_key, number_of)
    crowded, common = shares(number_of, rows * top, reach, lean, True), shares(number_of, rows * top, reach, lean, False)
    places = jnp.arange(number_of)

    def named(tallies, offset_by):
        used = int((tallies > 0).sum())
        fixed = max(1, used // 4)
        passed = fixed + (places - fixed + offset_by * (used - fixed)) % max(1, number_of - fixed)
        return jnp.zeros((number_of,), jnp.int32).at[order[jnp.where(places < fixed, places, passed)]].set(jnp.asarray(tallies, jnp.int32))

    tallies = jnp.where(number % 4 == 0, named(crowded, number // 4), named(common, number - number // 4 - 1))
    mixed = jax.random.permutation(jax.random.fold_in(own, 3), number_of)
    donor, receiver = mixed[0:number_of // 2 * 2:2], mixed[1:number_of // 2 * 2:2]
    margin = jnp.minimum(tallies[donor] - 1, reach - tallies[receiver]) // 2
    margin = jnp.where((donor == order[0]) | (receiver == order[0]) | (tallies[receiver] == 0), 0, jnp.maximum(margin, 0))
    passed = jax.random.randint(jax.random.fold_in(own, 4), (number_of // 2,), 0, 1 << 20) % (margin + 1)
    tallies = tallies.at[donor].add(-passed).at[receiver].add(passed)
    labels = jnp.searchsorted(jnp.cumsum(tallies), jnp.arange(rows * top), side="right").astype(jnp.int32)
    table = labels.reshape(top, rows).T
    table = table[jax.random.permutation(jax.random.fold_in(own, 1), rows)]
    offset_by = jax.random.randint(jax.random.fold_in(own, 2), (rows, 1), 0, top)
    return jnp.take_along_axis(table, (jnp.arange(top)[None, :] + offset_by) % top, axis=1)


def shares(number_of, total, most, lean, full):
    weights = [(1 << 20) // math.isqrt(rank ** lean) + 1 for rank in range(1, number_of + 1)]
    largest = most if full else min(most, max(-(-total // number_of), total * weights[0] // sum(weights)))
    least = 1 if total - largest >= number_of - 1 else 0
    counts, surplus = [largest] + [least] * (number_of - 1), total - largest - least * (number_of - 1)
    while surplus > 0:
        candidates = [i for i in range(1, number_of) if counts[i] < largest] or [i for i in range(1, number_of) if counts[i] < most]
        whole, left = sum([weights[i] for i in candidates]), surplus
        for i in candidates:
            extra = min(most - counts[i], max(1, left * weights[i] // whole), surplus)
            counts[i] = counts[i] + extra
            surplus = surplus - extra
    return np.array(counts)


def scatter_about(key, shape, scale, most, cuts=(), held_as=jnp.bfloat16):
    result = scale * jax.random.normal(key, shape, jnp.float32)
    if cuts:
        result = result * level_of(key, shape, cuts, -0.22, 0.18)
    return jnp.clip(result, -most, most).astype(held_as)


def setup_inputs(seed: int = 0) -> dict:
    arg_keys = jax.random.split(jax.random.key(seed), 15)
    queries = draw_queries(jax.random.fold_in(arg_keys[14], 71), 0)
    key_cache = draw_key_cache(jax.random.fold_in(arg_keys[14], 71), 0)
    value_cache = scatter_about(arg_keys[2], (ROWS, CACHE, KV_HEADS * HEAD), 1.0, 6.0, ((0, 16), (2, 2)))
    new_key = draw_new_key(jax.random.fold_in(arg_keys[14], 71), 0)
    new_value = scatter_about(arg_keys[4], (ROWS, KV_HEADS * HEAD), 1.0, 6.0, ((0, 16), (1, 2)))
    cache_lengths = ragged(arg_keys[5], ROWS, ROWS * CACHE // 2, CACHE, 2).astype(jnp.int32)
    residual_in = draw_residual_in(jax.random.fold_in(arg_keys[14], 71), 0)
    out_weight = scatter_about(arg_keys[7], (HEADS * HEAD, D), (HEADS * HEAD // 64) ** -0.5, 0.5, ((0, 2), (1, 16)))
    norm_gain = jnp.clip(1.0 + 0.18 * jax.random.normal(arg_keys[8], (D,), jnp.float32), 0.1, 1.9)
    router_weight = draw_router_weight(jax.random.fold_in(arg_keys[14], 71), 0)
    expert_ids_keys = jax.random.split(jax.random.fold_in(arg_keys[10], 1), ROWS // ROW_DEV)
    expert_ids_turns = jax.random.permutation(jax.random.fold_in(arg_keys[10], 3), ROWS // ROW_DEV)
    expert_ids = jax.vmap(lambda own, number: assign_block(jax.random.fold_in(arg_keys[10], 2), own, number, ROW_DEV, EXPERTS, TOPK, CAP, 2))(expert_ids_keys, expert_ids_turns).reshape((ROWS, TOPK))
    gate_weight = scatter_about(arg_keys[11], (EXPERTS, D, FFW), D ** -0.5, 0.09375, ((0, 16), (2, 2)))
    up_weight = scatter_about(arg_keys[12], (EXPERTS, D, FFW), D ** -0.5, 0.09375, ((0, 16), (2, 2)))
    down_weight = scatter_about(arg_keys[13], (EXPERTS, FFW, D), (FFW // 8) ** -0.5, 0.625, ((0, 16), (1, 2)))
    return dict(queries=queries, key_cache=key_cache, value_cache=value_cache, new_key=new_key, new_value=new_value, cache_lengths=cache_lengths, residual_in=residual_in, out_weight=out_weight, norm_gain=norm_gain, router_weight=router_weight, expert_ids=expert_ids, gate_weight=gate_weight, up_weight=up_weight, down_weight=down_weight)


masked_score = -1e+30

def attend_rows(packed):
    query_rows, key_rows, value_rows, fresh_key, fresh_value, length_rows = packed
    block_rows = query_rows.shape[0]
    group_count = KV_HEADS
    per_group = HEADS // KV_HEADS
    score_scale = 1.0 / math.sqrt(HEAD)
    query_heads = query_rows.astype(jnp.float32).reshape(block_rows, group_count, per_group, HEAD)
    keys_f = key_rows.astype(jnp.float32).reshape(block_rows, CACHE, group_count, HEAD)
    values_f = value_rows.astype(jnp.float32).reshape(block_rows, CACHE, group_count, HEAD)
    scores = jnp.einsum('rgqh,rcgh->rgqc', query_heads, keys_f) * score_scale
    positions = jnp.arange(CACHE, dtype=jnp.int32)
    live_mask = positions[None, :] < length_rows[:, None]
    scores = jnp.where(live_mask[:, None, None, :], scores, masked_score)
    fresh_keys = fresh_key.astype(jnp.float32).reshape(block_rows, group_count, HEAD)
    fresh_score = jnp.einsum('rgqh,rgh->rgq', query_heads, fresh_keys) * score_scale
    row_max = jnp.maximum(lax.optimization_barrier(jnp.max(scores, axis=-1)), fresh_score)
    exp_cache = jnp.exp(scores - row_max[..., None])
    exp_fresh = jnp.exp(fresh_score - row_max)
    denominator = lax.optimization_barrier(jnp.sum(exp_cache, axis=-1)) + exp_fresh
    weights_bf = (exp_cache / denominator[..., None]).astype(jnp.bfloat16)
    fresh_weight = (exp_fresh / denominator).astype(jnp.bfloat16)
    attended = jnp.einsum('rgqc,rcgh->rgqh', weights_bf.astype(jnp.float32), values_f)
    fresh_values = fresh_value.astype(jnp.float32).reshape(block_rows, group_count, 1, HEAD)
    attended = attended + fresh_weight.astype(jnp.float32)[..., None] * fresh_values
    return attended.reshape(block_rows, HEADS * HEAD).astype(jnp.bfloat16)

def reference(queries, key_cache, value_cache, new_key, new_value, cache_lengths, residual_in, out_weight, norm_gain, router_weight, expert_ids, gate_weight, up_weight, down_weight):
    block_rows = math.gcd(ROWS, 64)
    block_total = ROWS // block_rows

    def split_rows(array):
        return array.reshape((block_total, block_rows) + array.shape[1:])
    packed = tuple((split_rows(array) for array in (queries, key_cache, value_cache, new_key, new_value, cache_lengths)))
    attended = lax.map(attend_rows, packed).reshape(ROWS, HEADS * HEAD)
    projected = jnp.dot(attended, out_weight, preferred_element_type=jnp.float32).astype(jnp.bfloat16)
    mixed = (residual_in.astype(jnp.float32) + projected.astype(jnp.float32)).astype(jnp.bfloat16)
    mixed_f = mixed.astype(jnp.float32)
    mean_square = lax.optimization_barrier(jnp.mean(mixed_f * mixed_f, axis=-1, keepdims=True))
    normed = (mixed_f * lax.rsqrt(mean_square + 1e-06) * norm_gain).astype(jnp.bfloat16)
    logits = jnp.dot(normed, router_weight, preferred_element_type=jnp.float32)
    chosen = jnp.take_along_axis(logits, expert_ids, axis=1)
    route_weights = jax.nn.softmax(chosen, axis=-1)
    pair_total = ROWS * TOPK
    flat_ids = expert_ids.reshape(pair_total)
    expert_hot = (flat_ids[:, None] == jnp.arange(EXPERTS, dtype=jnp.int32)[None, :]).astype(jnp.int32)
    rank = lax.optimization_barrier(jnp.sum((jnp.cumsum(expert_hot, axis=0) - expert_hot) * expert_hot, axis=1)).astype(jnp.int32)
    slot_total = N_DEV * CAP
    row_of_pair = (jnp.arange(pair_total, dtype=jnp.int32) // TOPK).astype(jnp.int32)
    table = jnp.zeros((EXPERTS, slot_total), jnp.int32).at[flat_ids, rank].set(row_of_pair)
    half_units = FFW // 2

    def run_expert(expert_pack):
        table_row, gate_e, up_e, down_e = expert_pack
        inputs_e = normed[table_row]
        gate_act = jnp.dot(inputs_e, gate_e, preferred_element_type=jnp.float32)
        up_act = jnp.dot(inputs_e, up_e, preferred_element_type=jnp.float32)
        hidden = (jax.nn.silu(gate_act) * up_act).astype(jnp.bfloat16)
        first_half = jnp.dot(hidden[:, :half_units], down_e[:half_units], preferred_element_type=jnp.float32).astype(jnp.bfloat16)
        second_half = jnp.dot(hidden[:, half_units:], down_e[half_units:], preferred_element_type=jnp.float32).astype(jnp.bfloat16)
        return (first_half, second_half)
    first_out, second_out = lax.map(run_expert, (table, gate_weight, up_weight, down_weight))
    picked = first_out[flat_ids, rank].astype(jnp.float32) + second_out[flat_ids, rank].astype(jnp.float32)
    weighted = picked * route_weights.reshape(pair_total)[:, None]
    contribution = lax.optimization_barrier(jnp.sum(weighted.reshape(ROWS, TOPK, D), axis=1))
    return (mixed.astype(jnp.float32) + contribution).astype(jnp.bfloat16)
```

```python
import functools
import math

import jax
import jax.numpy as jnp
from jax import lax
from jax.experimental import pallas as pl
from jax.experimental.pallas import tpu as pltpu
from jax.sharding import PartitionSpec as P

HEAD = 128
masked_score = -1e30
BF = jnp.bfloat16
F32 = jnp.float32


def grid_of(n):
    known = {16: (4, 2, 2), 64: (4, 4, 4)}
    return known.get(n, (n, 1, 1))


def strides_of(dims):
    return {"z": dims[1] * dims[2], "y": dims[2], "x": 1}


def rotate(value, dims, axis, step):
    nz, ny, nx = dims
    pairs = []
    for z in range(nz):
        for y in range(ny):
            for x in range(nx):
                src = (z * ny + y) * nx + x
                tz, ty, tx = z, y, x
                if axis == "z":
                    tz = (z + step) % nz
                elif axis == "y":
                    ty = (y + step) % ny
                else:
                    tx = (x + step) % nx
                pairs.append((src, (tz * ny + ty) * nx + tx))
    return lax.ppermute(value, "dev", pairs)


def swap_sec(value):
    return lax.ppermute(value, "sec", [(0, 1), (1, 0)])


def spread(block, dims, first, second):
    extent = dict(zip("zyx", dims))
    stacked = jnp.concatenate(
        [block] + [rotate(block, dims, "z", k) for k in range(1, extent["z"])], axis=0
    )
    found = {}
    for a in range(extent[first]):
        near = stacked if a == 0 else rotate(stacked, dims, first, a)
        for b in range(extent[second]):
            far = near if b == 0 else rotate(near, dims, second, b)
            found[(a, b) if first == "y" else (b, a)] = far
    return found


def position(dims):
    nz, ny, nx = dims
    d = lax.axis_index("dev")
    return d // (ny * nx), (d // nx) % ny, d % nx


def back(dims, pos, kz, ky, kx):
    nz, ny, nx = dims
    z, y, x = pos
    return (
        (lax.rem(z - kz + nz, nz) * ny + lax.rem(y - ky + ny, ny)) * nx + lax.rem(x - kx + nx, nx)
    )


def ahead(dims, pos, kz, ky, kx):
    nz, ny, nx = dims
    z, y, x = pos
    return (lax.rem(z + kz, nz) * ny + lax.rem(y + ky, ny)) * nx + lax.rem(x + kx, nx)


ANY = pl.BlockSpec(memory_space=pl.ANY)
VM = pl.BlockSpec(memory_space=pltpu.VMEM)


def project_kernel(dims, keys, rows, *refs):
    nz, ny, nx = dims
    count = len(keys)
    a_refs, b_refs = refs[:count], refs[count : 2 * count]
    w_ref, keep_ref, send_ref, held, weight, sems, wsem = refs[2 * count :]
    depth = held.shape[1]
    half = depth // 2
    pos = position(dims)
    sec = lax.axis_index("sec")
    wcopy = pltpu.make_async_copy(w_ref, weight, wsem)
    wcopy.start()
    copies = []
    for i, (ky, kx) in enumerate(keys):
        for kz in range(nz):
            place = pl.multiple_of(back(dims, pos, kz, ky, kx) * rows, rows)
            for h, group in enumerate((a_refs, b_refs)):
                copies.append(
                    pltpu.make_async_copy(
                        group[i].at[pl.ds(kz * rows, rows)],
                        held.at[pl.ds(place, rows), pl.ds(h * half, half)],
                        sems.at[(i * nz + kz) * 2 + h],
                    )
                )
    for c in copies:
        c.start()
    wcopy.wait()
    for c in copies:
        c.wait()
    total = jnp.dot(held[...], weight[...], preferred_element_type=F32)
    part = total.shape[1] // 2
    low, high = total[:, :part], total[:, part:]
    keep_ref[...] = jnp.where(sec == 0, low, high)
    send_ref[...] = jnp.where(sec == 0, high, low)


def project(a, b, weight, dims, rows):
    keys = sorted(a)
    n = dims[0] * dims[1] * dims[2]
    depth, cols = weight.shape
    out = jax.ShapeDtypeStruct((n * rows, cols // 2), F32)
    return pl.pallas_call(
        functools.partial(project_kernel, dims, keys, rows),
        out_shape=(out, out),
        in_specs=[ANY] * (2 * len(keys) + 1),
        out_specs=(VM, VM),
        scratch_shapes=[
            pltpu.VMEM((n * rows, depth), BF),
            pltpu.VMEM((depth, cols), BF),
            pltpu.SemaphoreType.DMA((2 * n,)),
            pltpu.SemaphoreType.DMA,
        ],
        compiler_params=pltpu.CompilerParams(vmem_limit_bytes=48 * 1024 * 1024),
        cost_estimate=pl.CostEstimate(
            flops=2 * n * rows * depth * cols,
            bytes_accessed=2 * depth * (cols + n * rows),
            transcendentals=0,
        ),
        name="project",
    )(*[a[k] for k in keys], *[b[k] for k in keys], weight)


STEPS = 8


def expert_kernel(dims, keys, rows, eps, *refs):
    nz, ny, nx = dims
    n = nz * ny * nx
    count = len(keys)
    groups = [refs[i * count : (i + 1) * count] for i in range(4)]
    (
        mask_ref,
        gain_ref,
        router_ref,
        gate_ref,
        up_ref,
        down_ref,
        keep_refs,
        send_refs,
        own_ref,
        held,
        gate_w,
        up_w,
        down_w,
        gate_acc,
        up_acc,
        route_acc,
        square,
        hidden,
        hidden_a,
        hidden_b,
        xsems,
        gsems,
        dsems,
    ) = (
        refs[4 * count],
        refs[4 * count + 1],
        refs[4 * count + 2],
        refs[4 * count + 3],
        refs[4 * count + 4],
        refs[4 * count + 5],
        refs[4 * count + 6 : 4 * count + 8],
        refs[4 * count + 8 : 4 * count + 10],
        *refs[4 * count + 10 :],
    )
    total_rows, width = held.shape
    half_rows = total_rows // 2
    part = width // n // 2
    pos = position(dims)
    me = lax.axis_index("dev")
    sec = lax.axis_index("sec")
    step = width // STEPS
    weight_copies = []
    for c in range(STEPS):
        span = pl.ds(c * step, step)
        weight_copies.append(
            (
                pltpu.make_async_copy(gate_ref.at[0, span], gate_w.at[span], gsems.at[c]),
                pltpu.make_async_copy(up_ref.at[0, span], up_w.at[span], gsems.at[STEPS + c]),
            )
        )
    copies = []
    if part % 128:
        copies.append(pltpu.make_async_copy(groups[0][0], held, xsems.at[0]))
    for i, (ky, kx) in enumerate(keys if part % 128 == 0 else ()):
        for kz in range(nz):
            owner = back(dims, pos, kz, ky, kx)
            for g in range(4):
                whose = sec if g < 2 else 1 - sec
                column = pl.multiple_of((owner * 2 + whose) * part, part)
                copies.append(
                    pltpu.make_async_copy(
                        groups[g][i].at[pl.ds(kz * half_rows, half_rows)],
                        held.at[pl.ds((g % 2) * half_rows, half_rows), pl.ds(column, part)],
                        xsems.at[(i * nz + kz) * 4 + g],
                    )
                )
    for c in copies:
        c.start()
    for pair in weight_copies:
        for c in pair:
            c.start()
    halves = []
    for h, whose in enumerate((sec, 1 - sec)):
        span = pl.ds(pl.multiple_of(whose * (width // 2), width // 2), width // 2)
        halves.append(pltpu.make_async_copy(down_ref.at[0, :, span], down_w.at[h], dsems.at[h]))
    for c in halves:
        c.start()
    for c in copies:
        c.wait()
    gate_acc[...] = jnp.zeros_like(gate_acc)
    up_acc[...] = jnp.zeros_like(up_acc)
    route_acc[...] = jnp.zeros_like(route_acc)
    square[...] = jnp.zeros_like(square)

    def body(c, carry):
        span = pl.ds(pl.multiple_of(c * step, step), step)
        x = held[:, span].astype(F32)
        square[...] += jnp.sum(x * x, axis=1, keepdims=True)
        scaled = (x * gain_ref[:, span]).astype(BF)
        pltpu.make_async_copy(gate_ref.at[0, span], gate_w.at[span], gsems.at[c]).wait()
        pltpu.make_async_copy(up_ref.at[0, span], up_w.at[span], gsems.at[STEPS + c]).wait()
        gate_acc[...] += jnp.dot(scaled, gate_w[span], preferred_element_type=F32)
        up_acc[...] += jnp.dot(scaled, up_w[span], preferred_element_type=F32)
        route_acc[...] += jnp.dot(scaled, router_ref[span], preferred_element_type=F32)
        return carry

    lax.fori_loop(0, STEPS, body, 0)
    inverse = lax.rsqrt(square[:, :1] * (1.0 / width) + eps)
    mask = mask_ref[...].astype(F32)
    live = mask > 0.5
    logits = jnp.where(live, route_acc[...] * inverse, masked_score)
    top = jnp.max(logits, axis=1, keepdims=True)
    powers = jnp.where(live, jnp.exp(logits - top), 0.0)
    lane = lax.broadcasted_iota(jnp.int32, powers.shape, 1)
    mine = jnp.sum(jnp.where(lane == me, powers, 0.0), axis=1, keepdims=True)
    weight = mine / jnp.sum(powers, axis=1, keepdims=True)
    gate = gate_acc[...] * inverse
    up = up_acc[...] * inverse
    hidden[...] = (gate / (1.0 + jnp.exp(-gate)) * up * weight).astype(BF)
    own_ref[...] = held[pl.ds(pl.multiple_of(me * rows, rows), rows)]
    for kz in range(nz):
        for ky in range(ny):
            for kx in range(nx):
                place = pl.multiple_of(ahead(dims, pos, kz, ky, kx) * rows, rows)
                block = hidden[pl.ds(place, rows)]
                hidden_a[pl.ds(((kx * ny + ky) * nz + kz) * rows, rows)] = block
                hidden_b[pl.ds(((ky * nx + kx) * nz + kz) * rows, rows)] = block
    quarter = width // 4
    for c in halves:
        c.wait()
    for h, outs in enumerate((keep_refs, send_refs)):
        for q, source in enumerate((hidden_a, hidden_b)):
            for t in range(2):
                wide = quarter // 2
                outs[q][:, t * wide : (t + 1) * wide] = jnp.dot(
                    source[...],
                    down_w[h, :, pl.ds(q * quarter + t * wide, wide)],
                    preferred_element_type=F32,
                ).astype(BF)


def in_order(own, other, dims):
    nz, ny, nx = dims
    pos = position(dims)
    sides = []
    for pair in (own, other):
        parts = []
        for found in pair:
            stacked = jnp.stack([jnp.stack([found[(b, a)] for a in range(nx)]) for b in range(ny)])
            half = stacked.shape[2] // nz
            stacked = stacked.reshape(ny, nx, nz, half, -1).transpose(2, 0, 1, 3, 4)
            for axis in range(3):
                order = (pos[axis] - jnp.arange(dims[axis], dtype=jnp.int32)) % dims[axis]
                stacked = jnp.take(stacked, order, axis=axis)
            parts.append(stacked.reshape(nz * ny * nx, half, -1))
        sides.append(jnp.concatenate(parts, axis=1))
    first = lax.axis_index("sec") == 0
    both = jnp.stack([jnp.where(first, sides[0], sides[1]), jnp.where(first, sides[1], sides[0])])
    return both.transpose(2, 1, 0, 3).reshape(both.shape[2], -1)


def experts(own, other, mask, gain, router, gate, up, down, dims, rows):
    keys = sorted(own[0])
    n = dims[0] * dims[1] * dims[2]
    total_rows = n * rows
    _, width, units = gate.shape
    quarter = width // 4
    lanes = router.shape[1]
    result = jax.ShapeDtypeStruct((total_rows, quarter), BF)
    arrays = [g[k] for g in (*own, *other) for k in keys]
    if (width // n // 2) % 128:
        arrays = [in_order(own, other, dims)] * len(arrays)
    outs = pl.pallas_call(
        functools.partial(expert_kernel, dims, keys, rows, 1e-6),
        out_shape=(result,) * 4 + (jax.ShapeDtypeStruct((rows, width), BF),),
        in_specs=[ANY] * len(arrays) + [VM, VM, VM, ANY, ANY, ANY],
        out_specs=(VM,) * 5,
        scratch_shapes=[
            pltpu.VMEM((total_rows, width), BF),
            pltpu.VMEM((width, units), BF),
            pltpu.VMEM((width, units), BF),
            pltpu.VMEM((2, units, width // 2), BF),
            pltpu.VMEM((total_rows, units), F32),
            pltpu.VMEM((total_rows, units), F32),
            pltpu.VMEM((total_rows, lanes), F32),
            pltpu.VMEM((total_rows, 128), F32),
            pltpu.VMEM((total_rows, units), BF),
            pltpu.VMEM((total_rows, units), BF),
            pltpu.VMEM((total_rows, units), BF),
            pltpu.SemaphoreType.DMA((4 * n,)),
            pltpu.SemaphoreType.DMA((2 * STEPS,)),
            pltpu.SemaphoreType.DMA((2,)),
        ],
        compiler_params=pltpu.CompilerParams(vmem_limit_bytes=56 * 1024 * 1024),
        cost_estimate=pl.CostEstimate(
            flops=6 * total_rows * width * units,
            bytes_accessed=6 * width * units + 6 * total_rows * width,
            transcendentals=0,
        ),
        name="experts",
    )(*arrays, mask, gain, router, gate, up, down)
    return outs[:2], outs[2:4], outs[4]


def attention(queries, key_cache, value_cache, new_key, new_value, cache_lengths):
    row_count = queries.shape[0]
    group_count = new_key.shape[1] // HEAD
    per_group = queries.shape[1] // (group_count * HEAD)
    cache_span = key_cache.shape[1]
    score_scale = 1.0 / math.sqrt(HEAD)
    query_heads = queries.reshape(row_count, group_count, per_group, HEAD)
    fresh_keys = new_key.reshape(row_count, group_count, HEAD)
    fresh_values = new_value.reshape(row_count, group_count, HEAD)
    fresh_score = (
        jnp.einsum("rgqh,rgh->rgq", query_heads, fresh_keys, preferred_element_type=F32)
        * score_scale
    )
    keys_whole = key_cache.reshape(row_count, cache_span, group_count, HEAD)
    scores = (
        jnp.einsum("rgqh,rcgh->rgqc", query_heads, keys_whole, preferred_element_type=F32)
        * score_scale
    )
    positions = jnp.arange(cache_span, dtype=jnp.int32)
    live_mask = positions[None, :] < cache_lengths[:, None]
    scores = jnp.where(live_mask[:, None, None, :], scores, masked_score)
    row_max = jnp.maximum(jnp.max(scores, axis=-1), fresh_score)
    exp_cache = jnp.exp(scores - row_max[..., None])
    denominator = jnp.sum(exp_cache, axis=-1) + jnp.exp(fresh_score - row_max)
    weights_bf = (exp_cache / denominator[..., None]).astype(BF)
    values_whole = value_cache.reshape(row_count, cache_span, group_count, HEAD)
    attended = jnp.einsum("rgqc,rcgh->rgqh", weights_bf, values_whole, preferred_element_type=F32)
    fresh_weight = (jnp.exp(fresh_score - row_max) / denominator).astype(BF)
    attended = (
        attended
        + fresh_weight.astype(F32)[..., None] * fresh_values.astype(F32)[:, :, None, :]
    )
    return attended.reshape(row_count, group_count * per_group * HEAD).astype(BF)


def local(
    dims,
    queries,
    key_cache,
    value_cache,
    new_key,
    new_value,
    cache_lengths,
    residual_in,
    out_weight,
    norm_gain,
    router_weight,
    expert_ids,
    gate_weight,
    up_weight,
    down_weight,
):
    nz, ny, nx = dims
    n = nz * ny * nx
    rows, width = residual_in.shape
    expert_total = router_weight.shape[1]
    sec = lax.axis_index("sec")
    lanes = -(-expert_total // 128) * 128
    part = width // n // 2
    chosen = jnp.any(
        expert_ids[:, :, None] == jnp.arange(lanes, dtype=jnp.int32)[None, None, :], axis=1
    ).astype(BF)
    mine = lax.dynamic_index_in_dim(
        residual_in.reshape(rows, n, 2, part), sec, axis=2, keepdims=False
    )
    outgoing = jnp.concatenate(
        [jnp.swapaxes(mine, 0, 1), jnp.broadcast_to(chosen[None], (n, rows, lanes))], axis=2
    )
    incoming = lax.all_to_all(outgoing, "dev", split_axis=0, concat_axis=0, tiled=True)
    residual = incoming[:, :, :part].reshape(n * rows, part)
    mask = incoming[:, :, part:].reshape(n * rows, lanes)

    attended = attention(queries, key_cache, value_cache, new_key, new_value, cache_lengths)
    middle = attended.shape[1] // 2
    a = spread(attended[:, :middle], dims, "x", "y")
    b = spread(attended[:, middle:], dims, "y", "x")
    keep, send = project(a, b, out_weight, dims, rows)
    projected = (keep + swap_sec(send)).astype(BF)
    mixed = (residual.astype(F32) + projected.astype(F32)).astype(BF)

    half_rows = n * rows // 2
    ma = spread(mixed[:half_rows], dims, "x", "y")
    mb = spread(mixed[half_rows:], dims, "y", "x")
    other_a = {k: swap_sec(v) for k, v in ma.items()}
    other_b = {k: swap_sec(v) for k, v in mb.items()}
    router = jnp.pad(router_weight, ((0, 0), (0, lanes - expert_total)))
    keeps, sends, own_mixed = experts(
        (ma, mb),
        (other_a, other_b),
        mask,
        norm_gain.reshape(1, width),
        router,
        gate_weight,
        up_weight,
        down_weight,
        dims,
        rows,
    )
    finals = []
    for q, (first, second) in enumerate((("x", "y"), ("y", "x"))):
        extent = dict(zip("zyx", dims))
        nf, ns = extent[first], extent[second]
        quarter = keeps[q].shape[1]
        summed = keeps[q].astype(F32) + swap_sec(sends[q]).astype(F32)
        summed = summed.reshape(nf, ns * nz * rows, quarter)
        total = summed[0]
        for k in range(1, nf):
            total = total + rotate(summed[k].astype(BF), dims, first, k).astype(F32)
        total = total.reshape(ns, nz * rows, quarter)
        inner = total[0]
        for k in range(1, ns):
            inner = inner + rotate(total[k].astype(BF), dims, second, k).astype(F32)
        inner = inner.reshape(nz, rows, quarter)
        last = inner[0]
        for k in range(1, nz):
            last = last + rotate(inner[k].astype(BF), dims, "z", k).astype(F32)
        finals.append(last)
    own_half = lax.dynamic_slice_in_dim(own_mixed, sec * (width // 2), width // 2, 1)
    done = (own_half.astype(F32) + jnp.concatenate(finals, axis=1)).astype(BF)
    other = swap_sec(done)
    return jnp.where(
        sec == 0, jnp.concatenate([done, other], axis=1), jnp.concatenate([other, done], axis=1)
    )


def solution(mesh):
    dims = grid_of(mesh.shape["dev"])
    placed = (
        P("dev", "sec"),
        P("dev", None, "sec"),
        P("dev", None, "sec"),
        P("dev", "sec"),
        P("dev", "sec"),
        P("dev"),
        P("dev", None),
        P("sec", "dev"),
        P(),
        P(),
        P("dev", None),
        P("dev", None, "sec"),
        P("dev", None, "sec"),
        P("dev", "sec", None),
    )
    return jax.shard_map(
        functools.partial(local, dims),
        mesh=mesh,
        in_specs=placed,
        out_specs=P("dev", None),
        check_vma=False,
    )
```

```python
import functools
import math

import jax
import jax.numpy as jnp
from jax import lax
from jax.experimental import pallas as pl
from jax.experimental.pallas import tpu as pltpu
from jax.sharding import PartitionSpec as P

HEAD = 128
masked_score = -1e30
BF = jnp.bfloat16
F32 = jnp.float32


def grid_of(n):
    known = {16: (4, 2, 2), 64: (4, 4, 4)}
    return known.get(n, (n, 1, 1))


def code_of(dims, kz, ky, kx):
    return (kz * dims[1] + ky) * dims[2] + kx


def trade(value, dims, kz=0, ky=0, kx=0):
    code = code_of(dims, kz, ky, kx)
    n = dims[0] * dims[1] * dims[2]
    return lax.ppermute(value, "dev", [(d, d ^ code) for d in range(n)])


def along_z(dims):
    return sorted(range(1, dims[0]), key=lambda k: (k == 1, k))


def swap_sec(value):
    return lax.ppermute(value, "sec", [(0, 1), (1, 0)])


def planes(a, b, dims):
    _, ny, nx = dims
    first, second, third = [], [], []
    near_a = {kx: trade(a, dims, kx=kx) for kx in range(1, nx)}
    near_b = {ky: trade(b, dims, ky=ky) for ky in range(1, ny)}
    first += [((0, kx), 0, v) for kx, v in near_a.items()]
    first += [((ky, 0), 1, v) for ky, v in near_b.items()]
    second += [((ky, 0), 0, trade(a, dims, ky=ky)) for ky in range(1, ny)]
    second += [((0, kx), 1, trade(b, dims, kx=kx)) for kx in range(1, nx)]
    third += [
        ((ky, kx), 0, trade(v, dims, ky=ky)) for kx, v in near_a.items() for ky in range(1, ny)
    ]
    third += [
        ((ky, kx), 1, trade(v, dims, kx=kx)) for ky, v in near_b.items() for kx in range(1, nx)
    ]
    return first, second, third


ANY = pl.BlockSpec(memory_space=pl.ANY)
VM = pl.BlockSpec(memory_space=pltpu.VMEM)
HBM = pl.BlockSpec(memory_space=pltpu.HBM)
MIB = 1024 * 1024


def project_kernel(pieces, rows, count, *refs):
    arrays = refs[:count]
    w_ref, keep_ref, send_ref, held, sems = refs[count:]
    half = held.shape[1] // 2
    me = lax.axis_index("dev")
    sec = lax.axis_index("sec")
    copies = []
    for i, (which, offset, code, column) in enumerate(pieces):
        place = pl.multiple_of((me ^ code) * rows, rows)
        copies.append(
            pltpu.make_async_copy(
                arrays[which].at[pl.ds(offset, rows), pl.ds(0, half)],
                held.at[pl.ds(place, rows), pl.ds(column * half, half)],
                sems.at[i],
            )
        )
    for c in copies:
        c.start()
    for c in copies:
        c.wait()
    total = jnp.dot(held[...], w_ref[...], preferred_element_type=F32)
    part = total.shape[1] // 2
    low, high = total[:, :part], total[:, part:]
    keep_ref[...] = jnp.where(sec == 0, low, high)
    send_ref[...] = jnp.where(sec == 0, high, low)


def project(arrays, pieces, weight, n, rows):
    depth, cols = weight.shape
    out = jax.ShapeDtypeStruct((n * rows, cols // 2), F32)
    return pl.pallas_call(
        functools.partial(project_kernel, pieces, rows, len(arrays)),
        out_shape=(out, out),
        in_specs=[ANY] * len(arrays) + [VM],
        out_specs=(VM, VM),
        scratch_shapes=[
            pltpu.VMEM((n * rows, depth), BF),
            pltpu.SemaphoreType.DMA((len(pieces),)),
        ],
        compiler_params=pltpu.CompilerParams(vmem_limit_bytes=(4 + n // 2) * MIB),
        cost_estimate=pl.CostEstimate(
            flops=2 * n * rows * depth * cols,
            bytes_accessed=2 * depth * (cols + n * rows),
            transcendentals=0,
        ),
        name="project",
    )(*arrays, weight)


STEPS = 8


def expert_kernel(dims, pieces, rows, eps, count, *refs):
    nz, ny, nx = dims
    arrays = refs[:count]
    (
        mask_ref,
        gain_ref,
        router_ref,
        gate_ref,
        up_ref,
        down_ref,
        keep_near,
        keep_far,
        send_near,
        send_far,
        own_ref,
        held,
        acc,
        route_acc,
        square,
        hidden,
        hidden_a,
        hidden_b,
        xsems,
    ) = refs[count:]
    width = held.shape[1]
    units = down_ref.shape[1]
    part = width // (nz * ny * nx) // 2
    me = lax.axis_index("dev")
    sec = lax.axis_index("sec")
    step = width // STEPS

    copies = []
    if not pieces:
        copies.append(pltpu.make_async_copy(arrays[0], held, xsems.at[0]))
    for i, (which, offset, length, code, side, start) in enumerate(pieces):
        whose = sec if side == 0 else 1 - sec
        column = pl.multiple_of(((me ^ code) * 2 + whose) * part, part)
        copies.append(
            pltpu.make_async_copy(
                arrays[which].at[pl.ds(offset, length)],
                held.at[pl.ds(start, length), pl.ds(column, part)],
                xsems.at[i],
            )
        )
    for c in copies:
        c.start()
    for c in copies:
        c.wait()
    acc[...] = jnp.zeros_like(acc)
    route_acc[...] = jnp.zeros_like(route_acc)
    square[...] = jnp.zeros_like(square)

    def body(c, carry):
        span = pl.ds(pl.multiple_of(c * step, step), step)
        x = held[:, span].astype(F32)
        total = square[...]
        for t in range(step // 128):
            piece = x[:, t * 128 : (t + 1) * 128]
            total = total + piece * piece
        square[...] = total
        scaled = (x * gain_ref[:, span]).astype(BF)
        both = jnp.concatenate([gate_ref[0, span], up_ref[0, span]], axis=1)
        acc[...] += jnp.dot(scaled, both, preferred_element_type=F32)
        route_acc[...] += lax.dot_general(
            scaled, router_ref[:, span], (((1,), (1,)), ((), ())), preferred_element_type=F32
        )
        return carry

    lax.fori_loop(0, STEPS, body, 0)
    mean = jnp.sum(square[...], axis=1, keepdims=True) * (1.0 / width)
    inverse = lax.rsqrt(mean + eps)
    live = mask_ref[:, : route_acc.shape[1]].astype(F32) > 0.5
    logits = jnp.where(live, route_acc[...] * inverse, masked_score)
    top = jnp.max(logits, axis=1, keepdims=True)
    powers = jnp.where(live, jnp.exp(logits - top), 0.0)
    lane = lax.broadcasted_iota(jnp.int32, powers.shape, 1)
    mine = jnp.sum(jnp.where(lane == me, powers, 0.0), axis=1, keepdims=True)
    weight = mine / jnp.sum(powers, axis=1, keepdims=True)
    gate = acc[:, :units] * inverse
    up = acc[:, units:] * inverse
    hidden[...] = (gate / (1.0 + jnp.exp(-gate)) * up * weight).astype(BF)
    own_ref[...] = held[pl.ds(pl.multiple_of(me * rows, rows), rows)]
    for kz in range(nz):
        for ky in range(ny):
            for kx in range(nx):
                place = pl.multiple_of((me ^ code_of(dims, kz, ky, kx)) * rows, rows)
                block = hidden[pl.ds(place, rows)]
                hidden_a[pl.ds(((kx * ny + ky) * nz + kz) * rows, rows)] = block
                hidden_b[pl.ds(((ky * nx + kx) * nz + kz) * rows, rows)] = block
    quarter = width // 4
    wide = quarter // 2
    for h, near, far in ((1, send_near, send_far), (0, keep_near, keep_far)):
        near_cut = hidden.shape[0] // nx
        far_cut = hidden.shape[0] - near_cut
        for q, (source, first) in enumerate(((hidden_a, nx), (hidden_b, ny))):
            cut = source.shape[0] // first
            rest = source.shape[0] - cut
            for t in range(2):
                whose = sec if h == 0 else 1 - sec
                place = pl.multiple_of(whose * 2 * quarter + q * quarter + t * wide, wide)
                found = jnp.dot(
                    source[...],
                    down_ref[0, :, pl.ds(place, wide)],
                    preferred_element_type=F32,
                ).astype(BF)
                span = slice(t * wide, (t + 1) * wide)
                near[q * near_cut : q * near_cut + cut, span] = found[:cut]
                far[q * far_cut : q * far_cut + rest, span] = found[cut:]


def in_order(arrays, pieces, n, total_rows, part):
    me = lax.axis_index("dev")
    sec = lax.axis_index("sec")
    held = jnp.zeros((total_rows, n * 2 * part), BF)
    for which, offset, length, code, side, start in pieces:
        whose = sec if side == 0 else 1 - sec
        column = ((me ^ code) * 2 + whose) * part
        held = lax.dynamic_update_slice(
            held, arrays[which][offset : offset + length], (start, column)
        )
    return held


def experts(arrays, pieces, mask, gain, router, gate, up, down, dims, rows):
    nz, ny, nx = dims
    n = nz * ny * nx
    total_rows = n * rows
    _, width, units = gate.shape
    quarter = width // 4
    lanes = router.shape[0]
    near = total_rows // nx + total_rows // ny
    far = 2 * total_rows - near
    part = width // n // 2
    if part % 128:
        arrays = [in_order(arrays, pieces, n, total_rows, part)]
        pieces = ()
    shapes = [jax.ShapeDtypeStruct((r, quarter), BF) for r in (near, far, near, far)]
    return pl.pallas_call(
        functools.partial(expert_kernel, dims, pieces, rows, 1e-6, len(arrays)),
        out_shape=(*shapes, jax.ShapeDtypeStruct((rows, width), BF)),
        in_specs=[ANY] * len(arrays) + [VM] * 6,
        out_specs=(VM,) * 5,
        scratch_shapes=[
            pltpu.VMEM((total_rows, width), BF),
            pltpu.VMEM((total_rows, 2 * units), F32),
            pltpu.VMEM((total_rows, lanes), F32),
            pltpu.VMEM((total_rows, 128), F32),
            pltpu.VMEM((total_rows, units), BF),
            pltpu.VMEM((total_rows, units), BF),
            pltpu.VMEM((total_rows, units), BF),
            pltpu.SemaphoreType.DMA((max(1, len(pieces)),)),
        ],
        compiler_params=pltpu.CompilerParams(vmem_limit_bytes=(6 + n // 2) * MIB),
        cost_estimate=pl.CostEstimate(
            flops=6 * total_rows * width * units,
            bytes_accessed=6 * width * units + 6 * total_rows * width,
            transcendentals=0,
        ),
        name="experts",
    )(*arrays, mask, gain, router, gate, up, down)


GROUP = 4
CHUNK = 128


def attend_kernel(dims, lanes, *refs):
    (
        len_ref,
        ids_ref,
        q_ref,
        nk_ref,
        nv_ref,
        extra_ref,
        k_ref,
        v_ref,
        *outs,
        keys,
        values,
        apart,
        joined,
        ksems,
        vsems,
    ) = refs
    b_ref, sends = outs[0], outs[1:]
    rows, span, cols = keys.shape
    heads = q_ref.shape[1] // HEAD
    half = b_ref.shape[1]
    groups = cols // HEAD
    per = heads // groups
    me = lax.axis_index("dev")
    sec = lax.axis_index("sec")

    def fetch(r, source, target, sem):
        live = (len_ref[r] + CHUNK - 1) // CHUNK * CHUNK
        part = pl.ds(0, pl.multiple_of(live, CHUNK))
        return pltpu.make_async_copy(source.at[r, part], target.at[r, part], sem.at[r])

    for start in range(0, rows, GROUP):
        for r in range(start, start + GROUP):
            fetch(r, k_ref, keys, ksems).start()
        values[pl.ds(start, GROUP)] = jnp.zeros((GROUP, span, cols), BF)
        for r in range(start, start + GROUP):
            fetch(r, v_ref, values, vsems).start()

    lane_ids = lax.broadcasted_iota(jnp.int32, (lanes, rows), 0)
    chosen = jnp.zeros((lanes, rows), F32)
    for k in range(ids_ref.shape[0]):
        chosen = jnp.where(lane_ids == ids_ref[k : k + 1, :], 1.0, chosen)
    chosen = chosen.T.astype(BF)
    plane = dims[1] * dims[2]
    for kz in range(dims[0]):
        target = sends[kz]
        for c in range(plane):
            owner = me ^ (kz * plane + c)
            if len(extra_ref.shape) == 3:
                block = extra_ref[owner]
            else:
                place = pl.multiple_of((owner * 2 + sec) * 128, 128)
                block = extra_ref[:, pl.ds(place, 128)]
            target[:, half + c * 128 : half + (c + 1) * 128] = block
        target[:, half + plane * 128 :] = chosen

    for h in range(heads):
        apart[pl.ds(h * rows, rows)] = q_ref[:, h * HEAD : (h + 1) * HEAD].astype(F32)
    fresh_k = nk_ref[...].astype(F32)
    fresh_v = nv_ref[...].astype(F32)
    head = lax.broadcasted_iota(jnp.int32, (heads, HEAD), 0)
    belongs = [(head >= g * per) & (head < (g + 1) * per) for g in range(groups)]
    place = lax.broadcasted_iota(jnp.int32, (heads, span), 1)
    scale = 1.0 / math.sqrt(HEAD)

    def of_group(wide):
        found = jnp.broadcast_to(wide[:, :HEAD], (heads, HEAD))
        for g in range(1, groups):
            piece = wide[:, g * HEAD : (g + 1) * HEAD]
            found = jnp.where(belongs[g], jnp.broadcast_to(piece, (heads, HEAD)), found)
        return found

    for start in range(0, rows, GROUP):
        group = range(start, start + GROUP)
        for r in group:
            fetch(r, k_ref, keys, ksems).wait()
            fetch(r, v_ref, values, vsems).wait()
        queries, scores = {}, {}
        for r in group:
            q = apart[pl.ds(r, heads, stride=rows), :]
            queries[r] = q
            wide = jnp.concatenate([jnp.where(m, q, 0.0) for m in belongs], axis=1)
            scores[r] = lax.dot_general(
                wide.astype(BF), keys[r], (((1,), (1,)), ((), ())), preferred_element_type=F32
            )
        for r in group:
            s = jnp.where(place < len_ref[r], scores[r] * scale, masked_score)
            own = jnp.sum(queries[r] * of_group(fresh_k[r : r + 1]), axis=1, keepdims=True) * scale
            top = jnp.maximum(jnp.max(s, axis=1, keepdims=True), own)
            power = jnp.exp(s - top)
            own_power = jnp.exp(own - top)
            total = jnp.sum(power, axis=1, keepdims=True) + own_power
            mixed = jnp.dot(power.astype(BF), values[r], preferred_element_type=F32)
            picked = mixed[:, :HEAD]
            for g in range(1, groups):
                picked = jnp.where(belongs[g], mixed[:, g * HEAD : (g + 1) * HEAD], picked)
            picked = (picked + own_power * of_group(fresh_v[r : r + 1])) / total
            joined[pl.ds(r, heads, stride=rows), :] = picked
    for h in range(heads):
        block = joined[pl.ds(h * rows, rows)].astype(BF)
        at = h * HEAD
        for target in sends if at < half else (b_ref,):
            target[:, at % half : at % half + HEAD] = block


def attention(
    queries, key_cache, value_cache, new_key, new_value, cache_lengths, ids, extra, lanes, dims
):
    rows, span, cols = key_cache.shape
    width = queries.shape[1]
    heads = width // HEAD
    half = width // 2
    side = dims[1] * dims[2] * 128 + lanes
    outs = [(rows, half)] + [(rows, half + side)] * dims[0]
    return pl.pallas_call(
        functools.partial(attend_kernel, dims, lanes),
        out_shape=tuple(jax.ShapeDtypeStruct(o, BF) for o in outs),
        in_specs=[pl.BlockSpec(memory_space=pltpu.SMEM)] + [VM] * 5 + [HBM, HBM],
        out_specs=(VM,) * len(outs),
        scratch_shapes=[
            pltpu.VMEM((rows, span, cols), BF),
            pltpu.VMEM((rows, span, cols), BF),
            pltpu.VMEM((rows * heads, HEAD), F32),
            pltpu.VMEM((rows * heads, HEAD), F32),
            pltpu.SemaphoreType.DMA((rows,)),
            pltpu.SemaphoreType.DMA((rows,)),
        ],
        compiler_params=pltpu.CompilerParams(vmem_limit_bytes=60 * MIB),
        cost_estimate=pl.CostEstimate(
            flops=4 * rows * heads * span * cols,
            bytes_accessed=4 * rows * span * cols,
            transcendentals=rows * heads * span,
        ),
        name="attend",
    )(cache_lengths, ids, queries, new_key, new_value, extra, key_cache, value_cache)


def pack_kernel(dims, lanes, *refs):
    nz, ny, nx = dims
    lines, outs = refs[:nz], refs[nz:]
    mine_ref, xa, ya = outs[0], outs[1 : nx], outs[nx:]
    rows = lines[0].shape[0]
    plane = ny * nx * 128
    half = lines[0].shape[1] - plane - lanes
    for kz in range(nz):
        span = slice(kz * rows, (kz + 1) * rows)
        source = lines[kz]

        def block(ky, kx):
            at = half + (ky * nx + kx) * 128
            return source[:, at : at + 128]

        a, mask = source[:, :half], source[:, half + plane :]
        mine_ref[span, :half] = a
        mine_ref[span, half : half + 128] = block(0, 0)
        mine_ref[span, half + 128 :] = mask
        for kx in range(1, nx):
            xa[kx - 1][span, :half] = a
            for ky in range(ny):
                xa[kx - 1][span, half + ky * 128 : half + (ky + 1) * 128] = block(ky, kx)
            xa[kx - 1][span, half + ny * 128 :] = mask
        for ky in range(1, ny):
            ya[ky - 1][span, :half] = a
            ya[ky - 1][span, half : half + 128] = block(ky, 0)
            ya[ky - 1][span, half + 128 :] = mask


def pack(lines, lanes, dims):
    nz, ny, nx = dims
    rows, width = lines[0].shape
    half = width - ny * nx * 128 - lanes
    widths = [half + 128 + lanes]
    widths += [half + ny * 128 + lanes] * (nx - 1)
    widths += [half + 128 + lanes] * (ny - 1)
    outs = pl.pallas_call(
        functools.partial(pack_kernel, dims, lanes),
        out_shape=tuple(jax.ShapeDtypeStruct((nz * rows, w), BF) for w in widths),
        in_specs=[VM] * nz,
        out_specs=(VM,) * len(widths),
        compiler_params=pltpu.CompilerParams(vmem_limit_bytes=16 * MIB),
        name="pack",
    )(*lines)
    return outs[0], outs[1:nx], outs[nx:]


def arrange_kernel(pieces, rows, count, *refs):
    arrays, outs, sems = refs[:count], refs[count : count + 2], refs[count + 2]
    me = lax.axis_index("dev")
    copies = []
    for i, (which, offset, code, column, target) in enumerate(pieces):
        place = pl.multiple_of((me ^ code) * rows, rows)
        out = outs[target]
        copies.append(
            pltpu.make_async_copy(
                arrays[which].at[pl.ds(offset, rows), pl.ds(column, out.shape[1])],
                out.at[pl.ds(place, rows)],
                sems.at[i],
            )
        )
    for c in copies:
        c.start()
    for c in copies:
        c.wait()


def arrange(arrays, pieces, lanes, n, rows):
    return pl.pallas_call(
        functools.partial(arrange_kernel, pieces, rows, len(arrays)),
        out_shape=tuple(jax.ShapeDtypeStruct((n * rows, w), BF) for w in (128, lanes)),
        in_specs=[ANY] * len(arrays),
        out_specs=(VM, VM),
        scratch_shapes=[pltpu.SemaphoreType.DMA((len(pieces),))],
        compiler_params=pltpu.CompilerParams(vmem_limit_bytes=8 * MIB),
        name="arrange",
    )(*arrays)


def local(
    dims,
    queries,
    key_cache,
    value_cache,
    new_key,
    new_value,
    cache_lengths,
    residual_in,
    out_weight,
    norm_gain,
    router_weight,
    expert_ids,
    gate_weight,
    up_weight,
    down_weight,
):
    nz, ny, nx = dims
    n = nz * ny * nx
    rows, width = residual_in.shape
    total_rows = n * rows
    expert_total = router_weight.shape[1]
    sec = lax.axis_index("sec")
    lanes = -(-expert_total // 128) * 128
    part = width // n // 2

    if part % 128:
        extra = lax.dynamic_index_in_dim(
            residual_in.reshape(rows, n, 2, part), sec, axis=2, keepdims=False
        )
        extra = jnp.pad(jnp.swapaxes(extra, 0, 1), ((0, 0), (0, 0), (0, 128 - part)))
    else:
        extra = residual_in
    b_own, *a_own = attention(
        queries,
        key_cache,
        value_cache,
        new_key,
        new_value,
        cache_lengths,
        expert_ids.T,
        extra,
        lanes,
        dims,
    )
    middle = b_own.shape[1]

    steps = along_z(dims)
    a_lines = {kz: trade(a_own[kz], dims, kz=kz) for kz in steps}
    b_own, a_lines[steps[-1]] = lax.optimization_barrier((b_own, a_lines[steps[-1]]))
    b_lines = {kz: trade(b_own, dims, kz=kz) for kz in steps}
    mine, xa, ya = pack([a_own[0]] + [a_lines[kz] for kz in range(1, nz)], lanes, dims)
    arrays, pieces, places = [], [], []

    def add(array, ky, kx, column, block=None, mask=None):
        arrays.append(array)
        for kz in range(nz):
            code = code_of(dims, kz, ky, kx)
            pieces.append((len(arrays) - 1, kz * rows, code, column))
            if block is not None:
                places.append((len(arrays) - 1, kz * rows, code, block, 0))
                places.append((len(arrays) - 1, kz * rows, code, mask, 1))

    add(mine, 0, 0, 0, middle, middle + 128)
    near_a = {kx: trade(xa[kx - 1], dims, kx=kx) for kx in range(1, nx)}
    for kx, v in near_a.items():
        add(v, 0, kx, 0, middle, middle + ny * 128)
    for ky in range(1, ny):
        add(trade(ya[ky - 1], dims, ky=ky), ky, 0, 0, middle, middle + 128)
    b = jnp.concatenate([b_own] + [b_lines[kz] for kz in range(1, nz)], axis=0)
    add(b, 0, 0, 1)
    near_b = {ky: trade(b, dims, ky=ky) for ky in range(1, ny)}
    for ky, v in near_b.items():
        add(v, ky, 0, 1)
    for kx in range(1, nx):
        add(trade(b, dims, kx=kx), 0, kx, 1)
    for kx, v in near_a.items():
        for ky in range(1, ny):
            add(trade(v, dims, ky=ky), ky, kx, 0, middle + ky * 128, middle + ny * 128)
    for ky, v in near_b.items():
        for kx in range(1, nx):
            add(trade(v, dims, kx=kx), ky, kx, 1)
    keep, send = project(arrays, tuple(pieces), out_weight, n, rows)
    residual, mask = arrange(arrays, tuple(places), lanes, n, rows)
    residual = residual[:, :part]
    projected = (keep + swap_sec(send)).astype(BF)
    mixed = (residual.astype(F32) + projected.astype(F32)).astype(BF)

    half_rows = total_rows // 2
    lines = {kz: trade(mixed, dims, kz=kz) for kz in steps}
    stacked = jnp.concatenate([mixed] + [lines[kz] for kz in range(1, nz)], axis=0)
    arrays, pieces = [stacked, swap_sec(stacked)], []
    for side in range(2):
        for kz in range(nz):
            pieces.append((side, kz * total_rows, total_rows, code_of(dims, kz, 0, 0), side, 0))
    parted = stacked.reshape(nz, 2, half_rows, part)
    a, b = (parted[:, h].reshape(nz * half_rows, part) for h in range(2))
    for wave in planes(a, b, dims):
        whole = swap_sec(jnp.concatenate([array for _, _, array in wave], axis=0))
        for i, ((ky, kx), half, array) in enumerate(wave):
            for which, base, side in ((len(arrays), 0, 0), (None, i * nz * half_rows, 1)):
                for kz in range(nz):
                    pieces.append(
                        (
                            which if side == 0 else -1,
                            base + kz * half_rows,
                            half_rows,
                            code_of(dims, kz, ky, kx),
                            side,
                            half * half_rows,
                        )
                    )
            arrays.append(array)
        arrays.append(whole)
        pieces = [
            (len(arrays) - 1 if p[0] == -1 else p[0],) + tuple(p[1:]) for p in pieces
        ]
    keep_near, keep_far, send_near, send_far, own_mixed = experts(
        arrays,
        tuple(pieces),
        mask,
        norm_gain.reshape(1, width),
        router_weight.T,
        gate_weight,
        up_weight,
        down_weight,
        dims,
        rows,
    )

    quarter = width // 4
    far = keep_far.astype(F32) + swap_sec(send_far).astype(F32)
    near = keep_near.astype(F32) + swap_sec(send_near).astype(F32)
    cut_far = total_rows - total_rows // nx
    cut_near = total_rows // nx
    sums = []
    for h, (nf, ns) in enumerate(((nx, ny), (ny, nx))):
        away = (far[:cut_far] if h == 0 else far[cut_far:]).astype(BF)
        total = near[:cut_near] if h == 0 else near[cut_near:]
        size = total_rows // nf
        for k in range(1, nf):
            came = trade(
                away[(k - 1) * size : k * size], dims, **({"kx": k} if h == 0 else {"ky": k})
            )
            total = total + came.astype(F32)
        total = total.reshape(ns, nz * rows, quarter)
        inner = total[0]
        for k in range(1, ns):
            came = trade(total[k].astype(BF), dims, **({"ky": k} if h == 0 else {"kx": k}))
            inner = inner + came.astype(F32)
        sums.append(inner)
    joined = jnp.concatenate(sums, axis=1).reshape(nz, rows, width // 2)
    last = joined[0]
    came = [trade(joined[k].astype(BF), dims, kz=k) for k in steps]
    for v in came:
        last = last + v.astype(F32)
    own_half = lax.dynamic_slice_in_dim(own_mixed, sec * (width // 2), width // 2, 1)
    done = (own_half.astype(F32) + last).astype(BF)
    other = swap_sec(done)
    return jnp.where(
        sec == 0, jnp.concatenate([done, other], axis=1), jnp.concatenate([other, done], axis=1)
    )


def solution(mesh):
    dims = grid_of(mesh.shape["dev"])
    placed = (
        P("dev", "sec"),
        P("dev", None, "sec"),
        P("dev", None, "sec"),
        P("dev", "sec"),
        P("dev", "sec"),
        P("dev"),
        P("dev", None),
        P("sec", "dev"),
        P(),
        P(),
        P("dev", None),
        P("dev", None, "sec"),
        P("dev", None, "sec"),
        P("dev", "sec", None),
    )
    return jax.shard_map(
        functools.partial(local, dims),
        mesh=mesh,
        in_specs=placed,
        out_specs=P("dev", None),
        check_vma=False,
    )
```

```python
import functools
import math

import jax
import jax.numpy as jnp
from jax import lax
from jax.experimental import pallas as pl
from jax.experimental.pallas import tpu as pltpu
from jax.sharding import PartitionSpec as P

HEAD = 128
masked_score = -1e30
BF = jnp.bfloat16
F32 = jnp.float32


def grid_of(n):
    known = {16: (4, 2, 2), 64: (4, 4, 4)}
    return known.get(n, (n, 1, 1))


def code_of(dims, kz, ky, kx):
    return (kz * dims[1] + ky) * dims[2] + kx


def row_of(dims, chip):
    plane = dims[1] * dims[2]
    return (chip % plane) * dims[0] + chip // plane


def trade(value, dims, kz=0, ky=0, kx=0):
    code = code_of(dims, kz, ky, kx)
    n = dims[0] * dims[1] * dims[2]
    return lax.ppermute(value, "dev", [(d, d ^ code) for d in range(n)])


def along_z(dims):
    return sorted(range(1, dims[0]), key=lambda k: (k == 1, k))


def swap_sec(value):
    return lax.ppermute(value, "sec", [(0, 1), (1, 0)])


def planes(a, b, dims):
    _, ny, nx = dims
    first, second, third = [], [], []
    near_a = {kx: trade(a, dims, kx=kx) for kx in range(1, nx)}
    near_b = {ky: trade(b, dims, ky=ky) for ky in range(1, ny)}
    first += [((0, kx), 0, v) for kx, v in near_a.items()]
    first += [((ky, 0), 1, v) for ky, v in near_b.items()]
    second += [((ky, 0), 0, trade(a, dims, ky=ky)) for ky in range(1, ny)]
    second += [((0, kx), 1, trade(b, dims, kx=kx)) for kx in range(1, nx)]
    third += [
        ((ky, kx), 0, trade(v, dims, ky=ky)) for kx, v in near_a.items() for ky in range(1, ny)
    ]
    third += [
        ((ky, kx), 1, trade(v, dims, kx=kx)) for ky, v in near_b.items() for kx in range(1, nx)
    ]
    return first, second, third


ANY = pl.BlockSpec(memory_space=pl.ANY)
VM = pl.BlockSpec(memory_space=pltpu.VMEM)
HBM = pl.BlockSpec(memory_space=pltpu.HBM)
MIB = 1024 * 1024


def project_kernel(nz, plane, pieces, rows, *refs):
    count = len(pieces)
    arrays = refs[:count]
    w_ref, keep_ref, send_ref, held, sems = refs[count:]
    half = held.shape[1] // 2
    sec = lax.axis_index("sec")
    z = lax.axis_index("dev") // plane
    copies = []

    def move(i, source, place, size, column):
        copies.append(
            pltpu.make_async_copy(
                arrays[i].at[pl.ds(source, size), pl.ds(0, half)],
                held.at[pl.ds(place, size), pl.ds(column * half, half)],
                sems.at[len(copies)],
            )
        )

    for i, (slot, column, ordered) in enumerate(pieces):
        if ordered:
            move(i, 0, slot * nz * rows, nz * rows, column)
            continue
        for kz in range(nz):
            place = pl.multiple_of((slot * nz + (z ^ kz)) * rows, rows)
            move(i, kz * rows, place, rows, column)
    for c in copies:
        c.start()
    for c in copies:
        c.wait()
    total = jnp.dot(held[...], w_ref[...], preferred_element_type=F32)
    part = total.shape[1] // 2
    low, high = total[:, :part], total[:, part:]
    keep_ref[...] = jnp.where(sec == 0, low, high)
    send_ref[...] = jnp.where(sec == 0, high, low)


def project(arrays, pieces, weight, dims, rows):
    depth, cols = weight.shape
    nz, ny, nx = dims
    tall = nz * ny * nx * rows
    out = jax.ShapeDtypeStruct((tall, cols // 2), F32)
    return pl.pallas_call(
        functools.partial(project_kernel, nz, ny * nx, pieces, rows),
        out_shape=(out, out),
        in_specs=[ANY] * len(arrays) + [VM],
        out_specs=(VM, VM),
        scratch_shapes=[
            pltpu.VMEM((tall, depth), BF),
            pltpu.SemaphoreType.DMA((sum(1 if p[2] else nz for p in pieces),)),
        ],
        compiler_params=pltpu.CompilerParams(vmem_limit_bytes=(4 + tall // 32) * MIB),
        cost_estimate=pl.CostEstimate(
            flops=2 * tall * depth * cols,
            bytes_accessed=2 * depth * (cols + tall),
            transcendentals=0,
        ),
        name="project",
    )(*arrays, weight)


def gather_products(dims, codes, arrays, gain_ref, router_ref, gate_ref, up_ref, sums, own_ref):
    acc, route, square = sums
    nz, ny, nx = dims
    plane = ny * nx
    me = lax.axis_index("dev")
    sec = lax.axis_index("sec")
    total = acc.shape[0]
    rows = own_ref.shape[0]
    part = arrays[0].shape[1]
    place = pl.multiple_of(row_of(dims, me) * rows, rows)

    def add_products(x, at):
        power = x * x
        for t in range(0, power.shape[1], 128):
            square[...] += power[:, t : t + 128]
        scaled = (x * gain_ref[:, at]).astype(BF)
        weights = jnp.concatenate([gate_ref[0, at], up_ref[0, at]], axis=1)
        acc[...] += jnp.dot(scaled, weights, preferred_element_type=F32)
        route[...] += lax.dot_general(
            scaled, router_ref[:, at], (((1,), (1,)), ((), ())), preferred_element_type=F32
        )

    if codes is None:
        for t in range(0, gain_ref.shape[1], 256):
            add_products(arrays[0][:, t : t + 256].astype(F32), pl.ds(t, 256))
        own_ref[...] = arrays[0][pl.ds(place, rows), :]
        return
    for i, code in enumerate(codes):
        here, there = arrays[2 * i : 2 * i + 2]
        for kz in range(nz):
            span = slice(kz * total, (kz + 1) * total)
            low = jnp.where(sec == 0, here[span, :], there[span, :])
            high = jnp.where(sec == 0, there[span, :], here[span, :])
            block = jnp.concatenate([low, high], axis=1)
            owner = me ^ (kz * plane + code)
            at = pl.ds(pl.multiple_of(owner * 2 * part, 2 * part), 2 * part)
            add_products(block.astype(F32), at)
        for kz in range(nz):
            owner = me ^ (kz * plane + code)
            spot = pl.ds(pl.multiple_of(kz * total + place, rows), rows)
            mine = [here[spot, :], there[spot, :]]
            first = jnp.where(sec == 0, mine[0], mine[1])
            second = jnp.where(sec == 0, mine[1], mine[0])
            at = pl.ds(pl.multiple_of(owner * 2 * part, 2 * part), 2 * part)
            own_ref[:, at] = jnp.concatenate([first, second], axis=1)


def early_kernel(dims, codes, count, *refs):
    arrays = refs[:count]
    gain_ref, router_ref, gate_ref, up_ref, acc, route, square, own_ref = refs[count:]
    acc[...] = jnp.zeros_like(acc)
    route[...] = jnp.zeros_like(route)
    square[...] = jnp.zeros_like(square)
    own_ref[...] = jnp.zeros_like(own_ref)
    gather_products(
        dims, codes, arrays, gain_ref, router_ref, gate_ref, up_ref, (acc, route, square), own_ref
    )


def late_kernel(dims, codes, eps, count, *refs):
    nz, ny, nx = dims
    arrays = refs[:count]
    (
        gain_ref,
        router_ref,
        gate_ref,
        up_ref,
        acc_in,
        route_in,
        square_in,
        own_in,
        down_ref,
        mask_ref,
        *outs,
        own_ref,
        acc,
        route,
        square,
        hidden,
        hidden_a,
        hidden_b,
    ) = refs[count:]
    acc[...] = acc_in[...]
    route[...] = route_in[...]
    square[...] = square_in[...]
    own_ref[...] = own_in[...]
    gather_products(
        dims, codes, arrays, gain_ref, router_ref, gate_ref, up_ref, (acc, route, square), own_ref
    )
    width = gain_ref.shape[1]
    units = down_ref.shape[1]
    rows = own_ref.shape[0]
    me = lax.axis_index("dev")
    sec = lax.axis_index("sec")
    mean = jnp.sum(square[...], axis=1, keepdims=True) * (1.0 / width)
    inverse = lax.rsqrt(mean + eps)
    live = mask_ref[:, : route.shape[1]].astype(F32) > 0.5
    logits = jnp.where(live, route[...] * inverse, masked_score)
    top = jnp.max(logits, axis=1, keepdims=True)
    powers = jnp.where(live, jnp.exp(logits - top), 0.0)
    lane = lax.broadcasted_iota(jnp.int32, powers.shape, 1)
    mine = jnp.sum(jnp.where(lane == me, powers, 0.0), axis=1, keepdims=True)
    weight = mine / jnp.sum(powers, axis=1, keepdims=True)
    gate = acc[:, :units] * inverse
    up = acc[:, units:] * inverse
    hidden[...] = (gate / (1.0 + jnp.exp(-gate)) * up * weight).astype(BF)
    for kz in range(nz):
        for ky in range(ny):
            for kx in range(nx):
                chip = me ^ code_of(dims, kz, ky, kx)
                place = pl.multiple_of(row_of(dims, chip) * rows, rows)
                block = hidden[pl.ds(place, rows)]
                hidden_a[pl.ds(((kx * ny + ky) * nz + kz) * rows, rows)] = block
                hidden_b[pl.ds(((ky * nx + kx) * nz + kz) * rows, rows)] = block
    finish(dims, sec, hidden_a, hidden_b, down_ref, outs)


def finish(dims, sec, hidden_a, hidden_b, down_ref, outs):
    _, ny, nx = dims
    keep_near, keep_far, send_near, send_far = outs
    quarter = keep_near.shape[1]
    wide = quarter // 2
    near_cut = hidden_a.shape[0] // nx
    far_cut = hidden_a.shape[0] - near_cut
    for h, near, far in ((1, send_near, send_far), (0, keep_near, keep_far)):
        whose = sec if h == 0 else 1 - sec
        for q, (source, first) in enumerate(((hidden_a, nx), (hidden_b, ny))):
            cut = source.shape[0] // first
            rest = source.shape[0] - cut
            for t in range(2):
                place = pl.multiple_of(whose * 2 * quarter + q * quarter + t * wide, wide)
                found = jnp.dot(
                    source[...], down_ref[0, :, pl.ds(place, wide)], preferred_element_type=F32
                ).astype(BF)
                span = slice(t * wide, (t + 1) * wide)
                near[q * near_cut : q * near_cut + cut, span] = found[:cut]
                far[q * far_cut : q * far_cut + rest, span] = found[cut:]


def in_order(pairs, n, total_rows, part, dims):
    me = lax.axis_index("dev")
    sec = lax.axis_index("sec")
    held = jnp.zeros((total_rows, n * 2 * part), BF)
    for code, *both in pairs:
        for side, array in enumerate(both):
            for kz in range(dims[0]):
                owner = me ^ (kz * dims[1] * dims[2] + code)
                whose = sec if side == 0 else 1 - sec
                block = array[kz * total_rows : (kz + 1) * total_rows]
                held = lax.dynamic_update_slice(held, block, (0, (owner * 2 + whose) * part))
    return held


def experts(pairs, mask, gain, router, gate, up, down, dims, rows):
    nz, ny, nx = dims
    total_rows = nz * ny * nx * rows
    _, width, units = gate.shape
    count = max(1, len(pairs) // 2)
    sums = [
        jax.ShapeDtypeStruct((total_rows, 2 * units), F32),
        jax.ShapeDtypeStruct((total_rows, router.shape[0]), F32),
        jax.ShapeDtypeStruct((total_rows, 128), F32),
        jax.ShapeDtypeStruct((rows, width), BF),
    ]
    params = pltpu.CompilerParams(vmem_limit_bytes=(4 + total_rows // 64) * MIB)

    def cost(share):
        return pl.CostEstimate(
            flops=int(6 * total_rows * width * units * share),
            bytes_accessed=int(6 * width * units * share),
            transcendentals=0,
        )

    early = [v for _, *both in pairs[:count] for v in both]
    late = [v for _, *both in pairs[count:] for v in both]
    codes = [p[0] for p in pairs]
    part = pairs[0][1].shape[1]
    found = None
    if part % 128:
        late, codes = [in_order(pairs, nz * ny * nx, total_rows, part, dims)], None
        found = [jnp.zeros(v.shape, v.dtype) for v in sums]
    found = found or pl.pallas_call(
        functools.partial(early_kernel, dims, codes and codes[:count], len(early)),
        out_shape=tuple(sums),
        in_specs=[VM] * (len(early) + 4),
        out_specs=(VM,) * 4,
        compiler_params=params,
        cost_estimate=cost(0.33),
        name="experts_early",
    )(*early, gain, router, gate, up)
    near = total_rows // nx + total_rows // ny
    shapes = [
        jax.ShapeDtypeStruct((r, width // 4), BF)
        for r in (near, 2 * total_rows - near, near, 2 * total_rows - near)
    ]
    return pl.pallas_call(
        functools.partial(late_kernel, dims, codes and codes[count:], 1e-6, len(late)),
        out_shape=(*shapes, sums[3]),
        in_specs=[VM] * (len(late) + 10),
        out_specs=(VM,) * 5,
        scratch_shapes=[pltpu.VMEM(v.shape, v.dtype) for v in sums[:3]]
        + [pltpu.VMEM((total_rows, units), BF)] * 3,
        compiler_params=params,
        cost_estimate=cost(0.67),
        name="experts_late",
    )(*late, gain, router, gate, up, *found, down, mask)


GROUP = 4
CHUNK = 128


def attend_kernel(dims, lanes, *refs):
    (
        len_ref,
        ids_ref,
        q_ref,
        nk_ref,
        nv_ref,
        extra_ref,
        k_ref,
        v_ref,
        *outs,
        keys,
        values,
        apart,
        joined,
        ksems,
        vsems,
    ) = refs
    b_ref, sends = outs[0], outs[1:]
    rows, span, cols = keys.shape
    heads = q_ref.shape[1] // HEAD
    half = b_ref.shape[1]
    groups = cols // HEAD
    per = heads // groups
    me = lax.axis_index("dev")
    sec = lax.axis_index("sec")

    def fetch(r, source, target, sem):
        live = (len_ref[r] + CHUNK - 1) // CHUNK * CHUNK
        part = pl.ds(0, pl.multiple_of(live, CHUNK))
        return pltpu.make_async_copy(source.at[r, part], target.at[r, part], sem.at[r])

    for start in range(0, rows, GROUP):
        for r in range(start, start + GROUP):
            fetch(r, k_ref, keys, ksems).start()
        values[pl.ds(start, GROUP)] = jnp.zeros((GROUP, span, cols), BF)
        for r in range(start, start + GROUP):
            fetch(r, v_ref, values, vsems).start()

    lane_ids = lax.broadcasted_iota(jnp.int32, (lanes, rows), 0)
    chosen = jnp.zeros((lanes, rows), F32)
    for k in range(ids_ref.shape[0]):
        chosen = jnp.where(lane_ids == ids_ref[k : k + 1, :], 1.0, chosen)
    chosen = chosen.T.astype(BF)
    plane = dims[1] * dims[2]
    for kz in range(dims[0]):
        target = sends[kz]
        for c in range(plane):
            owner = me ^ (kz * plane + c)
            if len(extra_ref.shape) == 3:
                block = extra_ref[owner]
            else:
                place = pl.multiple_of((owner * 2 + sec) * 128, 128)
                block = extra_ref[:, pl.ds(place, 128)]
            target[:, half + c * 128 : half + (c + 1) * 128] = block
        target[:, half + plane * 128 :] = chosen

    for h in range(heads):
        apart[pl.ds(h * rows, rows)] = q_ref[:, h * HEAD : (h + 1) * HEAD].astype(F32)
    fresh_k = nk_ref[...].astype(F32)
    fresh_v = nv_ref[...].astype(F32)
    head = lax.broadcasted_iota(jnp.int32, (heads, HEAD), 0)
    belongs = [(head >= g * per) & (head < (g + 1) * per) for g in range(groups)]
    place = lax.broadcasted_iota(jnp.int32, (heads, span), 1)
    scale = 1.0 / math.sqrt(HEAD)

    def of_group(wide):
        found = jnp.broadcast_to(wide[:, :HEAD], (heads, HEAD))
        for g in range(1, groups):
            piece = wide[:, g * HEAD : (g + 1) * HEAD]
            found = jnp.where(belongs[g], jnp.broadcast_to(piece, (heads, HEAD)), found)
        return found

    for start in range(0, rows, GROUP):
        group = range(start, start + GROUP)
        for r in group:
            fetch(r, k_ref, keys, ksems).wait()
            fetch(r, v_ref, values, vsems).wait()
        queries, scores = {}, {}
        for r in group:
            q = apart[pl.ds(r, heads, stride=rows), :]
            queries[r] = q
            wide = jnp.concatenate([jnp.where(m, q, 0.0) for m in belongs], axis=1)
            scores[r] = lax.dot_general(
                wide.astype(BF), keys[r], (((1,), (1,)), ((), ())), preferred_element_type=F32
            )
        for r in group:
            s = jnp.where(place < len_ref[r], scores[r] * scale, masked_score)
            own = jnp.sum(queries[r] * of_group(fresh_k[r : r + 1]), axis=1, keepdims=True) * scale
            top = jnp.maximum(jnp.max(s, axis=1, keepdims=True), own)
            power = jnp.exp(s - top)
            own_power = jnp.exp(own - top)
            total = jnp.sum(power, axis=1, keepdims=True) + own_power
            mixed = jnp.dot(power.astype(BF), values[r], preferred_element_type=F32)
            picked = mixed[:, :HEAD]
            for g in range(1, groups):
                picked = jnp.where(belongs[g], mixed[:, g * HEAD : (g + 1) * HEAD], picked)
            picked = (picked + own_power * of_group(fresh_v[r : r + 1])) / total
            joined[pl.ds(r, heads, stride=rows), :] = picked
    for h in range(heads):
        block = joined[pl.ds(h * rows, rows)].astype(BF)
        at = h * HEAD
        for target in sends if at < half else (b_ref,):
            target[:, at % half : at % half + HEAD] = block


def attention(
    queries, key_cache, value_cache, new_key, new_value, cache_lengths, ids, extra, lanes, dims
):
    rows, span, cols = key_cache.shape
    width = queries.shape[1]
    heads = width // HEAD
    half = width // 2
    side = dims[1] * dims[2] * 128 + lanes
    outs = [(rows, half)] + [(rows, half + side)] * dims[0]
    return pl.pallas_call(
        functools.partial(attend_kernel, dims, lanes),
        out_shape=tuple(jax.ShapeDtypeStruct(o, BF) for o in outs),
        in_specs=[pl.BlockSpec(memory_space=pltpu.SMEM)] + [VM] * 5 + [HBM, HBM],
        out_specs=(VM,) * len(outs),
        scratch_shapes=[
            pltpu.VMEM((rows, span, cols), BF),
            pltpu.VMEM((rows, span, cols), BF),
            pltpu.VMEM((rows * heads, HEAD), F32),
            pltpu.VMEM((rows * heads, HEAD), F32),
            pltpu.SemaphoreType.DMA((rows,)),
            pltpu.SemaphoreType.DMA((rows,)),
        ],
        compiler_params=pltpu.CompilerParams(vmem_limit_bytes=60 * MIB),
        cost_estimate=pl.CostEstimate(
            flops=4 * rows * heads * span * cols,
            bytes_accessed=4 * rows * span * cols,
            transcendentals=rows * heads * span,
        ),
        name="attend",
    )(cache_lengths, ids, queries, new_key, new_value, extra, key_cache, value_cache)


def pack_kernel(ny, nx, lanes, extras, count, *refs):
    lines, outs = refs[:count], refs[count:]
    rows = lines[0].shape[0]
    z = lax.axis_index("dev") // (ny * nx)
    for kz, source in enumerate(lines):
        span = pl.ds(pl.multiple_of((z ^ kz) * rows, rows), rows)
        if not extras:
            outs[0][span, :] = source[...]
            continue
        mine_ref, xa, ya = outs[0], outs[1:nx], outs[nx:]
        plane = ny * nx * 128
        half = source.shape[1] - plane - lanes

        def block(ky, kx):
            at = half + (ky * nx + kx) * 128
            return source[:, at : at + 128]

        a, mask = source[:, :half], source[:, half + plane :]
        mine_ref[span, :half] = a
        mine_ref[span, half : half + 128] = block(0, 0)
        mine_ref[span, half + 128 :] = mask
        for kx in range(1, nx):
            xa[kx - 1][span, :half] = a
            for ky in range(ny):
                xa[kx - 1][span, half + ky * 128 : half + (ky + 1) * 128] = block(ky, kx)
            xa[kx - 1][span, half + ny * 128 :] = mask
        for ky in range(1, ny):
            ya[ky - 1][span, :half] = a
            ya[ky - 1][span, half : half + 128] = block(ky, 0)
            ya[ky - 1][span, half + 128 :] = mask


def pack(lines, lanes, dims, extras):
    _, ny, nx = dims
    rows, width = lines[0].shape
    widths = [width]
    if extras:
        half = width - ny * nx * 128 - lanes
        widths = [half + 128 + lanes]
        widths += [half + ny * 128 + lanes] * (nx - 1)
        widths += [half + 128 + lanes] * (ny - 1)
    outs = pl.pallas_call(
        functools.partial(pack_kernel, ny, nx, lanes, extras, len(lines)),
        out_shape=tuple(jax.ShapeDtypeStruct((len(lines) * rows, w), BF) for w in widths),
        in_specs=[VM] * len(lines),
        out_specs=(VM,) * len(widths),
        compiler_params=pltpu.CompilerParams(vmem_limit_bytes=16 * MIB),
        name="pack",
    )(*lines)
    return outs[0], outs[1:nx], outs[nx:]


def arrange_kernel(places, size, *refs):
    count = len(places)
    arrays, outs, sems = refs[:count], refs[count : count + 2], refs[count + 2]
    copies = []
    for i, (slot, *columns) in enumerate(places):
        for j, out in enumerate(outs):
            copies.append(
                pltpu.make_async_copy(
                    arrays[i].at[:, pl.ds(columns[j], out.shape[1])],
                    out.at[pl.ds(slot * size, size)],
                    sems.at[2 * i + j],
                )
            )
    for c in copies:
        c.start()
    for c in copies:
        c.wait()


def arrange(arrays, places, lanes, size):
    tall = len(places) * size
    return pl.pallas_call(
        functools.partial(arrange_kernel, places, size),
        out_shape=tuple(jax.ShapeDtypeStruct((tall, w), BF) for w in (128, lanes)),
        in_specs=[ANY] * len(arrays),
        out_specs=(VM, VM),
        scratch_shapes=[pltpu.SemaphoreType.DMA((2 * len(places),))],
        compiler_params=pltpu.CompilerParams(vmem_limit_bytes=8 * MIB),
        name="arrange",
    )(*arrays)


def merge_kernel(dims, rows, *refs):
    nz, ny, nx = dims
    parts, mask, (stacked, mask_out) = refs[:nz], refs[nz], refs[nz + 1 :]
    here = lax.axis_index("dev") % (ny * nx)
    size = nz * rows
    total = ny * nx * size
    for code in range(ny * nx):
        place = (here ^ code) * size
        span = slice(code * size, (code + 1) * size)
        mask_out[pl.ds(pl.multiple_of(place, size), size), :] = mask[span, :]
        for kz in range(nz):
            spot = pl.ds(pl.multiple_of(kz * total + place, size), size)
            stacked[spot, :] = parts[kz][span, :]


def merge(parts, mask, dims, rows):
    nz, ny, nx = dims
    total = nz * ny * nx * rows
    shapes = [(nz * total, parts[0].shape[1]), (total, mask.shape[1])]
    return pl.pallas_call(
        functools.partial(merge_kernel, dims, rows),
        out_shape=tuple(jax.ShapeDtypeStruct(t, BF) for t in shapes),
        in_specs=[VM] * (nz + 1),
        out_specs=(VM, VM),
        compiler_params=pltpu.CompilerParams(vmem_limit_bytes=16 * MIB),
        name="merge",
    )(*parts, mask)


def local(
    dims,
    queries,
    key_cache,
    value_cache,
    new_key,
    new_value,
    cache_lengths,
    residual_in,
    out_weight,
    norm_gain,
    router_weight,
    expert_ids,
    gate_weight,
    up_weight,
    down_weight,
):
    nz, ny, nx = dims
    n = nz * ny * nx
    rows, width = residual_in.shape
    total_rows = n * rows
    expert_total = router_weight.shape[1]
    sec = lax.axis_index("sec")
    lanes = -(-expert_total // 128) * 128
    part = width // n // 2

    if part % 128:
        extra = lax.dynamic_index_in_dim(
            residual_in.reshape(rows, n, 2, part), sec, axis=2, keepdims=False
        )
        extra = jnp.pad(jnp.swapaxes(extra, 0, 1), ((0, 0), (0, 0), (0, 128 - part)))
    else:
        extra = residual_in
    b_own, *a_own = attention(
        queries,
        key_cache,
        value_cache,
        new_key,
        new_value,
        cache_lengths,
        expert_ids.T,
        extra,
        lanes,
        dims,
    )
    middle = b_own.shape[1]

    steps = along_z(dims)
    a_lines = {kz: trade(a_own[kz], dims, kz=kz) for kz in steps}
    b_own, a_lines[steps[-1]] = lax.optimization_barrier((b_own, a_lines[steps[-1]]))
    b_lines = {kz: trade(b_own, dims, kz=kz) for kz in steps}
    mine, xa, ya = pack([a_own[0]] + [a_lines[kz] for kz in range(1, nz)], lanes, dims, True)
    found = [(mine, 0, 0, 0, True, middle, middle + 128)]
    near_a = {kx: trade(xa[kx - 1], dims, kx=kx) for kx in range(1, nx)}
    for kx, v in near_a.items():
        found.append((v, 0, kx, 0, True, middle, middle + ny * 128))
    for ky in range(1, ny):
        v = trade(ya[ky - 1], dims, ky=ky)
        found.append((v, ky, 0, 0, True, middle, middle + 128))
    b = jnp.concatenate([b_own] + [b_lines[kz] for kz in range(1, nz)], axis=0)
    found.append((b, 0, 0, 1, False))
    near_b = {ky: trade(b, dims, ky=ky) for ky in range(1, ny)}
    for ky, v in near_b.items():
        found.append((v, ky, 0, 1, False))
    for kx in range(1, nx):
        found.append((trade(b, dims, kx=kx), 0, kx, 1, False))
    for kx, v in near_a.items():
        for ky in range(1, ny):
            third = trade(v, dims, ky=ky)
            found.append((third, ky, kx, 0, True, middle + ky * 128, middle + ny * 128))
    for ky, v in near_b.items():
        for kx in range(1, nx):
            found.append((trade(v, dims, kx=kx), ky, kx, 1, False))

    size = nz * rows
    pieces = tuple((f[1] * nx + f[2], f[3], f[4]) for f in found)
    keep, send = project([f[0] for f in found], pieces, out_weight, dims, rows)
    carriers = [f for f in found if len(f) > 5]
    places = tuple((f[1] * nx + f[2], f[5], f[6]) for f in carriers)
    residual, mask = arrange([f[0] for f in carriers], places, lanes, size)
    projected = (keep + swap_sec(send)).astype(BF)
    mixed = (residual[:, :part].astype(F32) + projected.astype(F32)).astype(BF)

    lines = {kz: trade(mixed, dims, kz=kz) for kz in steps}
    stacked, mask = merge([mixed] + [lines[kz] for kz in range(1, nz)], mask, dims, rows)
    pairs = []
    for ky in range(ny):
        for kx in range(nx):
            got = stacked if ky + kx == 0 else trade(stacked, dims, ky=ky, kx=kx)
            pairs.append((ky * nx + kx, got, swap_sec(got)))
    keep_near, keep_far, send_near, send_far, own_mixed = experts(
        pairs,
        mask,
        norm_gain.reshape(1, width),
        router_weight.T,
        gate_weight,
        up_weight,
        down_weight,
        dims,
        rows,
    )

    quarter = width // 4
    far = keep_far.astype(F32) + swap_sec(send_far).astype(F32)
    near = keep_near.astype(F32) + swap_sec(send_near).astype(F32)
    cut_far = total_rows - total_rows // nx
    cut_near = total_rows // nx
    sums = []
    for h, (nf, ns) in enumerate(((nx, ny), (ny, nx))):
        away = (far[:cut_far] if h == 0 else far[cut_far:]).astype(BF)
        total = near[:cut_near] if h == 0 else near[cut_near:]
        size = total_rows // nf
        for k in range(1, nf):
            came = trade(
                away[(k - 1) * size : k * size], dims, **({"kx": k} if h == 0 else {"ky": k})
            )
            total = total + came.astype(F32)
        total = total.reshape(ns, nz * rows, quarter)
        inner = total[0]
        for k in range(1, ns):
            came = trade(total[k].astype(BF), dims, **({"ky": k} if h == 0 else {"kx": k}))
            inner = inner + came.astype(F32)
        sums.append(inner)
    joined = jnp.concatenate(sums, axis=1).reshape(nz, rows, width // 2)
    last = joined[0]
    came = [trade(joined[k].astype(BF), dims, kz=k) for k in steps]
    for v in came:
        last = last + v.astype(F32)
    own_half = lax.dynamic_slice_in_dim(own_mixed, sec * (width // 2), width // 2, 1)
    done = (own_half.astype(F32) + last).astype(BF)
    other = swap_sec(done)
    return jnp.where(
        sec == 0, jnp.concatenate([done, other], axis=1), jnp.concatenate([other, done], axis=1)
    )


def solution(mesh):
    dims = grid_of(mesh.shape["dev"])
    placed = (
        P("dev", "sec"),
        P("dev", None, "sec"),
        P("dev", None, "sec"),
        P("dev", "sec"),
        P("dev", "sec"),
        P("dev"),
        P("dev", None),
        P("sec", "dev"),
        P(),
        P(),
        P("dev", None),
        P("dev", None, "sec"),
        P("dev", None, "sec"),
        P("dev", "sec", None),
    )
    return jax.shard_map(
        functools.partial(local, dims),
        mesh=mesh,
        in_specs=placed,
        out_specs=P("dev", None),
        check_vma=False,
    )
```

```python
import functools
import math

import jax
import jax.numpy as jnp
from jax import lax
from jax.experimental import pallas as pl
from jax.experimental.pallas import tpu as pltpu
from jax.sharding import PartitionSpec as P

HEAD = 128
masked_score = -1e30
BF = jnp.bfloat16
F32 = jnp.float32


def grid_of(n):
    known = {16: (4, 2, 2), 64: (4, 4, 4)}
    return known.get(n, (n, 1, 1))


def code_of(dims, kz, ky, kx):
    return (kz * dims[1] + ky) * dims[2] + kx


def row_of(dims, chip):
    plane = dims[1] * dims[2]
    return (chip % plane) * dims[0] + chip // plane


def trade(value, dims, kz=0, ky=0, kx=0):
    code = code_of(dims, kz, ky, kx)
    n = dims[0] * dims[1] * dims[2]
    return lax.ppermute(value, "dev", [(d, d ^ code) for d in range(n)])


def along_z(dims):
    return sorted(range(1, dims[0]), key=lambda k: (k == 1, k))


def swap_sec(value):
    return lax.ppermute(value, "sec", [(0, 1), (1, 0)])


def planes(a, b, dims):
    _, ny, nx = dims
    first, second, third = [], [], []
    near_a = {kx: trade(a, dims, kx=kx) for kx in range(1, nx)}
    near_b = {ky: trade(b, dims, ky=ky) for ky in range(1, ny)}
    first += [((0, kx), 0, v) for kx, v in near_a.items()]
    first += [((ky, 0), 1, v) for ky, v in near_b.items()]
    second += [((ky, 0), 0, trade(a, dims, ky=ky)) for ky in range(1, ny)]
    second += [((0, kx), 1, trade(b, dims, kx=kx)) for kx in range(1, nx)]
    third += [
        ((ky, kx), 0, trade(v, dims, ky=ky)) for kx, v in near_a.items() for ky in range(1, ny)
    ]
    third += [
        ((ky, kx), 1, trade(v, dims, kx=kx)) for ky, v in near_b.items() for kx in range(1, nx)
    ]
    return first, second, third


ANY = pl.BlockSpec(memory_space=pl.ANY)
VM = pl.BlockSpec(memory_space=pltpu.VMEM)
HBM = pl.BlockSpec(memory_space=pltpu.HBM)
MIB = 1024 * 1024


def project_kernel(nz, plane, pieces, rows, *refs):
    count = len(pieces)
    arrays = refs[:count]
    w_ref, keep_ref, send_ref, held, sems = refs[count:]
    half = held.shape[1] // 2
    sec = lax.axis_index("sec")
    z = lax.axis_index("dev") // plane
    copies = []

    def move(i, source, place, size, column):
        copies.append(
            pltpu.make_async_copy(
                arrays[i].at[pl.ds(source, size), pl.ds(0, half)],
                held.at[pl.ds(place, size), pl.ds(column * half, half)],
                sems.at[len(copies)],
            )
        )

    for i, (slot, column, ordered) in enumerate(pieces):
        if ordered:
            move(i, 0, slot * nz * rows, nz * rows, column)
            continue
        for kz in range(nz):
            place = pl.multiple_of((slot * nz + (z ^ kz)) * rows, rows)
            move(i, kz * rows, place, rows, column)
    for c in copies:
        c.start()
    for c in copies:
        c.wait()
    total = jnp.dot(held[...], w_ref[...], preferred_element_type=F32)
    part = total.shape[1] // 2
    low, high = total[:, :part], total[:, part:]
    keep_ref[...] = jnp.where(sec == 0, low, high)
    send_ref[...] = jnp.where(sec == 0, high, low)


def project(arrays, pieces, weight, dims, rows):
    depth, cols = weight.shape
    nz, ny, nx = dims
    tall = nz * ny * nx * rows
    out = jax.ShapeDtypeStruct((tall, cols // 2), F32)
    return pl.pallas_call(
        functools.partial(project_kernel, nz, ny * nx, pieces, rows),
        out_shape=(out, out),
        in_specs=[ANY] * len(arrays) + [VM],
        out_specs=(VM, VM),
        scratch_shapes=[
            pltpu.VMEM((tall, depth), BF),
            pltpu.SemaphoreType.DMA((sum(1 if p[2] else nz for p in pieces),)),
        ],
        compiler_params=pltpu.CompilerParams(vmem_limit_bytes=(4 + tall // 32) * MIB),
        cost_estimate=pl.CostEstimate(
            flops=2 * tall * depth * cols,
            bytes_accessed=2 * depth * (cols + tall),
            transcendentals=0,
        ),
        name="project",
    )(*arrays, weight)


def gather_products(dims, codes, arrays, gain_ref, router_ref, gate_ref, up_ref, sums, own_ref):
    acc, route, square = sums
    nz, ny, nx = dims
    plane = ny * nx
    me = lax.axis_index("dev")
    sec = lax.axis_index("sec")
    total = acc.shape[0]
    rows = own_ref.shape[0]
    part = arrays[0].shape[1]
    place = pl.multiple_of(row_of(dims, me) * rows, rows)

    def add_products(x, at):
        power = x * x
        for t in range(0, power.shape[1], 128):
            square[...] += power[:, t : t + 128]
        scaled = (x * gain_ref[:, at]).astype(BF)
        weights = jnp.concatenate([gate_ref[0, at], up_ref[0, at]], axis=1)
        acc[...] += jnp.dot(scaled, weights, preferred_element_type=F32)
        route[...] += lax.dot_general(
            scaled, router_ref[:, at], (((1,), (1,)), ((), ())), preferred_element_type=F32
        )

    if codes is None:
        for t in range(0, gain_ref.shape[1], 256):
            add_products(arrays[0][:, t : t + 256].astype(F32), pl.ds(t, 256))
        own_ref[...] = arrays[0][pl.ds(place, rows), :]
        return
    for i, code in enumerate(codes):
        here, there = arrays[2 * i : 2 * i + 2]
        for kz in range(nz):
            span = slice(kz * total, (kz + 1) * total)
            low = jnp.where(sec == 0, here[span, :], there[span, :])
            high = jnp.where(sec == 0, there[span, :], here[span, :])
            block = jnp.concatenate([low, high], axis=1)
            owner = me ^ (kz * plane + code)
            at = pl.ds(pl.multiple_of(owner * 2 * part, 2 * part), 2 * part)
            add_products(block.astype(F32), at)
        for kz in range(nz):
            owner = me ^ (kz * plane + code)
            spot = pl.ds(pl.multiple_of(kz * total + place, rows), rows)
            mine = [here[spot, :], there[spot, :]]
            first = jnp.where(sec == 0, mine[0], mine[1])
            second = jnp.where(sec == 0, mine[1], mine[0])
            at = pl.ds(pl.multiple_of(owner * 2 * part, 2 * part), 2 * part)
            own_ref[:, at] = jnp.concatenate([first, second], axis=1)


def early_kernel(dims, codes, count, *refs):
    arrays = refs[:count]
    gain_ref, router_ref, gate_ref, up_ref, acc, route, square, own_ref = refs[count:]
    acc[...] = jnp.zeros_like(acc)
    route[...] = jnp.zeros_like(route)
    square[...] = jnp.zeros_like(square)
    own_ref[...] = jnp.zeros_like(own_ref)
    gather_products(
        dims, codes, arrays, gain_ref, router_ref, gate_ref, up_ref, (acc, route, square), own_ref
    )


def late_kernel(dims, codes, eps, count, *refs):
    nz, ny, nx = dims
    arrays = refs[:count]
    (
        gain_ref,
        router_ref,
        gate_ref,
        up_ref,
        acc_in,
        route_in,
        square_in,
        own_in,
        down_ref,
        mask_ref,
        *outs,
        own_ref,
        acc,
        route,
        square,
        hidden,
        hidden_a,
        hidden_b,
    ) = refs[count:]
    acc[...] = acc_in[...]
    route[...] = route_in[...]
    square[...] = square_in[...]
    own_ref[...] = own_in[...]
    gather_products(
        dims, codes, arrays, gain_ref, router_ref, gate_ref, up_ref, (acc, route, square), own_ref
    )
    width = gain_ref.shape[1]
    units = down_ref.shape[1]
    rows = own_ref.shape[0]
    me = lax.axis_index("dev")
    sec = lax.axis_index("sec")
    mean = jnp.sum(square[...], axis=1, keepdims=True) * (1.0 / width)
    inverse = lax.rsqrt(mean + eps)
    live = mask_ref[:, : route.shape[1]].astype(F32) > 0.5
    logits = jnp.where(live, route[...] * inverse, masked_score)
    top = jnp.max(logits, axis=1, keepdims=True)
    powers = jnp.where(live, jnp.exp(logits - top), 0.0)
    lane = lax.broadcasted_iota(jnp.int32, powers.shape, 1)
    mine = jnp.sum(jnp.where(lane == me, powers, 0.0), axis=1, keepdims=True)
    weight = mine / jnp.sum(powers, axis=1, keepdims=True)
    gate = acc[:, :units] * inverse
    up = acc[:, units:] * inverse
    hidden[...] = (gate / (1.0 + jnp.exp(-gate)) * up * weight).astype(BF)
    for kz in range(nz):
        for ky in range(ny):
            for kx in range(nx):
                chip = me ^ code_of(dims, kz, ky, kx)
                place = pl.multiple_of(row_of(dims, chip) * rows, rows)
                block = hidden[pl.ds(place, rows)]
                hidden_a[pl.ds(((kx * ny + ky) * nz + kz) * rows, rows)] = block
                hidden_b[pl.ds(((ky * nx + kx) * nz + kz) * rows, rows)] = block
    finish(dims, sec, hidden_a, hidden_b, down_ref, outs)


def finish(dims, sec, hidden_a, hidden_b, down_ref, outs):
    _, ny, nx = dims
    keep_near, keep_far, send_near, send_far = outs
    quarter = keep_near.shape[1]
    wide = quarter // 2
    near_cut = hidden_a.shape[0] // nx
    far_cut = hidden_a.shape[0] - near_cut
    for h, near, far in ((1, send_near, send_far), (0, keep_near, keep_far)):
        whose = sec if h == 0 else 1 - sec
        for q, (source, first) in enumerate(((hidden_a, nx), (hidden_b, ny))):
            cut = source.shape[0] // first
            rest = source.shape[0] - cut
            for t in range(2):
                place = pl.multiple_of(whose * 2 * quarter + q * quarter + t * wide, wide)
                found = jnp.dot(
                    source[...], down_ref[0, :, pl.ds(place, wide)], preferred_element_type=F32
                ).astype(BF)
                span = slice(t * wide, (t + 1) * wide)
                near[q * near_cut : q * near_cut + cut, span] = found[:cut]
                far[q * far_cut : q * far_cut + rest, span] = found[cut:]


def in_order(pairs, n, total_rows, part, dims):
    me = lax.axis_index("dev")
    sec = lax.axis_index("sec")
    held = jnp.zeros((total_rows, n * 2 * part), BF)
    for code, *both in pairs:
        for side, array in enumerate(both):
            for kz in range(dims[0]):
                owner = me ^ (kz * dims[1] * dims[2] + code)
                whose = sec if side == 0 else 1 - sec
                block = array[kz * total_rows : (kz + 1) * total_rows]
                held = lax.dynamic_update_slice(held, block, (0, (owner * 2 + whose) * part))
    return held


def experts(pairs, mask, gain, router, gate, up, down, dims, rows):
    nz, ny, nx = dims
    total_rows = nz * ny * nx * rows
    _, width, units = gate.shape
    count = max(1, len(pairs) // 2)
    sums = [
        jax.ShapeDtypeStruct((total_rows, 2 * units), F32),
        jax.ShapeDtypeStruct((total_rows, router.shape[0]), F32),
        jax.ShapeDtypeStruct((total_rows, 128), F32),
        jax.ShapeDtypeStruct((rows, width), BF),
    ]
    params = pltpu.CompilerParams(vmem_limit_bytes=(4 + total_rows // 64) * MIB)

    def cost(share):
        return pl.CostEstimate(
            flops=int(6 * total_rows * width * units * share),
            bytes_accessed=int(6 * width * units * share),
            transcendentals=0,
        )

    early = [v for _, *both in pairs[:count] for v in both]
    late = [v for _, *both in pairs[count:] for v in both]
    codes = [p[0] for p in pairs]
    part = pairs[0][1].shape[1]
    found = None
    if part % 128:
        late, codes = [in_order(pairs, nz * ny * nx, total_rows, part, dims)], None
        found = [jnp.zeros(v.shape, v.dtype) for v in sums]
    found = found or pl.pallas_call(
        functools.partial(early_kernel, dims, codes and codes[:count], len(early)),
        out_shape=tuple(sums),
        in_specs=[VM] * (len(early) + 4),
        out_specs=(VM,) * 4,
        compiler_params=params,
        cost_estimate=cost(0.33),
        name="experts_early",
    )(*early, gain, router, gate, up)
    near = total_rows // nx + total_rows // ny
    shapes = [
        jax.ShapeDtypeStruct((r, width // 4), BF)
        for r in (near, 2 * total_rows - near, near, 2 * total_rows - near)
    ]
    return pl.pallas_call(
        functools.partial(late_kernel, dims, codes and codes[count:], 1e-6, len(late)),
        out_shape=(*shapes, sums[3]),
        in_specs=[VM] * (len(late) + 10),
        out_specs=(VM,) * 5,
        scratch_shapes=[pltpu.VMEM(v.shape, v.dtype) for v in sums[:3]]
        + [pltpu.VMEM((total_rows, units), BF)] * 3,
        compiler_params=params,
        cost_estimate=cost(0.67),
        name="experts_late",
    )(*late, gain, router, gate, up, *found, down, mask)


LINE_HEADS = 24
GROUP = 4
CHUNK = 128


def attend_kernel(dims, lanes, *refs):
    (
        len_ref,
        ids_ref,
        q_ref,
        nk_ref,
        nv_ref,
        extra_ref,
        k_ref,
        v_ref,
        *outs,
        keys,
        values,
        apart,
        joined,
        ksems,
        vsems,
    ) = refs
    a_ref, sends = outs[0], outs[1:]
    rows, span, cols = keys.shape
    heads = q_ref.shape[1] // HEAD
    wide = a_ref.shape[1]
    rest = heads * HEAD - wide
    groups = cols // HEAD
    per = heads // groups
    me = lax.axis_index("dev")
    sec = lax.axis_index("sec")

    def fetch(r, source, target, sem):
        live = (len_ref[r] + CHUNK - 1) // CHUNK * CHUNK
        part = pl.ds(0, pl.multiple_of(live, CHUNK))
        return pltpu.make_async_copy(source.at[r, part], target.at[r, part], sem.at[r])

    for start in range(0, rows, GROUP):
        for r in range(start, start + GROUP):
            fetch(r, k_ref, keys, ksems).start()
        values[pl.ds(start, GROUP)] = jnp.zeros((GROUP, span, cols), BF)
        for r in range(start, start + GROUP):
            fetch(r, v_ref, values, vsems).start()

    lane_ids = lax.broadcasted_iota(jnp.int32, (lanes, rows), 0)
    chosen = jnp.zeros((lanes, rows), F32)
    for k in range(ids_ref.shape[0]):
        chosen = jnp.where(lane_ids == ids_ref[k : k + 1, :], 1.0, chosen)
    chosen = chosen.T.astype(BF)
    plane = dims[1] * dims[2]
    for code, target in enumerate(sends):
        for kz in range(dims[0]):
            owner = me ^ (kz * plane + code)
            if len(extra_ref.shape) == 3:
                block = extra_ref[owner]
            else:
                place = pl.multiple_of((owner * 2 + sec) * 128, 128)
                block = extra_ref[:, pl.ds(place, 128)]
            at = rest + kz * 128
            target[:, at : at + 128] = block
        target[:, rest + dims[0] * 128 :] = chosen

    for h in range(heads):
        apart[pl.ds(h * rows, rows)] = q_ref[:, h * HEAD : (h + 1) * HEAD].astype(F32)
    fresh_k = nk_ref[...].astype(F32)
    fresh_v = nv_ref[...].astype(F32)
    head = lax.broadcasted_iota(jnp.int32, (heads, HEAD), 0)
    belongs = [(head >= g * per) & (head < (g + 1) * per) for g in range(groups)]
    place = lax.broadcasted_iota(jnp.int32, (heads, span), 1)
    scale = 1.0 / math.sqrt(HEAD)

    def of_group(wide):
        found = jnp.broadcast_to(wide[:, :HEAD], (heads, HEAD))
        for g in range(1, groups):
            piece = wide[:, g * HEAD : (g + 1) * HEAD]
            found = jnp.where(belongs[g], jnp.broadcast_to(piece, (heads, HEAD)), found)
        return found

    for start in range(0, rows, GROUP):
        group = range(start, start + GROUP)
        for r in group:
            fetch(r, k_ref, keys, ksems).wait()
            fetch(r, v_ref, values, vsems).wait()
        queries, scores = {}, {}
        for r in group:
            q = apart[pl.ds(r, heads, stride=rows), :]
            queries[r] = q
            apart_q = jnp.concatenate([jnp.where(m, q, 0.0) for m in belongs], axis=1)
            scores[r] = lax.dot_general(
                apart_q.astype(BF), keys[r], (((1,), (1,)), ((), ())), preferred_element_type=F32
            )
        for r in group:
            s = jnp.where(place < len_ref[r], scores[r] * scale, masked_score)
            own = jnp.sum(queries[r] * of_group(fresh_k[r : r + 1]), axis=1, keepdims=True) * scale
            top = jnp.maximum(jnp.max(s, axis=1, keepdims=True), own)
            power = jnp.exp(s - top)
            own_power = jnp.exp(own - top)
            total = jnp.sum(power, axis=1, keepdims=True) + own_power
            mixed = jnp.dot(power.astype(BF), values[r], preferred_element_type=F32)
            picked = mixed[:, :HEAD]
            for g in range(1, groups):
                picked = jnp.where(belongs[g], mixed[:, g * HEAD : (g + 1) * HEAD], picked)
            picked = (picked + own_power * of_group(fresh_v[r : r + 1])) / total
            joined[pl.ds(r, heads, stride=rows), :] = picked
    for h in range(heads):
        block = joined[pl.ds(h * rows, rows)].astype(BF)
        at = h * HEAD
        if at < wide:
            a_ref[:, at : at + HEAD] = block
        else:
            for target in sends:
                target[:, at - wide : at - wide + HEAD] = block


def attention(
    queries, key_cache, value_cache, new_key, new_value, cache_lengths, ids, extra, lanes, dims
):
    rows, span, cols = key_cache.shape
    width = queries.shape[1]
    heads = width // HEAD
    wide = LINE_HEADS * HEAD
    side = width - wide + dims[0] * 128 + lanes
    outs = [(rows, wide)] + [(rows, side)] * (dims[1] * dims[2])
    return pl.pallas_call(
        functools.partial(attend_kernel, dims, lanes),
        out_shape=tuple(jax.ShapeDtypeStruct(o, BF) for o in outs),
        in_specs=[pl.BlockSpec(memory_space=pltpu.SMEM)] + [VM] * 5 + [HBM, HBM],
        out_specs=(VM,) * len(outs),
        scratch_shapes=[
            pltpu.VMEM((rows, span, cols), BF),
            pltpu.VMEM((rows, span, cols), BF),
            pltpu.VMEM((rows * heads, HEAD), F32),
            pltpu.VMEM((rows * heads, HEAD), F32),
            pltpu.SemaphoreType.DMA((rows,)),
            pltpu.SemaphoreType.DMA((rows,)),
        ],
        compiler_params=pltpu.CompilerParams(vmem_limit_bytes=60 * MIB),
        cost_estimate=pl.CostEstimate(
            flops=4 * rows * heads * span * cols,
            bytes_accessed=4 * rows * span * cols,
            transcendentals=rows * heads * span,
        ),
        name="attend",
    )(cache_lengths, ids, queries, new_key, new_value, extra, key_cache, value_cache)


def pack_line_kernel(plane, *refs):
    lines, (a_ref, b_ref) = refs[:-2], refs[-2:]
    rows = lines[0].shape[0]
    half = a_ref.shape[1]
    z = lax.axis_index("dev") // plane
    for kz, source in enumerate(lines):
        span = pl.ds(pl.multiple_of((z ^ kz) * rows, rows), rows)
        a_ref[span, :] = source[:, :half]
        b_ref[span, :] = source[:, half:]


def pack_line(lines, plane):
    rows, width = lines[0].shape
    out = jax.ShapeDtypeStruct((len(lines) * rows, width // 2), BF)
    return pl.pallas_call(
        functools.partial(pack_line_kernel, plane),
        out_shape=(out, out),
        in_specs=[VM] * len(lines),
        out_specs=(VM, VM),
        compiler_params=pltpu.CompilerParams(vmem_limit_bytes=16 * MIB),
        name="pack_line",
    )(*lines)


def pack_plane_kernel(nz, lanes, count, *refs):
    blocks, outs = refs[:count], refs[count:]
    rows = blocks[0].shape[0]
    share = blocks[0].shape[1] - nz * 128 - lanes
    here = lax.axis_index("dev") % count
    for code, source in enumerate(blocks):
        span = pl.ds(pl.multiple_of((here ^ code) * rows, rows), rows)
        for kz in range(nz):
            outs[kz][span, :share] = source[:, :share]
            at = share + kz * 128
            outs[kz][span, share : share + 128] = source[:, at : at + 128]
            outs[kz][span, share + 128 :] = source[:, share + nz * 128 :]


def pack_plane(blocks, lanes, nz):
    count = len(blocks)
    rows, width = blocks[0].shape
    out = jax.ShapeDtypeStruct((count * rows, width - (nz - 1) * 128), BF)
    return pl.pallas_call(
        functools.partial(pack_plane_kernel, nz, lanes, count),
        out_shape=(out,) * nz,
        in_specs=[VM] * count,
        out_specs=(VM,) * nz,
        compiler_params=pltpu.CompilerParams(vmem_limit_bytes=16 * MIB),
        name="pack_plane",
    )(*blocks)


def scatter_rows(dims, kz, rows):
    nz, ny, nx = dims
    z = lax.axis_index("dev") // (ny * nx)
    for q in range(ny * nx):
        yield q * rows, pl.multiple_of((q * nz + (z ^ kz)) * rows, rows)


def project_kernel(dims, rows, codes, *refs):
    nz, ny, nx = dims
    count = len(codes)
    firsts, seconds = refs[:count], refs[count : 2 * count]
    rest = refs[2 * count : 2 * count + nz]
    w_ref, keep_ref, send_ref, held, sems = refs[2 * count + nz :]
    sec = lax.axis_index("sec")
    here = lax.axis_index("dev") % (ny * nx)
    half = firsts[0].shape[1]
    share = held.shape[1] - 2 * half
    size = nz * rows
    copies = []

    def move(source, target):
        copies.append(pltpu.make_async_copy(source, target, sems.at[len(copies)]))

    for i, code in enumerate(codes):
        span = pl.ds(pl.multiple_of((here ^ code) * size, size), size)
        move(firsts[i], held.at[span, pl.ds(0, half)])
        move(seconds[i], held.at[span, pl.ds(half, half)])
    for kz in range(nz):
        for source, target in scatter_rows(dims, kz, rows):
            move(
                rest[kz].at[pl.ds(source, rows), pl.ds(0, share)],
                held.at[pl.ds(target, rows), pl.ds(2 * half, share)],
            )
    for c in copies:
        c.start()
    for c in copies:
        c.wait()
    total = jnp.dot(held[...], w_ref[...], preferred_element_type=F32)
    part = total.shape[1] // 2
    low, high = total[:, :part], total[:, part:]
    keep_ref[...] = jnp.where(sec == 0, low, high)
    send_ref[...] = jnp.where(sec == 0, high, low)


def project(firsts, seconds, codes, rest, weight, dims, rows):
    depth, cols = weight.shape
    tall = dims[0] * dims[1] * dims[2] * rows
    out = jax.ShapeDtypeStruct((tall, cols // 2), F32)
    arrays = [*firsts, *seconds, *rest]
    return pl.pallas_call(
        functools.partial(project_kernel, dims, rows, codes),
        out_shape=(out, out),
        in_specs=[ANY] * len(arrays) + [VM],
        out_specs=(VM, VM),
        scratch_shapes=[
            pltpu.VMEM((tall, depth), BF),
            pltpu.SemaphoreType.DMA((2 * len(codes) + tall // rows,)),
        ],
        compiler_params=pltpu.CompilerParams(vmem_limit_bytes=(4 + tall // 32) * MIB),
        cost_estimate=pl.CostEstimate(
            flops=2 * tall * depth * cols,
            bytes_accessed=2 * depth * (cols + tall),
            transcendentals=0,
        ),
        name="project",
    )(*arrays, weight)


def arrange_kernel(dims, rows, *refs):
    nz = dims[0]
    rest, (residual, mask, sems) = refs[:nz], refs[nz:]
    share = rest[0].shape[1] - 128 - mask.shape[1]
    copies = []
    for kz in range(nz):
        for source, target in scatter_rows(dims, kz, rows):
            for start, out in ((share, residual), (share + 128, mask)):
                copies.append(
                    pltpu.make_async_copy(
                        rest[kz].at[pl.ds(source, rows), pl.ds(start, out.shape[1])],
                        out.at[pl.ds(target, rows)],
                        sems.at[len(copies)],
                    )
                )
    for c in copies:
        c.start()
    for c in copies:
        c.wait()


def arrange(rest, lanes, dims, rows):
    tall = dims[0] * dims[1] * dims[2] * rows
    return pl.pallas_call(
        functools.partial(arrange_kernel, dims, rows),
        out_shape=tuple(jax.ShapeDtypeStruct((tall, w), BF) for w in (128, lanes)),
        in_specs=[ANY] * len(rest),
        out_specs=(VM, VM),
        scratch_shapes=[pltpu.SemaphoreType.DMA((2 * tall // rows,))],
        compiler_params=pltpu.CompilerParams(vmem_limit_bytes=8 * MIB),
        name="arrange",
    )(*rest)


def local(
    dims,
    queries,
    key_cache,
    value_cache,
    new_key,
    new_value,
    cache_lengths,
    residual_in,
    out_weight,
    norm_gain,
    router_weight,
    expert_ids,
    gate_weight,
    up_weight,
    down_weight,
):
    nz, ny, nx = dims
    n = nz * ny * nx
    rows, width = residual_in.shape
    total_rows = n * rows
    expert_total = router_weight.shape[1]
    sec = lax.axis_index("sec")
    lanes = -(-expert_total // 128) * 128
    part = width // n // 2

    if part % 128:
        extra = lax.dynamic_index_in_dim(
            residual_in.reshape(rows, n, 2, part), sec, axis=2, keepdims=False
        )
        extra = jnp.pad(jnp.swapaxes(extra, 0, 1), ((0, 0), (0, 0), (0, 128 - part)))
    else:
        extra = residual_in
    a_own, *blocks = attention(
        queries,
        key_cache,
        value_cache,
        new_key,
        new_value,
        cache_lengths,
        expert_ids.T,
        extra,
        lanes,
        dims,
    )

    plane = ny * nx
    steps = along_z(dims)
    lines = {kz: trade(a_own, dims, kz=kz) for kz in steps}
    blocks = [blocks[0]] + [
        trade(blocks[c], dims, ky=c // nx, kx=c % nx) for c in range(1, plane)
    ]
    rest = pack_plane(blocks, lanes, nz)
    lines, rest = lax.optimization_barrier((lines, rest))
    rest = [rest[0]] + [trade(rest[kz], dims, kz=kz) for kz in range(1, nz)]
    a, b = pack_line([a_own] + [lines[kz] for kz in range(1, nz)], plane)
    firsts, seconds = {0: a}, {0: b}
    for wave in planes(a, b, dims):
        for (ky, kx), half, array in wave:
            (firsts, seconds)[half][ky * nx + kx] = array
    codes = sorted(firsts)

    keep, send = project(
        [firsts[c] for c in codes], [seconds[c] for c in codes], codes, rest, out_weight, dims, rows
    )
    residual, mask = arrange(rest, lanes, dims, rows)
    projected = (keep + swap_sec(send)).astype(BF)
    mixed = (residual[:, :part].astype(F32) + projected.astype(F32)).astype(BF)

    lines = {kz: trade(mixed, dims, kz=kz) for kz in steps}
    stacked = jnp.concatenate([mixed] + [lines[kz] for kz in range(1, nz)], axis=0)
    pairs = []
    for ky in range(ny):
        for kx in range(nx):
            got = stacked if ky + kx == 0 else trade(stacked, dims, ky=ky, kx=kx)
            pairs.append((ky * nx + kx, got, swap_sec(got)))
    keep_near, keep_far, send_near, send_far, own_mixed = experts(
        pairs,
        mask,
        norm_gain.reshape(1, width),
        router_weight.T,
        gate_weight,
        up_weight,
        down_weight,
        dims,
        rows,
    )

    quarter = width // 4
    far = keep_far.astype(F32) + swap_sec(send_far).astype(F32)
    near = keep_near.astype(F32) + swap_sec(send_near).astype(F32)
    cut_far = total_rows - total_rows // nx
    cut_near = total_rows // nx
    sums = []
    for h, (nf, ns) in enumerate(((nx, ny), (ny, nx))):
        away = (far[:cut_far] if h == 0 else far[cut_far:]).astype(BF)
        total = near[:cut_near] if h == 0 else near[cut_near:]
        size = total_rows // nf
        for k in range(1, nf):
            came = trade(
                away[(k - 1) * size : k * size], dims, **({"kx": k} if h == 0 else {"ky": k})
            )
            total = total + came.astype(F32)
        total = total.reshape(ns, nz * rows, quarter)
        inner = total[0]
        for k in range(1, ns):
            came = trade(total[k].astype(BF), dims, **({"ky": k} if h == 0 else {"kx": k}))
            inner = inner + came.astype(F32)
        sums.append(inner)
    joined = jnp.concatenate(sums, axis=1).reshape(nz, rows, width // 2)
    last = joined[0]
    came = [trade(joined[k].astype(BF), dims, kz=k) for k in steps]
    for v in came:
        last = last + v.astype(F32)
    own_half = lax.dynamic_slice_in_dim(own_mixed, sec * (width // 2), width // 2, 1)
    done = (own_half.astype(F32) + last).astype(BF)
    other = swap_sec(done)
    return jnp.where(
        sec == 0, jnp.concatenate([done, other], axis=1), jnp.concatenate([other, done], axis=1)
    )


def solution(mesh):
    dims = grid_of(mesh.shape["dev"])
    placed = (
        P("dev", "sec"),
        P("dev", None, "sec"),
        P("dev", None, "sec"),
        P("dev", "sec"),
        P("dev", "sec"),
        P("dev"),
        P("dev", None),
        P("sec", "dev"),
        P(),
        P(),
        P("dev", None),
        P("dev", None, "sec"),
        P("dev", None, "sec"),
        P("dev", "sec", None),
    )
    return jax.shard_map(
        functools.partial(local, dims),
        mesh=mesh,
        in_specs=placed,
        out_specs=P("dev", None),
        check_vma=False,
    )
```

```python
import functools
import math

import jax
import jax.numpy as jnp
from jax import lax
from jax.experimental import pallas as pl
from jax.experimental.pallas import tpu as pltpu
from jax.sharding import PartitionSpec as P

HEAD = 128
masked_score = -1e30
BF = jnp.bfloat16
F32 = jnp.float32


def grid_of(n):
    known = {16: (4, 2, 2), 64: (4, 4, 4)}
    return known.get(n, (n, 1, 1))


def code_of(dims, kz, ky, kx):
    return (kz * dims[1] + ky) * dims[2] + kx


def row_of(dims, chip):
    plane = dims[1] * dims[2]
    return (chip % plane) * dims[0] + chip // plane


def trade(value, dims, kz=0, ky=0, kx=0):
    code = code_of(dims, kz, ky, kx)
    n = dims[0] * dims[1] * dims[2]
    return lax.ppermute(value, "dev", [(d, d ^ code) for d in range(n)])


def along_z(dims):
    return sorted(range(1, dims[0]), key=lambda k: (k == 1, k))


def swap_sec(value):
    return lax.ppermute(value, "sec", [(0, 1), (1, 0)])


def over_plane(block, dims):
    _, ny, nx = dims
    heads = block.shape[1] // HEAD
    cuts = [i * heads // 3 * HEAD for i in range(4)]
    along_x = {kx: trade(block, dims, kx=kx) for kx in range(1, nx)}
    along_y = {ky: trade(block, dims, ky=ky) for ky in range(1, ny)}
    found = [(0, 0, block)]
    found += [(kx, 0, v) for kx, v in along_x.items()]
    found += [(ky * nx, 0, v) for ky, v in along_y.items()]
    for ky in range(1, ny):
        for kx in range(1, nx):
            for i, (start, stop) in enumerate(zip(cuts, cuts[1:])):
                if i < 2:
                    piece = trade(along_x[kx][:, start:stop], dims, ky=ky)
                else:
                    piece = trade(along_y[ky][:, start:stop], dims, kx=kx)
                found.append((ky * nx + kx, start, piece))
    return found


ANY = pl.BlockSpec(memory_space=pl.ANY)
VM = pl.BlockSpec(memory_space=pltpu.VMEM)
HBM = pl.BlockSpec(memory_space=pltpu.HBM)
MIB = 1024 * 1024


def gather_products(dims, codes, arrays, gain_ref, router_ref, gate_ref, up_ref, sums, own_ref):
    acc, route, square = sums
    nz, ny, nx = dims
    plane = ny * nx
    me = lax.axis_index("dev")
    sec = lax.axis_index("sec")
    total = acc.shape[0]
    rows = own_ref.shape[0]
    part = arrays[0].shape[1]
    place = pl.multiple_of(row_of(dims, me) * rows, rows)

    def add_products(x, at):
        power = x * x
        for t in range(0, power.shape[1], 128):
            square[...] += power[:, t : t + 128]
        scaled = (x * gain_ref[:, at]).astype(BF)
        weights = jnp.concatenate([gate_ref[0, at], up_ref[0, at]], axis=1)
        acc[...] += jnp.dot(scaled, weights, preferred_element_type=F32)
        route[...] += lax.dot_general(
            scaled, router_ref[:, at], (((1,), (1,)), ((), ())), preferred_element_type=F32
        )

    if codes is None:
        for t in range(0, gain_ref.shape[1], 256):
            add_products(arrays[0][:, t : t + 256].astype(F32), pl.ds(t, 256))
        own_ref[...] = arrays[0][pl.ds(place, rows), :]
        return
    for i, code in enumerate(codes):
        here, there = arrays[2 * i : 2 * i + 2]
        for kz in range(nz):
            span = slice(kz * total, (kz + 1) * total)
            low = jnp.where(sec == 0, here[span, :], there[span, :])
            high = jnp.where(sec == 0, there[span, :], here[span, :])
            block = jnp.concatenate([low, high], axis=1)
            owner = me ^ (kz * plane + code)
            at = pl.ds(pl.multiple_of(owner * 2 * part, 2 * part), 2 * part)
            add_products(block.astype(F32), at)
        for kz in range(nz):
            owner = me ^ (kz * plane + code)
            spot = pl.ds(pl.multiple_of(kz * total + place, rows), rows)
            mine = [here[spot, :], there[spot, :]]
            first = jnp.where(sec == 0, mine[0], mine[1])
            second = jnp.where(sec == 0, mine[1], mine[0])
            at = pl.ds(pl.multiple_of(owner * 2 * part, 2 * part), 2 * part)
            own_ref[:, at] = jnp.concatenate([first, second], axis=1)


def early_kernel(dims, codes, count, *refs):
    arrays = refs[:count]
    gain_ref, router_ref, gate_ref, up_ref, acc, route, square, own_ref = refs[count:]
    acc[...] = jnp.zeros_like(acc)
    route[...] = jnp.zeros_like(route)
    square[...] = jnp.zeros_like(square)
    own_ref[...] = jnp.zeros_like(own_ref)
    gather_products(
        dims, codes, arrays, gain_ref, router_ref, gate_ref, up_ref, (acc, route, square), own_ref
    )


def late_kernel(dims, codes, eps, count, *refs):
    nz, ny, nx = dims
    arrays = refs[:count]
    (
        gain_ref,
        router_ref,
        gate_ref,
        up_ref,
        acc_in,
        route_in,
        square_in,
        own_in,
        down_ref,
        mask_ref,
        *outs,
        own_ref,
        acc,
        route,
        square,
        hidden,
        hidden_a,
        hidden_b,
    ) = refs[count:]
    acc[...] = acc_in[...]
    route[...] = route_in[...]
    square[...] = square_in[...]
    own_ref[...] = own_in[...]
    gather_products(
        dims, codes, arrays, gain_ref, router_ref, gate_ref, up_ref, (acc, route, square), own_ref
    )
    width = gain_ref.shape[1]
    units = down_ref.shape[1]
    rows = own_ref.shape[0]
    me = lax.axis_index("dev")
    sec = lax.axis_index("sec")
    mean = jnp.sum(square[...], axis=1, keepdims=True) * (1.0 / width)
    inverse = lax.rsqrt(mean + eps)
    live = mask_ref[:, : route.shape[1]].astype(F32) > 0.5
    logits = jnp.where(live, route[...] * inverse, masked_score)
    top = jnp.max(logits, axis=1, keepdims=True)
    powers = jnp.where(live, jnp.exp(logits - top), 0.0)
    lane = lax.broadcasted_iota(jnp.int32, powers.shape, 1)
    mine = jnp.sum(jnp.where(lane == me, powers, 0.0), axis=1, keepdims=True)
    weight = mine / jnp.sum(powers, axis=1, keepdims=True)
    gate = acc[:, :units] * inverse
    up = acc[:, units:] * inverse
    hidden[...] = (gate / (1.0 + jnp.exp(-gate)) * up * weight).astype(BF)
    for kz in range(nz):
        for ky in range(ny):
            for kx in range(nx):
                chip = me ^ code_of(dims, kz, ky, kx)
                place = pl.multiple_of(row_of(dims, chip) * rows, rows)
                block = hidden[pl.ds(place, rows)]
                hidden_a[pl.ds(((kx * ny + ky) * nz + kz) * rows, rows)] = block
                hidden_b[pl.ds(((ky * nx + kx) * nz + kz) * rows, rows)] = block
    finish(dims, sec, hidden_a, hidden_b, down_ref, outs)


def finish(dims, sec, hidden_a, hidden_b, down_ref, outs):
    _, ny, nx = dims
    keep_near, keep_far, send_near, send_far = outs
    quarter = keep_near.shape[1]
    wide = quarter // 2
    near_cut = hidden_a.shape[0] // nx
    far_cut = hidden_a.shape[0] - near_cut
    for h, near, far in ((1, send_near, send_far), (0, keep_near, keep_far)):
        whose = sec if h == 0 else 1 - sec
        for q, (source, first) in enumerate(((hidden_a, nx), (hidden_b, ny))):
            cut = source.shape[0] // first
            rest = source.shape[0] - cut
            for t in range(2):
                place = pl.multiple_of(whose * 2 * quarter + q * quarter + t * wide, wide)
                found = jnp.dot(
                    source[...], down_ref[0, :, pl.ds(place, wide)], preferred_element_type=F32
                ).astype(BF)
                span = slice(t * wide, (t + 1) * wide)
                near[q * near_cut : q * near_cut + cut, span] = found[:cut]
                far[q * far_cut : q * far_cut + rest, span] = found[cut:]


def in_order(pairs, n, total_rows, part, dims):
    me = lax.axis_index("dev")
    sec = lax.axis_index("sec")
    held = jnp.zeros((total_rows, n * 2 * part), BF)
    for code, *both in pairs:
        for side, array in enumerate(both):
            for kz in range(dims[0]):
                owner = me ^ (kz * dims[1] * dims[2] + code)
                whose = sec if side == 0 else 1 - sec
                block = array[kz * total_rows : (kz + 1) * total_rows]
                held = lax.dynamic_update_slice(held, block, (0, (owner * 2 + whose) * part))
    return held


def experts(pairs, mask, gain, router, gate, up, down, dims, rows):
    nz, ny, nx = dims
    total_rows = nz * ny * nx * rows
    _, width, units = gate.shape
    count = max(1, len(pairs) // 2)
    sums = [
        jax.ShapeDtypeStruct((total_rows, 2 * units), F32),
        jax.ShapeDtypeStruct((total_rows, router.shape[0]), F32),
        jax.ShapeDtypeStruct((total_rows, 128), F32),
        jax.ShapeDtypeStruct((rows, width), BF),
    ]
    params = pltpu.CompilerParams(vmem_limit_bytes=(4 + total_rows // 64) * MIB)

    def cost(share):
        return pl.CostEstimate(
            flops=int(6 * total_rows * width * units * share),
            bytes_accessed=int(6 * width * units * share),
            transcendentals=0,
        )

    early = [v for _, *both in pairs[:count] for v in both]
    late = [v for _, *both in pairs[count:] for v in both]
    codes = [p[0] for p in pairs]
    part = pairs[0][1].shape[1]
    found = None
    if part % 128:
        late, codes = [in_order(pairs, nz * ny * nx, total_rows, part, dims)], None
        found = [jnp.zeros(v.shape, v.dtype) for v in sums]
    found = found or pl.pallas_call(
        functools.partial(early_kernel, dims, codes and codes[:count], len(early)),
        out_shape=tuple(sums),
        in_specs=[VM] * (len(early) + 4),
        out_specs=(VM,) * 4,
        compiler_params=params,
        cost_estimate=cost(0.33),
        name="experts_early",
    )(*early, gain, router, gate, up)
    near = total_rows // nx + total_rows // ny
    shapes = [
        jax.ShapeDtypeStruct((r, width // 4), BF)
        for r in (near, 2 * total_rows - near, near, 2 * total_rows - near)
    ]
    return pl.pallas_call(
        functools.partial(late_kernel, dims, codes and codes[count:], 1e-6, len(late)),
        out_shape=(*shapes, sums[3]),
        in_specs=[VM] * (len(late) + 10),
        out_specs=(VM,) * 5,
        scratch_shapes=[pltpu.VMEM(v.shape, v.dtype) for v in sums[:3]]
        + [pltpu.VMEM((total_rows, units), BF)] * 3,
        compiler_params=params,
        cost_estimate=cost(0.67),
        name="experts_late",
    )(*late, gain, router, gate, up, *found, down, mask)


GROUP = 4
CHUNK = 128


def attend_kernel(dims, lanes, *refs):
    (
        len_ref,
        ids_ref,
        q_ref,
        nk_ref,
        nv_ref,
        extra_ref,
        k_ref,
        v_ref,
        *outs,
        keys,
        values,
        apart,
        joined,
        ksems,
        vsems,
    ) = refs
    a_ref, sends = outs[0], outs[1:]
    rows, span, cols = keys.shape
    heads = q_ref.shape[1] // HEAD
    wide = a_ref.shape[1]
    rest = heads * HEAD - wide
    groups = cols // HEAD
    per = heads // groups
    me = lax.axis_index("dev")
    sec = lax.axis_index("sec")

    def fetch(r, source, target, sem):
        live = (len_ref[r] + CHUNK - 1) // CHUNK * CHUNK
        part = pl.ds(0, pl.multiple_of(live, CHUNK))
        return pltpu.make_async_copy(source.at[r, part], target.at[r, part], sem.at[r])

    for start in range(0, rows, GROUP):
        for r in range(start, start + GROUP):
            fetch(r, k_ref, keys, ksems).start()
        values[pl.ds(start, GROUP)] = jnp.zeros((GROUP, span, cols), BF)
        for r in range(start, start + GROUP):
            fetch(r, v_ref, values, vsems).start()

    lane_ids = lax.broadcasted_iota(jnp.int32, (lanes, rows), 0)
    chosen = jnp.zeros((lanes, rows), F32)
    for k in range(ids_ref.shape[0]):
        chosen = jnp.where(lane_ids == ids_ref[k : k + 1, :], 1.0, chosen)
    chosen = chosen.T.astype(BF)
    plane = dims[1] * dims[2]
    for code, target in enumerate(sends):
        for kz in range(dims[0]):
            owner = me ^ (kz * plane + code)
            if len(extra_ref.shape) == 3:
                block = extra_ref[owner]
            else:
                place = pl.multiple_of((owner * 2 + sec) * 128, 128)
                block = extra_ref[:, pl.ds(place, 128)]
            at = rest + kz * 128
            target[:, at : at + 128] = block
        target[:, rest + dims[0] * 128 :] = chosen

    for h in range(heads):
        apart[pl.ds(h * rows, rows)] = q_ref[:, h * HEAD : (h + 1) * HEAD].astype(F32)
    fresh_k = nk_ref[...].astype(F32)
    fresh_v = nv_ref[...].astype(F32)
    head = lax.broadcasted_iota(jnp.int32, (heads, HEAD), 0)
    belongs = [(head >= g * per) & (head < (g + 1) * per) for g in range(groups)]
    place = lax.broadcasted_iota(jnp.int32, (heads, span), 1)
    scale = 1.0 / math.sqrt(HEAD)

    def of_group(wide):
        found = jnp.broadcast_to(wide[:, :HEAD], (heads, HEAD))
        for g in range(1, groups):
            piece = wide[:, g * HEAD : (g + 1) * HEAD]
            found = jnp.where(belongs[g], jnp.broadcast_to(piece, (heads, HEAD)), found)
        return found

    for start in range(0, rows, GROUP):
        group = range(start, start + GROUP)
        for r in group:
            fetch(r, k_ref, keys, ksems).wait()
            fetch(r, v_ref, values, vsems).wait()
        queries, scores = {}, {}
        for r in group:
            q = apart[pl.ds(r, heads, stride=rows), :]
            queries[r] = q
            apart_q = jnp.concatenate([jnp.where(m, q, 0.0) for m in belongs], axis=1)
            scores[r] = lax.dot_general(
                apart_q.astype(BF), keys[r], (((1,), (1,)), ((), ())), preferred_element_type=F32
            )
        for r in group:
            s = jnp.where(place < len_ref[r], scores[r] * scale, masked_score)
            own = jnp.sum(queries[r] * of_group(fresh_k[r : r + 1]), axis=1, keepdims=True) * scale
            top = jnp.maximum(jnp.max(s, axis=1, keepdims=True), own)
            power = jnp.exp(s - top)
            own_power = jnp.exp(own - top)
            total = jnp.sum(power, axis=1, keepdims=True) + own_power
            mixed = jnp.dot(power.astype(BF), values[r], preferred_element_type=F32)
            picked = mixed[:, :HEAD]
            for g in range(1, groups):
                picked = jnp.where(belongs[g], mixed[:, g * HEAD : (g + 1) * HEAD], picked)
            picked = (picked + own_power * of_group(fresh_v[r : r + 1])) / total
            joined[pl.ds(r, heads, stride=rows), :] = picked
    for h in range(heads):
        block = joined[pl.ds(h * rows, rows)].astype(BF)
        at = h * HEAD
        if at < wide:
            a_ref[:, at : at + HEAD] = block
        else:
            for target in sends:
                target[:, at - wide : at - wide + HEAD] = block


def attention(
    queries, key_cache, value_cache, new_key, new_value, cache_lengths, ids, extra, lanes, dims
):
    rows, span, cols = key_cache.shape
    width = queries.shape[1]
    heads = width // HEAD
    wide = heads * 3 // 4 * HEAD
    side = width - wide + dims[0] * 128 + lanes
    outs = [(rows, wide)] + [(rows, side)] * (dims[1] * dims[2])
    return pl.pallas_call(
        functools.partial(attend_kernel, dims, lanes),
        out_shape=tuple(jax.ShapeDtypeStruct(o, BF) for o in outs),
        in_specs=[pl.BlockSpec(memory_space=pltpu.SMEM)] + [VM] * 5 + [HBM, HBM],
        out_specs=(VM,) * len(outs),
        scratch_shapes=[
            pltpu.VMEM((rows, span, cols), BF),
            pltpu.VMEM((rows, span, cols), BF),
            pltpu.VMEM((rows * heads, HEAD), F32),
            pltpu.VMEM((rows * heads, HEAD), F32),
            pltpu.SemaphoreType.DMA((rows,)),
            pltpu.SemaphoreType.DMA((rows,)),
        ],
        compiler_params=pltpu.CompilerParams(vmem_limit_bytes=60 * MIB),
        cost_estimate=pl.CostEstimate(
            flops=4 * rows * heads * span * cols,
            bytes_accessed=4 * rows * span * cols,
            transcendentals=rows * heads * span,
        ),
        name="attend",
    )(cache_lengths, ids, queries, new_key, new_value, extra, key_cache, value_cache)


def pack_line_kernel(plane, *refs):
    lines, out = refs[:-1], refs[-1]
    rows = lines[0].shape[0]
    z = lax.axis_index("dev") // plane
    for kz, source in enumerate(lines):
        out[pl.ds(pl.multiple_of((z ^ kz) * rows, rows), rows), :] = source[...]


def pack_line(lines, plane):
    rows, width = lines[0].shape
    return pl.pallas_call(
        functools.partial(pack_line_kernel, plane),
        out_shape=jax.ShapeDtypeStruct((len(lines) * rows, width), BF),
        in_specs=[VM] * len(lines),
        out_specs=VM,
        compiler_params=pltpu.CompilerParams(vmem_limit_bytes=16 * MIB),
        name="pack_line",
    )(*lines)


def pack_plane_kernel(nz, lanes, count, *refs):
    blocks, outs = refs[:count], refs[count:]
    rows = blocks[0].shape[0]
    share = blocks[0].shape[1] - nz * 128 - lanes
    here = lax.axis_index("dev") % count
    for code, source in enumerate(blocks):
        span = pl.ds(pl.multiple_of((here ^ code) * rows, rows), rows)
        for kz in range(nz):
            outs[kz][span, :share] = source[:, :share]
            at = share + kz * 128
            outs[kz][span, share : share + 128] = source[:, at : at + 128]
            outs[kz][span, share + 128 :] = source[:, share + nz * 128 :]


def pack_plane(blocks, lanes, nz):
    count = len(blocks)
    rows, width = blocks[0].shape
    out = jax.ShapeDtypeStruct((count * rows, width - (nz - 1) * 128), BF)
    return pl.pallas_call(
        functools.partial(pack_plane_kernel, nz, lanes, count),
        out_shape=(out,) * nz,
        in_specs=[VM] * count,
        out_specs=(VM,) * nz,
        compiler_params=pltpu.CompilerParams(vmem_limit_bytes=16 * MIB),
        name="pack_plane",
    )(*blocks)


def scatter_rows(dims, kz, rows):
    nz, ny, nx = dims
    z = lax.axis_index("dev") // (ny * nx)
    for q in range(ny * nx):
        yield q * rows, pl.multiple_of((q * nz + (z ^ kz)) * rows, rows)


def project_kernel(dims, rows, wide, spots, *refs):
    nz, ny, nx = dims
    count = len(spots)
    arrays = refs[:count]
    rest, w_ref, keep_ref, send_ref, held, sems = refs[count:]
    sec = lax.axis_index("sec")
    here = lax.axis_index("dev") % (ny * nx)
    size = nz * rows
    copies = []

    def move(source, target):
        copies.append(pltpu.make_async_copy(source, target, sems.at[len(copies)]))

    for source, (code, column) in zip(arrays, spots):
        span = pl.ds(pl.multiple_of((here ^ code) * size, size), size)
        move(source, held.at[span, pl.ds(column, source.shape[1])])
    move(rest, held.at[:, pl.ds(wide, rest.shape[1])])
    for c in copies:
        c.start()
    for c in copies:
        c.wait()
    total = jnp.dot(held[...], w_ref[...], preferred_element_type=F32)
    part = total.shape[1] // 2
    low, high = total[:, :part], total[:, part:]
    keep_ref[...] = jnp.where(sec == 0, low, high)
    send_ref[...] = jnp.where(sec == 0, high, low)


def project(found, rest, weight, dims, rows):
    depth, cols = weight.shape
    tall = dims[0] * dims[1] * dims[2] * rows
    out = jax.ShapeDtypeStruct((tall, cols // 2), F32)
    arrays = [*(f[2] for f in found), rest]
    spots = tuple(f[:2] for f in found)
    wide = found[0][2].shape[1]
    return pl.pallas_call(
        functools.partial(project_kernel, dims, rows, wide, spots),
        out_shape=(out, out),
        in_specs=[ANY] * len(arrays) + [VM],
        out_specs=(VM, VM),
        scratch_shapes=[
            pltpu.VMEM((tall, depth), BF),
            pltpu.SemaphoreType.DMA((len(arrays),)),
        ],
        compiler_params=pltpu.CompilerParams(vmem_limit_bytes=(4 + tall // 32) * MIB),
        cost_estimate=pl.CostEstimate(
            flops=2 * tall * depth * cols,
            bytes_accessed=2 * depth * (cols + tall),
            transcendentals=0,
        ),
        name="project",
    )(*arrays, weight)


def settle_kernel(dims, rows, *refs):
    nz = dims[0]
    rest, outs = refs[:nz], refs[nz:]
    for kz in range(nz):
        for source, target in scatter_rows(dims, kz, rows):
            at = 0
            for out in outs:
                cols = out.shape[1]
                out[pl.ds(target, rows), :] = rest[kz][source : source + rows, at : at + cols]
                at += cols


def settle(rest, lanes, dims, rows):
    tall = dims[0] * dims[1] * dims[2] * rows
    share = rest[0].shape[1] - 128 - lanes
    return pl.pallas_call(
        functools.partial(settle_kernel, dims, rows),
        out_shape=tuple(jax.ShapeDtypeStruct((tall, w), BF) for w in (share, 128, lanes)),
        in_specs=[VM] * len(rest),
        out_specs=(VM,) * 3,
        compiler_params=pltpu.CompilerParams(vmem_limit_bytes=(6 + tall // 64) * MIB),
        cost_estimate=pl.CostEstimate(
            flops=0, bytes_accessed=3 * MIB, transcendentals=0
        ),
        name="settle",
    )(*rest)


def local(
    dims,
    queries,
    key_cache,
    value_cache,
    new_key,
    new_value,
    cache_lengths,
    residual_in,
    out_weight,
    norm_gain,
    router_weight,
    expert_ids,
    gate_weight,
    up_weight,
    down_weight,
):
    nz, ny, nx = dims
    n = nz * ny * nx
    rows, width = residual_in.shape
    total_rows = n * rows
    expert_total = router_weight.shape[1]
    sec = lax.axis_index("sec")
    lanes = -(-expert_total // 128) * 128
    part = width // n // 2

    if part % 128:
        extra = lax.dynamic_index_in_dim(
            residual_in.reshape(rows, n, 2, part), sec, axis=2, keepdims=False
        )
        extra = jnp.pad(jnp.swapaxes(extra, 0, 1), ((0, 0), (0, 0), (0, 128 - part)))
    else:
        extra = residual_in
    a_own, *blocks = attention(
        queries,
        key_cache,
        value_cache,
        new_key,
        new_value,
        cache_lengths,
        expert_ids.T,
        extra,
        lanes,
        dims,
    )

    plane = ny * nx
    steps = along_z(dims)
    lines = {kz: trade(a_own, dims, kz=kz) for kz in steps}
    blocks = [blocks[0]] + [
        trade(blocks[c], dims, ky=c // nx, kx=c % nx) for c in range(1, plane)
    ]
    rest = pack_plane(blocks, lanes, nz)
    lines, rest = lax.optimization_barrier((lines, rest))
    rest = [rest[0]] + [trade(rest[kz], dims, kz=kz) for kz in range(1, nz)]
    block = pack_line([a_own] + [lines[kz] for kz in range(1, nz)], plane)
    found = over_plane(block, dims)

    rest, residual, mask = settle(rest, lanes, dims, rows)
    keep, send = project(found, rest, out_weight, dims, rows)
    projected = (keep + swap_sec(send)).astype(BF)
    mixed = (residual[:, :part].astype(F32) + projected.astype(F32)).astype(BF)

    lines = {kz: trade(mixed, dims, kz=kz) for kz in steps}
    stacked = jnp.concatenate([mixed] + [lines[kz] for kz in range(1, nz)], axis=0)
    pairs = []
    for ky in range(ny):
        for kx in range(nx):
            got = stacked if ky + kx == 0 else trade(stacked, dims, ky=ky, kx=kx)
            pairs.append((ky * nx + kx, got, swap_sec(got)))
    keep_near, keep_far, send_near, send_far, own_mixed = experts(
        pairs,
        mask,
        norm_gain.reshape(1, width),
        router_weight.T,
        gate_weight,
        up_weight,
        down_weight,
        dims,
        rows,
    )

    quarter = width // 4
    far = keep_far.astype(F32) + swap_sec(send_far).astype(F32)
    near = keep_near.astype(F32) + swap_sec(send_near).astype(F32)
    cut_far = total_rows - total_rows // nx
    cut_near = total_rows // nx
    sums = []
    for h, (nf, ns) in enumerate(((nx, ny), (ny, nx))):
        away = (far[:cut_far] if h == 0 else far[cut_far:]).astype(BF)
        total = near[:cut_near] if h == 0 else near[cut_near:]
        size = total_rows // nf
        for k in range(1, nf):
            came = trade(
                away[(k - 1) * size : k * size], dims, **({"kx": k} if h == 0 else {"ky": k})
            )
            total = total + came.astype(F32)
        total = total.reshape(ns, nz * rows, quarter)
        inner = total[0]
        for k in range(1, ns):
            came = trade(total[k].astype(BF), dims, **({"ky": k} if h == 0 else {"kx": k}))
            inner = inner + came.astype(F32)
        sums.append(inner)
    joined = jnp.concatenate(sums, axis=1).reshape(nz, rows, width // 2)
    last = joined[0]
    came = [trade(joined[k].astype(BF), dims, kz=k) for k in steps]
    for v in came:
        last = last + v.astype(F32)
    own_half = lax.dynamic_slice_in_dim(own_mixed, sec * (width // 2), width // 2, 1)
    done = (own_half.astype(F32) + last).astype(BF)
    other = swap_sec(done)
    return jnp.where(
        sec == 0, jnp.concatenate([done, other], axis=1), jnp.concatenate([other, done], axis=1)
    )


def solution(mesh):
    dims = grid_of(mesh.shape["dev"])
    placed = (
        P("dev", "sec"),
        P("dev", None, "sec"),
        P("dev", None, "sec"),
        P("dev", "sec"),
        P("dev", "sec"),
        P("dev"),
        P("dev", None),
        P("sec", "dev"),
        P(),
        P(),
        P("dev", None),
        P("dev", None, "sec"),
        P("dev", None, "sec"),
        P("dev", "sec", None),
    )
    return jax.shard_map(
        functools.partial(local, dims),
        mesh=mesh,
        in_specs=placed,
        out_specs=P("dev", None),
        check_vma=False,
    )
```

```python
import functools
import math

import jax
import jax.numpy as jnp
from jax import lax
from jax.experimental import pallas as pl
from jax.experimental.pallas import tpu as pltpu
from jax.sharding import PartitionSpec as P

HEAD = 128
masked_score = -1e30
BF = jnp.bfloat16
F32 = jnp.float32


def grid_of(n):
    known = {16: (4, 2, 2), 64: (4, 4, 4)}
    return known.get(n, (n, 1, 1))


def code_of(dims, kz, ky, kx):
    return (kz * dims[1] + ky) * dims[2] + kx


def row_of(dims, chip):
    plane = dims[1] * dims[2]
    return (chip % plane) * dims[0] + chip // plane


def trade(value, dims, kz=0, ky=0, kx=0):
    code = code_of(dims, kz, ky, kx)
    n = dims[0] * dims[1] * dims[2]
    return lax.ppermute(value, "dev", [(d, d ^ code) for d in range(n)])


def along_z(dims):
    return sorted(range(1, dims[0]), key=lambda k: (k == 1, k))


def swap_sec(value):
    return lax.ppermute(value, "sec", [(0, 1), (1, 0)])


def over_plane(block, dims):
    _, ny, nx = dims
    heads = block.shape[1] // HEAD
    cuts = [i * heads // 3 * HEAD for i in range(4)]
    along_x = {kx: trade(block, dims, kx=kx) for kx in range(1, nx)}
    along_y = {ky: trade(block, dims, ky=ky) for ky in range(1, ny)}
    found = [(0, 0, block)]
    found += [(kx, 0, v) for kx, v in along_x.items()]
    found += [(ky * nx, 0, v) for ky, v in along_y.items()]
    for ky in range(1, ny):
        for kx in range(1, nx):
            for i, (start, stop) in enumerate(zip(cuts, cuts[1:])):
                if i < 2:
                    piece = trade(along_x[kx][:, start:stop], dims, ky=ky)
                else:
                    piece = trade(along_y[ky][:, start:stop], dims, kx=kx)
                found.append((ky * nx + kx, start, piece))
    return found


ANY = pl.BlockSpec(memory_space=pl.ANY)
VM = pl.BlockSpec(memory_space=pltpu.VMEM)
HBM = pl.BlockSpec(memory_space=pltpu.HBM)
MIB = 1024 * 1024


def gather_products(dims, codes, arrays, gain_ref, router_ref, gate_ref, up_ref, sums, own_ref):
    acc, route, square = sums
    nz, ny, nx = dims
    plane = ny * nx
    me = lax.axis_index("dev")
    sec = lax.axis_index("sec")
    total = acc.shape[0]
    rows = own_ref.shape[0]
    part = arrays[0].shape[1]
    place = pl.multiple_of(row_of(dims, me) * rows, rows)

    def add_products(x, at):
        power = x * x
        for t in range(0, power.shape[1], 128):
            square[...] += power[:, t : t + 128]
        scaled = (x * gain_ref[:, at]).astype(BF)
        weights = jnp.concatenate([gate_ref[0, at], up_ref[0, at]], axis=1)
        acc[...] += jnp.dot(scaled, weights, preferred_element_type=F32)
        route[...] += lax.dot_general(
            scaled, router_ref[:, at], (((1,), (1,)), ((), ())), preferred_element_type=F32
        )

    if codes is None:
        for t in range(0, gain_ref.shape[1], 256):
            add_products(arrays[0][:, t : t + 256].astype(F32), pl.ds(t, 256))
        own_ref[...] = arrays[0][pl.ds(place, rows), :]
        return
    for i, code in enumerate(codes):
        here, there = arrays[2 * i : 2 * i + 2]
        for kz in range(nz):
            span = slice(kz * total, (kz + 1) * total)
            low = jnp.where(sec == 0, here[span, :], there[span, :])
            high = jnp.where(sec == 0, there[span, :], here[span, :])
            block = jnp.concatenate([low, high], axis=1)
            owner = me ^ (kz * plane + code)
            at = pl.ds(pl.multiple_of(owner * 2 * part, 2 * part), 2 * part)
            add_products(block.astype(F32), at)
        for kz in range(nz):
            owner = me ^ (kz * plane + code)
            spot = pl.ds(pl.multiple_of(kz * total + place, rows), rows)
            mine = [here[spot, :], there[spot, :]]
            first = jnp.where(sec == 0, mine[0], mine[1])
            second = jnp.where(sec == 0, mine[1], mine[0])
            at = pl.ds(pl.multiple_of(owner * 2 * part, 2 * part), 2 * part)
            own_ref[:, at] = jnp.concatenate([first, second], axis=1)


def early_kernel(dims, codes, count, *refs):
    arrays = refs[:count]
    gain_ref, router_ref, gate_ref, up_ref, acc, route, square, own_ref = refs[count:]
    acc[...] = jnp.zeros_like(acc)
    route[...] = jnp.zeros_like(route)
    square[...] = jnp.zeros_like(square)
    own_ref[...] = jnp.zeros_like(own_ref)
    gather_products(
        dims, codes, arrays, gain_ref, router_ref, gate_ref, up_ref, (acc, route, square), own_ref
    )


def late_kernel(dims, codes, eps, count, *refs):
    nz, ny, nx = dims
    arrays = refs[:count]
    (
        gain_ref,
        router_ref,
        gate_ref,
        up_ref,
        acc_in,
        route_in,
        square_in,
        own_in,
        down_ref,
        mask_ref,
        *outs,
        own_ref,
        acc,
        route,
        square,
        hidden,
        hidden_a,
        hidden_b,
    ) = refs[count:]
    acc[...] = acc_in[...]
    route[...] = route_in[...]
    square[...] = square_in[...]
    own_ref[...] = own_in[...]
    gather_products(
        dims, codes, arrays, gain_ref, router_ref, gate_ref, up_ref, (acc, route, square), own_ref
    )
    width = gain_ref.shape[1]
    units = down_ref.shape[1]
    rows = own_ref.shape[0]
    me = lax.axis_index("dev")
    sec = lax.axis_index("sec")
    mean = jnp.sum(square[...], axis=1, keepdims=True) * (1.0 / width)
    inverse = lax.rsqrt(mean + eps)
    live = mask_ref[:, : route.shape[1]].astype(F32) > 0.5
    logits = jnp.where(live, route[...] * inverse, masked_score)
    top = jnp.max(logits, axis=1, keepdims=True)
    powers = jnp.where(live, jnp.exp(logits - top), 0.0)
    lane = lax.broadcasted_iota(jnp.int32, powers.shape, 1)
    mine = jnp.sum(jnp.where(lane == me, powers, 0.0), axis=1, keepdims=True)
    weight = mine / jnp.sum(powers, axis=1, keepdims=True)
    gate = acc[:, :units] * inverse
    up = acc[:, units:] * inverse
    hidden[...] = (gate / (1.0 + jnp.exp(-gate)) * up * weight).astype(BF)
    for kz in range(nz):
        for ky in range(ny):
            for kx in range(nx):
                chip = me ^ code_of(dims, kz, ky, kx)
                place = pl.multiple_of(row_of(dims, chip) * rows, rows)
                block = hidden[pl.ds(place, rows)]
                hidden_a[pl.ds(((kx * ny + ky) * nz + kz) * rows, rows)] = block
                hidden_b[pl.ds(((ky * nx + kx) * nz + kz) * rows, rows)] = block
    finish(dims, sec, hidden_a, hidden_b, down_ref, outs)


def finish(dims, sec, hidden_a, hidden_b, down_ref, outs):
    _, ny, nx = dims
    keep_near, keep_far, send_near, send_far = outs
    quarter = keep_near.shape[1]
    wide = quarter // 2
    near_cut = hidden_a.shape[0] // nx
    far_cut = hidden_a.shape[0] - near_cut
    for h, near, far in ((1, send_near, send_far), (0, keep_near, keep_far)):
        whose = sec if h == 0 else 1 - sec
        for q, (source, first) in enumerate(((hidden_a, nx), (hidden_b, ny))):
            cut = source.shape[0] // first
            rest = source.shape[0] - cut
            for t in range(2):
                place = pl.multiple_of(whose * 2 * quarter + q * quarter + t * wide, wide)
                found = jnp.dot(
                    source[...], down_ref[0, :, pl.ds(place, wide)], preferred_element_type=F32
                ).astype(BF)
                span = slice(t * wide, (t + 1) * wide)
                near[q * near_cut : q * near_cut + cut, span] = found[:cut]
                far[q * far_cut : q * far_cut + rest, span] = found[cut:]


def in_order(pairs, n, total_rows, part, dims):
    me = lax.axis_index("dev")
    sec = lax.axis_index("sec")
    held = jnp.zeros((total_rows, n * 2 * part), BF)
    for code, *both in pairs:
        for side, array in enumerate(both):
            for kz in range(dims[0]):
                owner = me ^ (kz * dims[1] * dims[2] + code)
                whose = sec if side == 0 else 1 - sec
                block = array[kz * total_rows : (kz + 1) * total_rows]
                held = lax.dynamic_update_slice(held, block, (0, (owner * 2 + whose) * part))
    return held


def experts(pairs, mask, gain, router, gate, up, down, dims, rows):
    nz, ny, nx = dims
    total_rows = nz * ny * nx * rows
    _, width, units = gate.shape
    count = max(1, len(pairs) // 2)
    sums = [
        jax.ShapeDtypeStruct((total_rows, 2 * units), F32),
        jax.ShapeDtypeStruct((total_rows, router.shape[0]), F32),
        jax.ShapeDtypeStruct((total_rows, 128), F32),
        jax.ShapeDtypeStruct((rows, width), BF),
    ]
    params = pltpu.CompilerParams(vmem_limit_bytes=(4 + total_rows // 64) * MIB)

    def cost(share):
        return pl.CostEstimate(
            flops=int(6 * total_rows * width * units * share),
            bytes_accessed=int(6 * width * units * share),
            transcendentals=0,
        )

    early = [v for _, *both in pairs[:count] for v in both]
    late = [v for _, *both in pairs[count:] for v in both]
    codes = [p[0] for p in pairs]
    part = pairs[0][1].shape[1]
    found = None
    if part % 128:
        late, codes = [in_order(pairs, nz * ny * nx, total_rows, part, dims)], None
        found = [jnp.zeros(v.shape, v.dtype) for v in sums]
    found = found or pl.pallas_call(
        functools.partial(early_kernel, dims, codes and codes[:count], len(early)),
        out_shape=tuple(sums),
        in_specs=[VM] * (len(early) + 4),
        out_specs=(VM,) * 4,
        compiler_params=params,
        cost_estimate=cost(0.33),
        name="experts_early",
    )(*early, gain, router, gate, up)
    near = total_rows // nx + total_rows // ny
    shapes = [
        jax.ShapeDtypeStruct((r, width // 4), BF)
        for r in (near, 2 * total_rows - near, near, 2 * total_rows - near)
    ]
    return pl.pallas_call(
        functools.partial(late_kernel, dims, codes and codes[count:], 1e-6, len(late)),
        out_shape=(*shapes, sums[3]),
        in_specs=[VM] * (len(late) + 10),
        out_specs=(VM,) * 5,
        scratch_shapes=[pltpu.VMEM(v.shape, v.dtype) for v in sums[:3]]
        + [pltpu.VMEM((total_rows, units), BF)] * 3,
        compiler_params=params,
        cost_estimate=cost(0.67),
        name="experts_late",
    )(*late, gain, router, gate, up, *found, down, mask)


GROUP = 4
CHUNK = 128


def attend_kernel(dims, lanes, *refs):
    (
        len_ref,
        ids_ref,
        q_ref,
        nk_ref,
        nv_ref,
        extra_ref,
        k_ref,
        v_ref,
        *outs,
        keys,
        values,
        apart,
        joined,
        ksems,
        vsems,
    ) = refs
    a_ref, sends = outs[0], outs[1:]
    rows, span, cols = keys.shape
    heads = q_ref.shape[1] // HEAD
    wide = a_ref.shape[1]
    rest = heads * HEAD - wide
    groups = cols // HEAD
    per = heads // groups
    me = lax.axis_index("dev")
    sec = lax.axis_index("sec")

    def fetch(r, source, target, sem):
        live = (len_ref[r] + CHUNK - 1) // CHUNK * CHUNK
        part = pl.ds(0, pl.multiple_of(live, CHUNK))
        return pltpu.make_async_copy(source.at[r, part], target.at[r, part], sem.at[r])

    for start in range(0, rows, GROUP):
        for r in range(start, start + GROUP):
            fetch(r, k_ref, keys, ksems).start()
        values[pl.ds(start, GROUP)] = jnp.zeros((GROUP, span, cols), BF)
        for r in range(start, start + GROUP):
            fetch(r, v_ref, values, vsems).start()

    lane_ids = lax.broadcasted_iota(jnp.int32, (lanes, rows), 0)
    chosen = jnp.zeros((lanes, rows), F32)
    for k in range(ids_ref.shape[0]):
        chosen = jnp.where(lane_ids == ids_ref[k : k + 1, :], 1.0, chosen)
    chosen = chosen.T.astype(BF)
    plane = dims[1] * dims[2]
    for code, target in enumerate(sends):
        for kz in range(dims[0]):
            owner = me ^ (kz * plane + code)
            if len(extra_ref.shape) == 3:
                block = extra_ref[owner]
            else:
                place = pl.multiple_of((owner * 2 + sec) * 128, 128)
                block = extra_ref[:, pl.ds(place, 128)]
            at = rest + kz * 128
            target[:, at : at + 128] = block
        target[:, rest + dims[0] * 128 :] = chosen

    for h in range(heads):
        apart[pl.ds(h * rows, rows)] = q_ref[:, h * HEAD : (h + 1) * HEAD].astype(F32)
    fresh_k = nk_ref[...].astype(F32)
    fresh_v = nv_ref[...].astype(F32)
    head = lax.broadcasted_iota(jnp.int32, (heads, HEAD), 0)
    belongs = [(head >= g * per) & (head < (g + 1) * per) for g in range(groups)]
    place = lax.broadcasted_iota(jnp.int32, (heads, span), 1)
    scale = 1.0 / math.sqrt(HEAD)

    def of_group(wide):
        found = jnp.broadcast_to(wide[:, :HEAD], (heads, HEAD))
        for g in range(1, groups):
            piece = wide[:, g * HEAD : (g + 1) * HEAD]
            found = jnp.where(belongs[g], jnp.broadcast_to(piece, (heads, HEAD)), found)
        return found

    for start in range(0, rows, GROUP):
        group = range(start, start + GROUP)
        for r in group:
            fetch(r, k_ref, keys, ksems).wait()
            fetch(r, v_ref, values, vsems).wait()
        queries, scores = {}, {}
        for r in group:
            q = apart[pl.ds(r, heads, stride=rows), :]
            queries[r] = q
            apart_q = jnp.concatenate([jnp.where(m, q, 0.0) for m in belongs], axis=1)
            scores[r] = lax.dot_general(
                apart_q.astype(BF), keys[r], (((1,), (1,)), ((), ())), preferred_element_type=F32
            )
        for r in group:
            s = jnp.where(place < len_ref[r], scores[r] * scale, masked_score)
            own = jnp.sum(queries[r] * of_group(fresh_k[r : r + 1]), axis=1, keepdims=True) * scale
            top = jnp.maximum(jnp.max(s, axis=1, keepdims=True), own)
            power = jnp.exp(s - top)
            own_power = jnp.exp(own - top)
            total = jnp.sum(power, axis=1, keepdims=True) + own_power
            mixed = jnp.dot(power.astype(BF), values[r], preferred_element_type=F32)
            picked = mixed[:, :HEAD]
            for g in range(1, groups):
                picked = jnp.where(belongs[g], mixed[:, g * HEAD : (g + 1) * HEAD], picked)
            picked = (picked + own_power * of_group(fresh_v[r : r + 1])) / total
            joined[pl.ds(r, heads, stride=rows), :] = picked
    for h in range(heads):
        block = joined[pl.ds(h * rows, rows)].astype(BF)
        at = h * HEAD
        if at < wide:
            a_ref[:, at : at + HEAD] = block
        else:
            for target in sends:
                target[:, at - wide : at - wide + HEAD] = block


def attention(
    queries, key_cache, value_cache, new_key, new_value, cache_lengths, ids, extra, lanes, dims
):
    rows, span, cols = key_cache.shape
    width = queries.shape[1]
    heads = width // HEAD
    wide = heads * 3 // 4 * HEAD
    side = width - wide + dims[0] * 128 + lanes
    outs = [(rows, wide)] + [(rows, side)] * (dims[1] * dims[2])
    return pl.pallas_call(
        functools.partial(attend_kernel, dims, lanes),
        out_shape=tuple(jax.ShapeDtypeStruct(o, BF) for o in outs),
        in_specs=[pl.BlockSpec(memory_space=pltpu.SMEM)] + [VM] * 5 + [HBM, HBM],
        out_specs=(VM,) * len(outs),
        scratch_shapes=[
            pltpu.VMEM((rows, span, cols), BF),
            pltpu.VMEM((rows, span, cols), BF),
            pltpu.VMEM((rows * heads, HEAD), F32),
            pltpu.VMEM((rows * heads, HEAD), F32),
            pltpu.SemaphoreType.DMA((rows,)),
            pltpu.SemaphoreType.DMA((rows,)),
        ],
        compiler_params=pltpu.CompilerParams(vmem_limit_bytes=60 * MIB),
        cost_estimate=pl.CostEstimate(
            flops=4 * rows * heads * span * cols,
            bytes_accessed=4 * rows * span * cols,
            transcendentals=rows * heads * span,
        ),
        name="attend",
    )(cache_lengths, ids, queries, new_key, new_value, extra, key_cache, value_cache)


def pack_line_kernel(plane, *refs):
    lines, out = refs[:-1], refs[-1]
    rows = lines[0].shape[0]
    z = lax.axis_index("dev") // plane
    for kz, source in enumerate(lines):
        out[pl.ds(pl.multiple_of((z ^ kz) * rows, rows), rows), :] = source[...]


def pack_line(lines, plane):
    rows, width = lines[0].shape
    return pl.pallas_call(
        functools.partial(pack_line_kernel, plane),
        out_shape=jax.ShapeDtypeStruct((len(lines) * rows, width), BF),
        in_specs=[VM] * len(lines),
        out_specs=VM,
        compiler_params=pltpu.CompilerParams(vmem_limit_bytes=16 * MIB),
        name="pack_line",
    )(*lines)


def pack_plane_kernel(nz, lanes, count, *refs):
    blocks, outs = refs[:count], refs[count:]
    rows = blocks[0].shape[0]
    share = blocks[0].shape[1] - nz * 128 - lanes
    here = lax.axis_index("dev") % count
    for code, source in enumerate(blocks):
        span = pl.ds(pl.multiple_of((here ^ code) * rows, rows), rows)
        for kz in range(nz):
            outs[kz][span, :share] = source[:, :share]
            at = share + kz * 128
            outs[kz][span, share : share + 128] = source[:, at : at + 128]
            outs[kz][span, share + 128 :] = source[:, share + nz * 128 :]


def pack_plane(blocks, lanes, nz):
    count = len(blocks)
    rows, width = blocks[0].shape
    out = jax.ShapeDtypeStruct((count * rows, width - (nz - 1) * 128), BF)
    return pl.pallas_call(
        functools.partial(pack_plane_kernel, nz, lanes, count),
        out_shape=(out,) * nz,
        in_specs=[VM] * count,
        out_specs=(VM,) * nz,
        compiler_params=pltpu.CompilerParams(vmem_limit_bytes=16 * MIB),
        name="pack_plane",
    )(*blocks)


def scatter_rows(dims, kz, rows):
    nz, ny, nx = dims
    z = lax.axis_index("dev") // (ny * nx)
    for q in range(ny * nx):
        yield q * rows, pl.multiple_of((q * nz + (z ^ kz)) * rows, rows)


def project_kernel(dims, rows, wide, spots, *refs):
    nz, ny, nx = dims
    count = len(spots)
    arrays = refs[:count]
    rest, w_ref, keep_ref, send_ref, held, sems = refs[count:]
    sec = lax.axis_index("sec")
    here = lax.axis_index("dev") % (ny * nx)
    size = nz * rows
    copies = []

    def move(source, target):
        copies.append(pltpu.make_async_copy(source, target, sems.at[len(copies)]))

    for source, (code, column) in zip(arrays, spots):
        span = pl.ds(pl.multiple_of((here ^ code) * size, size), size)
        move(source, held.at[span, pl.ds(column, source.shape[1])])
    move(rest, held.at[:, pl.ds(wide, rest.shape[1])])
    for c in copies:
        c.start()
    for c in copies:
        c.wait()
    total = jnp.dot(held[...], w_ref[...], preferred_element_type=F32)
    part = total.shape[1] // 2
    low, high = total[:, :part], total[:, part:]
    keep_ref[...] = jnp.where(sec == 0, low, high)
    send_ref[...] = jnp.where(sec == 0, high, low)


def project(found, rest, weight, dims, rows):
    depth, cols = weight.shape
    tall = dims[0] * dims[1] * dims[2] * rows
    out = jax.ShapeDtypeStruct((tall, cols // 2), F32)
    arrays = [*(f[2] for f in found), rest]
    spots = tuple(f[:2] for f in found)
    wide = found[0][2].shape[1]
    return pl.pallas_call(
        functools.partial(project_kernel, dims, rows, wide, spots),
        out_shape=(out, out),
        in_specs=[ANY] * len(arrays) + [VM],
        out_specs=(VM, VM),
        scratch_shapes=[
            pltpu.VMEM((tall, depth), BF),
            pltpu.SemaphoreType.DMA((len(arrays),)),
        ],
        compiler_params=pltpu.CompilerParams(vmem_limit_bytes=(4 + tall // 32) * MIB),
        cost_estimate=pl.CostEstimate(
            flops=2 * tall * depth * cols,
            bytes_accessed=2 * depth * (cols + tall),
            transcendentals=0,
        ),
        name="project",
    )(*arrays, weight)


def settle_kernel(dims, rows, *refs):
    nz = dims[0]
    rest, outs = refs[:nz], refs[nz:]
    for kz in range(nz):
        for source, target in scatter_rows(dims, kz, rows):
            at = 0
            for out in outs:
                cols = out.shape[1]
                out[pl.ds(target, rows), :] = rest[kz][source : source + rows, at : at + cols]
                at += cols


def settle(rest, lanes, dims, rows):
    tall = dims[0] * dims[1] * dims[2] * rows
    share = rest[0].shape[1] - 128 - lanes
    return pl.pallas_call(
        functools.partial(settle_kernel, dims, rows),
        out_shape=tuple(jax.ShapeDtypeStruct((tall, w), BF) for w in (share, 128, lanes)),
        in_specs=[VM] * len(rest),
        out_specs=(VM,) * 3,
        compiler_params=pltpu.CompilerParams(vmem_limit_bytes=(6 + tall // 64) * MIB),
        cost_estimate=pl.CostEstimate(
            flops=0, bytes_accessed=3 * MIB, transcendentals=0
        ),
        name="settle",
    )(*rest)


def local(
    dims,
    queries,
    key_cache,
    value_cache,
    new_key,
    new_value,
    cache_lengths,
    residual_in,
    out_weight,
    norm_gain,
    router_weight,
    expert_ids,
    gate_weight,
    up_weight,
    down_weight,
):
    nz, ny, nx = dims
    n = nz * ny * nx
    rows, width = residual_in.shape
    total_rows = n * rows
    expert_total = router_weight.shape[1]
    sec = lax.axis_index("sec")
    lanes = -(-expert_total // 128) * 128
    part = width // n // 2

    if part % 128:
        extra = lax.dynamic_index_in_dim(
            residual_in.reshape(rows, n, 2, part), sec, axis=2, keepdims=False
        )
        extra = jnp.pad(jnp.swapaxes(extra, 0, 1), ((0, 0), (0, 0), (0, 128 - part)))
    else:
        extra = residual_in
    a_own, *blocks = attention(
        queries,
        key_cache,
        value_cache,
        new_key,
        new_value,
        cache_lengths,
        expert_ids.T,
        extra,
        lanes,
        dims,
    )

    plane = ny * nx
    steps = along_z(dims)
    lines = {kz: trade(a_own, dims, kz=kz) for kz in steps}
    blocks = [blocks[0]] + [
        trade(blocks[c], dims, ky=c // nx, kx=c % nx) for c in range(1, plane)
    ]
    rest = pack_plane(blocks, lanes, nz)
    lines, rest = lax.optimization_barrier((lines, rest))
    rest = [rest[0]] + [trade(rest[kz], dims, kz=kz) for kz in range(1, nz)]
    block = pack_line([a_own] + [lines[kz] for kz in range(1, nz)], plane)
    found = over_plane(block, dims)

    rest, residual, mask = settle(rest, lanes, dims, rows)
    keep, send = project(found, rest, out_weight, dims, rows)
    projected = (keep + swap_sec(send)).astype(BF)
    mixed = (residual[:, :part].astype(F32) + projected.astype(F32)).astype(BF)

    lines = {kz: trade(mixed, dims, kz=kz) for kz in steps}
    stacked = jnp.concatenate([mixed] + [lines[kz] for kz in range(1, nz)], axis=0)
    pairs = []
    along_x = {kx: trade(stacked, dims, kx=kx) for kx in range(1, nx)}
    along_y = {ky: trade(stacked, dims, ky=ky) for ky in range(1, ny)}
    middle = stacked.shape[0] // 2
    for ky in range(ny):
        for kx in range(nx):
            if ky == 0 or kx == 0:
                got = along_x[kx] if kx else along_y[ky] if ky else stacked
            else:
                top = trade(along_x[kx][:middle], dims, ky=ky)
                bottom = trade(along_y[ky][middle:], dims, kx=kx)
                got = jnp.concatenate([top, bottom], axis=0)
            pairs.append((ky * nx + kx, got, swap_sec(got)))
    keep_near, keep_far, send_near, send_far, own_mixed = experts(
        pairs,
        mask,
        norm_gain.reshape(1, width),
        router_weight.T,
        gate_weight,
        up_weight,
        down_weight,
        dims,
        rows,
    )

    quarter = width // 4
    far = keep_far.astype(F32) + swap_sec(send_far).astype(F32)
    near = keep_near.astype(F32) + swap_sec(send_near).astype(F32)
    cut_far = total_rows - total_rows // nx
    cut_near = total_rows // nx
    sums = []
    for h, (nf, ns) in enumerate(((nx, ny), (ny, nx))):
        away = (far[:cut_far] if h == 0 else far[cut_far:]).astype(BF)
        total = near[:cut_near] if h == 0 else near[cut_near:]
        size = total_rows // nf
        for k in range(1, nf):
            came = trade(
                away[(k - 1) * size : k * size], dims, **({"kx": k} if h == 0 else {"ky": k})
            )
            total = total + came.astype(F32)
        total = total.reshape(ns, nz * rows, quarter)
        inner = total[0]
        for k in range(1, ns):
            came = trade(total[k].astype(BF), dims, **({"ky": k} if h == 0 else {"kx": k}))
            inner = inner + came.astype(F32)
        sums.append(inner)
    joined = jnp.concatenate(sums, axis=1).reshape(nz, rows, width // 2)
    last = joined[0]
    came = [trade(joined[k].astype(BF), dims, kz=k) for k in steps]
    for v in came:
        last = last + v.astype(F32)
    own_half = lax.dynamic_slice_in_dim(own_mixed, sec * (width // 2), width // 2, 1)
    done = (own_half.astype(F32) + last).astype(BF)
    other = swap_sec(done)
    return jnp.where(
        sec == 0, jnp.concatenate([done, other], axis=1), jnp.concatenate([other, done], axis=1)
    )


def solution(mesh):
    dims = grid_of(mesh.shape["dev"])
    placed = (
        P("dev", "sec"),
        P("dev", None, "sec"),
        P("dev", None, "sec"),
        P("dev", "sec"),
        P("dev", "sec"),
        P("dev"),
        P("dev", None),
        P("sec", "dev"),
        P(),
        P(),
        P("dev", None),
        P("dev", None, "sec"),
        P("dev", None, "sec"),
        P("dev", "sec", None),
    )
    return jax.shard_map(
        functools.partial(local, dims),
        mesh=mesh,
        in_specs=placed,
        out_specs=P("dev", None),
        check_vma=False,
    )
```

```python
import functools
import math

import jax
import jax.numpy as jnp
from jax import lax
from jax.experimental import pallas as pl
from jax.experimental.pallas import tpu as pltpu
from jax.sharding import PartitionSpec as P

HEAD = 128
masked_score = -1e30
BF = jnp.bfloat16
F32 = jnp.float32


def grid_of(n):
    known = {16: (4, 2, 2), 64: (4, 4, 4)}
    return known.get(n, (n, 1, 1))


def code_of(dims, kz, ky, kx):
    return (kz * dims[1] + ky) * dims[2] + kx


def row_of(dims, chip):
    plane = dims[1] * dims[2]
    return (chip % plane) * dims[0] + chip // plane


def trade(value, dims, kz=0, ky=0, kx=0):
    code = code_of(dims, kz, ky, kx)
    n = dims[0] * dims[1] * dims[2]
    return lax.ppermute(value, "dev", [(d, d ^ code) for d in range(n)])


def along_z(dims):
    return sorted(range(1, dims[0]), key=lambda k: (k == 1, k))


def swap_sec(value):
    return lax.ppermute(value, "sec", [(0, 1), (1, 0)])


def over_plane(block, dims):
    _, ny, nx = dims
    heads = block.shape[1] // HEAD
    cuts = [i * heads // 3 * HEAD for i in range(4)]
    along_x = {kx: trade(block, dims, kx=kx) for kx in range(1, nx)}
    along_y = {ky: trade(block, dims, ky=ky) for ky in range(1, ny)}
    found = [(0, 0, block)]
    found += [(kx, 0, v) for kx, v in along_x.items()]
    found += [(ky * nx, 0, v) for ky, v in along_y.items()]
    for ky in range(1, ny):
        for kx in range(1, nx):
            for i, (start, stop) in enumerate(zip(cuts, cuts[1:])):
                if i < 2:
                    piece = trade(along_x[kx][:, start:stop], dims, ky=ky)
                else:
                    piece = trade(along_y[ky][:, start:stop], dims, kx=kx)
                found.append((ky * nx + kx, start, piece))
    return found


ANY = pl.BlockSpec(memory_space=pl.ANY)
VM = pl.BlockSpec(memory_space=pltpu.VMEM)
HBM = pl.BlockSpec(memory_space=pltpu.HBM)
MIB = 1024 * 1024


def gather_products(dims, codes, arrays, gain_ref, router_ref, gate_ref, up_ref, sums, own_ref):
    acc, route, square = sums
    nz, ny, nx = dims
    plane = ny * nx
    me = lax.axis_index("dev")
    sec = lax.axis_index("sec")
    total = acc.shape[0]
    rows = own_ref.shape[0]
    part = arrays[0].shape[1]
    place = pl.multiple_of(row_of(dims, me) * rows, rows)

    def add_products(x, at):
        power = x * x
        for t in range(0, power.shape[1], 128):
            square[...] += power[:, t : t + 128]
        scaled = (x * gain_ref[:, at]).astype(BF)
        weights = jnp.concatenate([gate_ref[0, at], up_ref[0, at]], axis=1)
        acc[...] += jnp.dot(scaled, weights, preferred_element_type=F32)
        route[...] += lax.dot_general(
            scaled, router_ref[:, at], (((1,), (1,)), ((), ())), preferred_element_type=F32
        )

    if codes is None:
        for t in range(0, gain_ref.shape[1], 256):
            add_products(arrays[0][:, t : t + 256].astype(F32), pl.ds(t, 256))
        own_ref[...] = arrays[0][pl.ds(place, rows), :]
        return
    for i, code in enumerate(codes):
        here, there = arrays[2 * i : 2 * i + 2]
        for kz in range(nz):
            span = slice(kz * total, (kz + 1) * total)
            low = jnp.where(sec == 0, here[span, :], there[span, :])
            high = jnp.where(sec == 0, there[span, :], here[span, :])
            block = jnp.concatenate([low, high], axis=1)
            owner = me ^ (kz * plane + code)
            at = pl.ds(pl.multiple_of(owner * 2 * part, 2 * part), 2 * part)
            add_products(block.astype(F32), at)
        for kz in range(nz):
            owner = me ^ (kz * plane + code)
            spot = pl.ds(pl.multiple_of(kz * total + place, rows), rows)
            mine = [here[spot, :], there[spot, :]]
            first = jnp.where(sec == 0, mine[0], mine[1])
            second = jnp.where(sec == 0, mine[1], mine[0])
            at = pl.ds(pl.multiple_of(owner * 2 * part, 2 * part), 2 * part)
            own_ref[:, at] = jnp.concatenate([first, second], axis=1)


def early_kernel(dims, codes, count, *refs):
    arrays = refs[:count]
    gain_ref, router_ref, gate_ref, up_ref, _, acc, route, square, own_ref = refs[count:]
    acc[...] = jnp.zeros_like(acc)
    route[...] = jnp.zeros_like(route)
    square[...] = jnp.zeros_like(square)
    own_ref[...] = jnp.zeros_like(own_ref)
    gather_products(
        dims, codes, arrays, gain_ref, router_ref, gate_ref, up_ref, (acc, route, square), own_ref
    )


def late_kernel(dims, codes, eps, count, *refs):
    nz, ny, nx = dims
    arrays = refs[:count]
    (
        gain_ref,
        router_ref,
        gate_ref,
        up_ref,
        acc_in,
        route_in,
        square_in,
        own_in,
        down_ref,
        mask_ref,
        *outs,
        own_ref,
        acc,
        route,
        square,
        hidden,
        hidden_a,
        hidden_b,
    ) = refs[count:]
    acc[...] = acc_in[...]
    route[...] = route_in[...]
    square[...] = square_in[...]
    own_ref[...] = own_in[...]
    gather_products(
        dims, codes, arrays, gain_ref, router_ref, gate_ref, up_ref, (acc, route, square), own_ref
    )
    width = gain_ref.shape[1]
    units = down_ref.shape[1]
    rows = own_ref.shape[0]
    me = lax.axis_index("dev")
    sec = lax.axis_index("sec")
    mean = jnp.sum(square[...], axis=1, keepdims=True) * (1.0 / width)
    inverse = lax.rsqrt(mean + eps)
    live = mask_ref[:, : route.shape[1]].astype(F32) > 0.5
    logits = jnp.where(live, route[...] * inverse, masked_score)
    top = jnp.max(logits, axis=1, keepdims=True)
    powers = jnp.where(live, jnp.exp(logits - top), 0.0)
    lane = lax.broadcasted_iota(jnp.int32, powers.shape, 1)
    mine = jnp.sum(jnp.where(lane == me, powers, 0.0), axis=1, keepdims=True)
    weight = mine / jnp.sum(powers, axis=1, keepdims=True)
    gate = acc[:, :units] * inverse
    up = acc[:, units:] * inverse
    hidden[...] = (gate / (1.0 + jnp.exp(-gate)) * up * weight).astype(BF)
    for kz in range(nz):
        for ky in range(ny):
            for kx in range(nx):
                chip = me ^ code_of(dims, kz, ky, kx)
                place = pl.multiple_of(row_of(dims, chip) * rows, rows)
                block = hidden[pl.ds(place, rows)]
                hidden_a[pl.ds(((kx * ny + ky) * nz + kz) * rows, rows)] = block
                hidden_b[pl.ds(((ky * nx + kx) * nz + kz) * rows, rows)] = block
    finish(dims, sec, hidden_a, hidden_b, down_ref, outs)


def finish(dims, sec, hidden_a, hidden_b, down_ref, outs):
    _, ny, nx = dims
    keep_near, keep_far, send_near, send_far = outs
    quarter = keep_near.shape[1]
    wide = quarter // 2
    near_cut = hidden_a.shape[0] // nx
    far_cut = hidden_a.shape[0] - near_cut
    for h, near, far in ((1, send_near, send_far), (0, keep_near, keep_far)):
        whose = sec if h == 0 else 1 - sec
        for q, (source, first) in enumerate(((hidden_a, nx), (hidden_b, ny))):
            cut = source.shape[0] // first
            rest = source.shape[0] - cut
            for t in range(2):
                place = pl.multiple_of(whose * 2 * quarter + q * quarter + t * wide, wide)
                found = jnp.dot(
                    source[...], down_ref[0, :, pl.ds(place, wide)], preferred_element_type=F32
                ).astype(BF)
                span = slice(t * wide, (t + 1) * wide)
                near[q * near_cut : q * near_cut + cut, span] = found[:cut]
                far[q * far_cut : q * far_cut + rest, span] = found[cut:]


def in_order(pairs, n, total_rows, part, dims):
    me = lax.axis_index("dev")
    sec = lax.axis_index("sec")
    held = jnp.zeros((total_rows, n * 2 * part), BF)
    for code, *both in pairs:
        for side, array in enumerate(both):
            for kz in range(dims[0]):
                owner = me ^ (kz * dims[1] * dims[2] + code)
                whose = sec if side == 0 else 1 - sec
                block = array[kz * total_rows : (kz + 1) * total_rows]
                held = lax.dynamic_update_slice(held, block, (0, (owner * 2 + whose) * part))
    return held


def experts(pairs, mask, gain, router, gate, up, down, dims, rows):
    nz, ny, nx = dims
    total_rows = nz * ny * nx * rows
    _, width, units = gate.shape
    count = max(1, len(pairs) // 2)
    sums = [
        jax.ShapeDtypeStruct((total_rows, 2 * units), F32),
        jax.ShapeDtypeStruct((total_rows, router.shape[0]), F32),
        jax.ShapeDtypeStruct((total_rows, 128), F32),
        jax.ShapeDtypeStruct((rows, width), BF),
    ]
    params = pltpu.CompilerParams(vmem_limit_bytes=(4 + total_rows // 64) * MIB)

    def cost(share):
        return pl.CostEstimate(
            flops=int(6 * total_rows * width * units * share),
            bytes_accessed=int(6 * width * units * share),
            transcendentals=0,
        )

    early = [v for _, *both in pairs[:count] for v in both]
    late = [v for _, *both in pairs[count:] for v in both]
    codes = [p[0] for p in pairs]
    part = pairs[0][1].shape[1]
    found = None
    if part % 128:
        late, codes = [in_order(pairs, nz * ny * nx, total_rows, part, dims)], None
        found = [jnp.zeros(v.shape, v.dtype) for v in sums]
    found = found or pl.pallas_call(
        functools.partial(early_kernel, dims, codes and codes[:count], len(early)),
        out_shape=tuple(sums),
        in_specs=[VM] * (len(early) + 5),
        out_specs=(VM,) * 4,
        compiler_params=params,
        cost_estimate=cost(0.33),
        name="experts_early",
    )(*early, gain, router, gate, up, down)
    near = total_rows // nx + total_rows // ny
    shapes = [
        jax.ShapeDtypeStruct((r, width // 4), BF)
        for r in (near, 2 * total_rows - near, near, 2 * total_rows - near)
    ]
    return pl.pallas_call(
        functools.partial(late_kernel, dims, codes and codes[count:], 1e-6, len(late)),
        out_shape=(*shapes, sums[3]),
        in_specs=[VM] * (len(late) + 10),
        out_specs=(VM,) * 5,
        scratch_shapes=[pltpu.VMEM(v.shape, v.dtype) for v in sums[:3]]
        + [pltpu.VMEM((total_rows, units), BF)] * 3,
        compiler_params=params,
        cost_estimate=cost(0.67),
        name="experts_late",
    )(*late, gain, router, gate, up, *found, down, mask)


GROUP = 4
CHUNK = 128


def attend_kernel(dims, lanes, *refs):
    (
        len_ref,
        ids_ref,
        q_ref,
        nk_ref,
        nv_ref,
        extra_ref,
        k_ref,
        v_ref,
        *outs,
        keys,
        values,
        apart,
        joined,
        ksems,
        vsems,
    ) = refs
    a_ref, sends = outs[0], outs[1:]
    rows, span, cols = keys.shape
    heads = q_ref.shape[1] // HEAD
    wide = a_ref.shape[1]
    rest = heads * HEAD - wide
    groups = cols // HEAD
    per = heads // groups
    me = lax.axis_index("dev")
    sec = lax.axis_index("sec")

    def fetch(r, source, target, sem):
        live = (len_ref[r] + CHUNK - 1) // CHUNK * CHUNK
        part = pl.ds(0, pl.multiple_of(live, CHUNK))
        return pltpu.make_async_copy(source.at[r, part], target.at[r, part], sem.at[r])

    for start in range(0, rows, GROUP):
        for r in range(start, start + GROUP):
            fetch(r, k_ref, keys, ksems).start()
        values[pl.ds(start, GROUP)] = jnp.zeros((GROUP, span, cols), BF)
        for r in range(start, start + GROUP):
            fetch(r, v_ref, values, vsems).start()

    lane_ids = lax.broadcasted_iota(jnp.int32, (lanes, rows), 0)
    chosen = jnp.zeros((lanes, rows), F32)
    for k in range(ids_ref.shape[0]):
        chosen = jnp.where(lane_ids == ids_ref[k : k + 1, :], 1.0, chosen)
    chosen = chosen.T.astype(BF)
    plane = dims[1] * dims[2]
    for code, target in enumerate(sends):
        for kz in range(dims[0]):
            owner = me ^ (kz * plane + code)
            if len(extra_ref.shape) == 3:
                block = extra_ref[owner]
            else:
                place = pl.multiple_of((owner * 2 + sec) * 128, 128)
                block = extra_ref[:, pl.ds(place, 128)]
            at = rest + kz * 128
            target[:, at : at + 128] = block
        target[:, rest + dims[0] * 128 :] = chosen

    for h in range(heads):
        apart[pl.ds(h * rows, rows)] = q_ref[:, h * HEAD : (h + 1) * HEAD].astype(F32)
    fresh_k = nk_ref[...].astype(F32)
    fresh_v = nv_ref[...].astype(F32)
    head = lax.broadcasted_iota(jnp.int32, (heads, HEAD), 0)
    belongs = [(head >= g * per) & (head < (g + 1) * per) for g in range(groups)]
    place = lax.broadcasted_iota(jnp.int32, (heads, span), 1)
    scale = 1.0 / math.sqrt(HEAD)

    def of_group(wide):
        found = jnp.broadcast_to(wide[:, :HEAD], (heads, HEAD))
        for g in range(1, groups):
            piece = wide[:, g * HEAD : (g + 1) * HEAD]
            found = jnp.where(belongs[g], jnp.broadcast_to(piece, (heads, HEAD)), found)
        return found

    for start in range(0, rows, GROUP):
        group = range(start, start + GROUP)
        for r in group:
            fetch(r, k_ref, keys, ksems).wait()
            fetch(r, v_ref, values, vsems).wait()
        queries, scores = {}, {}
        for r in group:
            q = apart[pl.ds(r, heads, stride=rows), :]
            queries[r] = q
            apart_q = jnp.concatenate([jnp.where(m, q, 0.0) for m in belongs], axis=1)
            scores[r] = lax.dot_general(
                apart_q.astype(BF), keys[r], (((1,), (1,)), ((), ())), preferred_element_type=F32
            )
        for r in group:
            s = jnp.where(place < len_ref[r], scores[r] * scale, masked_score)
            own = jnp.sum(queries[r] * of_group(fresh_k[r : r + 1]), axis=1, keepdims=True) * scale
            top = jnp.maximum(jnp.max(s, axis=1, keepdims=True), own)
            power = jnp.exp(s - top)
            own_power = jnp.exp(own - top)
            total = jnp.sum(power, axis=1, keepdims=True) + own_power
            mixed = jnp.dot(power.astype(BF), values[r], preferred_element_type=F32)
            picked = mixed[:, :HEAD]
            for g in range(1, groups):
                picked = jnp.where(belongs[g], mixed[:, g * HEAD : (g + 1) * HEAD], picked)
            picked = (picked + own_power * of_group(fresh_v[r : r + 1])) / total
            joined[pl.ds(r, heads, stride=rows), :] = picked
    for h in range(heads):
        block = joined[pl.ds(h * rows, rows)].astype(BF)
        at = h * HEAD
        if at < wide:
            a_ref[:, at : at + HEAD] = block
        else:
            for target in sends:
                target[:, at - wide : at - wide + HEAD] = block


def attention(
    queries, key_cache, value_cache, new_key, new_value, cache_lengths, ids, extra, lanes, dims
):
    rows, span, cols = key_cache.shape
    width = queries.shape[1]
    heads = width // HEAD
    wide = heads * 3 // 4 * HEAD
    side = width - wide + dims[0] * 128 + lanes
    outs = [(rows, wide)] + [(rows, side)] * (dims[1] * dims[2])
    return pl.pallas_call(
        functools.partial(attend_kernel, dims, lanes),
        out_shape=tuple(jax.ShapeDtypeStruct(o, BF) for o in outs),
        in_specs=[pl.BlockSpec(memory_space=pltpu.SMEM)] + [VM] * 5 + [HBM, HBM],
        out_specs=(VM,) * len(outs),
        scratch_shapes=[
            pltpu.VMEM((rows, span, cols), BF),
            pltpu.VMEM((rows, span, cols), BF),
            pltpu.VMEM((rows * heads, HEAD), F32),
            pltpu.VMEM((rows * heads, HEAD), F32),
            pltpu.SemaphoreType.DMA((rows,)),
            pltpu.SemaphoreType.DMA((rows,)),
        ],
        compiler_params=pltpu.CompilerParams(vmem_limit_bytes=60 * MIB),
        cost_estimate=pl.CostEstimate(
            flops=4 * rows * heads * span * cols,
            bytes_accessed=4 * rows * span * cols,
            transcendentals=rows * heads * span,
        ),
        name="attend",
    )(cache_lengths, ids, queries, new_key, new_value, extra, key_cache, value_cache)


def pack_line_kernel(plane, *refs):
    lines, out = refs[:-1], refs[-1]
    rows = lines[0].shape[0]
    z = lax.axis_index("dev") // plane
    for kz, source in enumerate(lines):
        out[pl.ds(pl.multiple_of((z ^ kz) * rows, rows), rows), :] = source[...]


def pack_line(lines, plane):
    rows, width = lines[0].shape
    return pl.pallas_call(
        functools.partial(pack_line_kernel, plane),
        out_shape=jax.ShapeDtypeStruct((len(lines) * rows, width), BF),
        in_specs=[VM] * len(lines),
        out_specs=VM,
        compiler_params=pltpu.CompilerParams(vmem_limit_bytes=16 * MIB),
        name="pack_line",
    )(*lines)


def pack_plane_kernel(nz, lanes, count, *refs):
    blocks, outs = refs[:count], refs[count:]
    rows = blocks[0].shape[0]
    share = blocks[0].shape[1] - nz * 128 - lanes
    here = lax.axis_index("dev") % count
    for code, source in enumerate(blocks):
        span = pl.ds(pl.multiple_of((here ^ code) * rows, rows), rows)
        for kz in range(nz):
            outs[kz][span, :share] = source[:, :share]
            at = share + kz * 128
            outs[kz][span, share : share + 128] = source[:, at : at + 128]
            outs[kz][span, share + 128 :] = source[:, share + nz * 128 :]


def pack_plane(blocks, lanes, nz):
    count = len(blocks)
    rows, width = blocks[0].shape
    out = jax.ShapeDtypeStruct((count * rows, width - (nz - 1) * 128), BF)
    return pl.pallas_call(
        functools.partial(pack_plane_kernel, nz, lanes, count),
        out_shape=(out,) * nz,
        in_specs=[VM] * count,
        out_specs=(VM,) * nz,
        compiler_params=pltpu.CompilerParams(vmem_limit_bytes=16 * MIB),
        name="pack_plane",
    )(*blocks)


def scatter_rows(dims, kz, rows):
    nz, ny, nx = dims
    z = lax.axis_index("dev") // (ny * nx)
    for q in range(ny * nx):
        yield q * rows, pl.multiple_of((q * nz + (z ^ kz)) * rows, rows)


def project_kernel(dims, rows, wide, spots, *refs):
    nz, ny, nx = dims
    count = len(spots)
    arrays = refs[:count]
    rest, w_ref, keep_ref, send_ref, held, sems = refs[count:]
    sec = lax.axis_index("sec")
    here = lax.axis_index("dev") % (ny * nx)
    size = nz * rows
    copies = []

    def move(source, target):
        copies.append(pltpu.make_async_copy(source, target, sems.at[len(copies)]))

    for source, (code, column) in zip(arrays, spots):
        span = pl.ds(pl.multiple_of((here ^ code) * size, size), size)
        move(source, held.at[span, pl.ds(column, source.shape[1])])
    move(rest, held.at[:, pl.ds(wide, rest.shape[1])])
    for c in copies:
        c.start()
    for c in copies:
        c.wait()
    total = jnp.dot(held[...], w_ref[...], preferred_element_type=F32)
    part = total.shape[1] // 2
    low, high = total[:, :part], total[:, part:]
    keep_ref[...] = jnp.where(sec == 0, low, high)
    send_ref[...] = jnp.where(sec == 0, high, low)


def project(found, rest, weight, dims, rows):
    depth, cols = weight.shape
    tall = dims[0] * dims[1] * dims[2] * rows
    out = jax.ShapeDtypeStruct((tall, cols // 2), F32)
    arrays = [*(f[2] for f in found), rest]
    spots = tuple(f[:2] for f in found)
    wide = found[0][2].shape[1]
    return pl.pallas_call(
        functools.partial(project_kernel, dims, rows, wide, spots),
        out_shape=(out, out),
        in_specs=[ANY] * len(arrays) + [VM],
        out_specs=(VM, VM),
        scratch_shapes=[
            pltpu.VMEM((tall, depth), BF),
            pltpu.SemaphoreType.DMA((len(arrays),)),
        ],
        compiler_params=pltpu.CompilerParams(vmem_limit_bytes=(4 + tall // 32) * MIB),
        cost_estimate=pl.CostEstimate(
            flops=2 * tall * depth * cols,
            bytes_accessed=2 * depth * (cols + tall),
            transcendentals=0,
        ),
        name="project",
    )(*arrays, weight)


def settle_kernel(dims, rows, *refs):
    nz = dims[0]
    rest, outs = refs[:nz], refs[nz:]
    for kz in range(nz):
        for source, target in scatter_rows(dims, kz, rows):
            at = 0
            for out in outs:
                cols = out.shape[1]
                out[pl.ds(target, rows), :] = rest[kz][source : source + rows, at : at + cols]
                at += cols


def settle(rest, lanes, dims, rows):
    tall = dims[0] * dims[1] * dims[2] * rows
    share = rest[0].shape[1] - 128 - lanes
    return pl.pallas_call(
        functools.partial(settle_kernel, dims, rows),
        out_shape=tuple(jax.ShapeDtypeStruct((tall, w), BF) for w in (share, 128, lanes)),
        in_specs=[VM] * len(rest),
        out_specs=(VM,) * 3,
        compiler_params=pltpu.CompilerParams(vmem_limit_bytes=(6 + tall // 64) * MIB),
        cost_estimate=pl.CostEstimate(
            flops=0, bytes_accessed=3 * MIB, transcendentals=0
        ),
        name="settle",
    )(*rest)


def local(
    dims,
    queries,
    key_cache,
    value_cache,
    new_key,
    new_value,
    cache_lengths,
    residual_in,
    out_weight,
    norm_gain,
    router_weight,
    expert_ids,
    gate_weight,
    up_weight,
    down_weight,
):
    nz, ny, nx = dims
    n = nz * ny * nx
    rows, width = residual_in.shape
    total_rows = n * rows
    expert_total = router_weight.shape[1]
    sec = lax.axis_index("sec")
    lanes = -(-expert_total // 128) * 128
    part = width // n // 2

    if part % 128:
        extra = lax.dynamic_index_in_dim(
            residual_in.reshape(rows, n, 2, part), sec, axis=2, keepdims=False
        )
        extra = jnp.pad(jnp.swapaxes(extra, 0, 1), ((0, 0), (0, 0), (0, 128 - part)))
    else:
        extra = residual_in
    a_own, *blocks = attention(
        queries,
        key_cache,
        value_cache,
        new_key,
        new_value,
        cache_lengths,
        expert_ids.T,
        extra,
        lanes,
        dims,
    )

    plane = ny * nx
    steps = along_z(dims)
    lines = {kz: trade(a_own, dims, kz=kz) for kz in steps}
    blocks = [blocks[0]] + [
        trade(blocks[c], dims, ky=c // nx, kx=c % nx) for c in range(1, plane)
    ]
    rest = pack_plane(blocks, lanes, nz)
    lines, rest = lax.optimization_barrier((lines, rest))
    rest = [rest[0]] + [trade(rest[kz], dims, kz=kz) for kz in range(1, nz)]
    block = pack_line([a_own] + [lines[kz] for kz in range(1, nz)], plane)
    found = over_plane(block, dims)

    rest, residual, mask = settle(rest, lanes, dims, rows)
    keep, send = project(found, rest, out_weight, dims, rows)
    projected = (keep + swap_sec(send)).astype(BF)
    mixed = (residual[:, :part].astype(F32) + projected.astype(F32)).astype(BF)

    lines = {kz: trade(mixed, dims, kz=kz) for kz in steps}
    stacked = jnp.concatenate([mixed] + [lines[kz] for kz in range(1, nz)], axis=0)
    pairs = []
    along_x = {kx: trade(stacked, dims, kx=kx) for kx in range(1, nx)}
    along_y = {ky: trade(stacked, dims, ky=ky) for ky in range(1, ny)}
    middle = stacked.shape[0] // 2
    for ky in range(ny):
        for kx in range(nx):
            if ky == 0 or kx == 0:
                got = along_x[kx] if kx else along_y[ky] if ky else stacked
            else:
                top = trade(along_x[kx][:middle], dims, ky=ky)
                bottom = trade(along_y[ky][middle:], dims, kx=kx)
                got = jnp.concatenate([top, bottom], axis=0)
            pairs.append((ky * nx + kx, got, swap_sec(got)))
    keep_near, keep_far, send_near, send_far, own_mixed = experts(
        pairs,
        mask,
        norm_gain.reshape(1, width),
        router_weight.T,
        gate_weight,
        up_weight,
        down_weight,
        dims,
        rows,
    )

    quarter = width // 4
    far = keep_far.astype(F32) + swap_sec(send_far).astype(F32)
    near = keep_near.astype(F32) + swap_sec(send_near).astype(F32)
    cut_far = total_rows - total_rows // nx
    cut_near = total_rows // nx
    sums = []
    for h, (nf, ns) in enumerate(((nx, ny), (ny, nx))):
        away = (far[:cut_far] if h == 0 else far[cut_far:]).astype(BF)
        total = near[:cut_near] if h == 0 else near[cut_near:]
        size = total_rows // nf
        for k in range(1, nf):
            came = trade(
                away[(k - 1) * size : k * size], dims, **({"kx": k} if h == 0 else {"ky": k})
            )
            total = total + came.astype(F32)
        total = total.reshape(ns, nz * rows, quarter)
        inner = total[0]
        for k in range(1, ns):
            came = trade(total[k].astype(BF), dims, **({"ky": k} if h == 0 else {"kx": k}))
            inner = inner + came.astype(F32)
        sums.append(inner)
    joined = jnp.concatenate(sums, axis=1).reshape(nz, rows, width // 2)
    last = joined[0]
    came = [trade(joined[k].astype(BF), dims, kz=k) for k in steps]
    for v in came:
        last = last + v.astype(F32)
    own_half = lax.dynamic_slice_in_dim(own_mixed, sec * (width // 2), width // 2, 1)
    done = (own_half.astype(F32) + last).astype(BF)
    other = swap_sec(done)
    return jnp.where(
        sec == 0, jnp.concatenate([done, other], axis=1), jnp.concatenate([other, done], axis=1)
    )


def solution(mesh):
    dims = grid_of(mesh.shape["dev"])
    placed = (
        P("dev", "sec"),
        P("dev", None, "sec"),
        P("dev", None, "sec"),
        P("dev", "sec"),
        P("dev", "sec"),
        P("dev"),
        P("dev", None),
        P("sec", "dev"),
        P(),
        P(),
        P("dev", None),
        P("dev", None, "sec"),
        P("dev", None, "sec"),
        P("dev", "sec", None),
    )
    return jax.shard_map(
        functools.partial(local, dims),
        mesh=mesh,
        in_specs=placed,
        out_specs=P("dev", None),
        check_vma=False,
    )
```
